32 devices in a mesh: dp: 8 (over y, x, core), mp: 4 (over z).
Axes of the slice: x: 2, y: 2, z: 4, core: 2. Of those that a mesh axis runs over, the one named last changes fastest.
Arguments:
- tokens: bfloat16 [2, 16, 512, 768], P(None, 'dp', 'mp'), may hold values from -6 to 6
- prev_logits: bfloat16 [2, 16, 12, 512, 512], P(None, 'dp', 'mp'), may hold values from -6 to 6
- segment_ids: int32 [2, 16, 512], P(None, 'dp'), may hold values from 0 to 3, as said below
- query_weight: bfloat16 [768, 768], P(None, 'mp'), may hold values from -0.21875 to 0.21875
- key_weight: bfloat16 [768, 768], P(None, 'mp'), may hold values from -0.21875 to 0.21875
- value_weight: bfloat16 [768, 768], P(None, 'mp'), may hold values from -0.21875 to 0.21875
- query_bias: float32 [768], P('mp'), may hold values from -1.8 to 1.8
- value_bias: float32 [768], P('mp'), may hold values from -1.8 to 1.8
- output_projection_weight: bfloat16 [768, 768], P('mp'), may hold values from -1.75 to 1.75
- output_bias: float32 [768], replicated, may hold values from -1.8 to 1.8
- first_gain: float32 [768], replicated, may hold values from 0.5 to 1.5
- first_shift: float32 [768], replicated, may hold values from -1.8 to 1.8
- inner_projection_weight: bfloat16 [768, 3072], P(None, 'mp'), may hold values from -0.21875 to 0.21875
- inner_bias: float32 [3072], P('mp'), may hold values from -1.8 to 1.8
- down_projection_weight: bfloat16 [3072, 768], P('mp'), may hold values from -0.21875 to 0.21875
- down_bias: float32 [768], replicated, may hold values from -1.8 to 1.8
- second_gain: float32 [768], replicated, may hold values from 0.5 to 1.5
- second_shift: float32 [768], replicated, may hold values from -1.8 to 1.8
- output_cot: bfloat16 [2, 16, 512, 768], P(None, 'dp', 'mp'), may hold values from -6 to 6
- logit_cot: bfloat16 [2, 16, 12, 512, 512], P(None, 'dp', 'mp'), may hold values from -1.5 to 1.5
Outputs:
- layer_output: bfloat16 [2, 16, 512, 768], P(None, 'dp', 'mp')
- new_logits: bfloat16 [2, 16, 12, 512, 512], P(None, 'dp', 'mp')
- tokens_grad: float32 [2, 16, 512, 768], P(None, 'dp', 'mp')
- prev_grad: float32 [2, 16, 12, 512, 512], P(None, 'dp', 'mp')
- query_weight_grad: float32 [768, 768], P(None, 'mp')
- key_weight_grad: float32 [768, 768], P(None, 'mp')
- value_weight_grad: float32 [768, 768], P(None, 'mp')
- query_bias_grad: float32 [768], P('mp')
- value_bias_grad: float32 [768], P('mp')
- output_weight_grad: float32 [768, 768], P('mp')
- output_bias_grad: float32 [768], replicated
- first_gain_grad: float32 [768], replicated
- first_shift_grad: float32 [768], replicated
- inner_weight_grad: float32 [768, 3072], P(None, 'mp')
- inner_bias_grad: float32 [3072], P('mp')
- down_weight_grad: float32 [3072, 768], P('mp')
- down_bias_grad: float32 [768], replicated
- second_gain_grad: float32 [768], replicated
- second_shift_grad: float32 [768], replicated
The draws below stay inside these ranges and needn't reach their ends.
Inputs may be any that keep to these rules, and one draw needn't show every extreme that they name: `segment_ids`: segment ids never decrease along a slot; each slot's ids start at 0 and end at 3.
All inputs are finite; a program needn't handle non-finite values.
Results may differ from the reference program's by a relative error of at most 0.017.
Values may be sent and summed in bfloat16 or wider, within the bound.
No kernel may reach another device: no remote copies, remote signals or barrier semaphores. Data moves between devices by JAX's collectives and lax.ppermute only.
A program may use at most 192 MiB of HBM per device.

```python
import math
import jax
import jax.numpy as jnp
from jax import lax

D = 768
H = 12
HD = 64
FF = 3072
LEN = 512
MB = 2
SLOTS = 16
HH = 768


def draw_segment_ids(key, part):
    key = jax.random.fold_in(key, 11)
    first_key, second_key, third_key = jax.random.split(key, 3)
    start_pos = jax.random.randint(first_key, (MB, SLOTS, 1), 1, LEN // 8 + 1)
    stop_pos = jax.random.randint(second_key, (MB, SLOTS, 1), LEN - LEN // 8, LEN - 1)
    extra_cut = jax.random.randint(third_key, (MB, SLOTS, LEN), 0, 16) == 0
    position = jnp.arange(LEN, dtype=jnp.int32)
    boundary = extra_cut & (position > stop_pos) | (position == start_pos) | (position == stop_pos) | (position == LEN - 1)
    counted = jnp.cumsum(boundary.astype(jnp.int32), axis=-1).astype(jnp.int32)
    return jnp.minimum(counted, 3).astype(jnp.int32)


def steps_of(rng, extent, cuts, smallest, largest):
    factor_of = 1.0
    for dim, blocks in cuts:
        steps = jax.random.uniform(jax.random.fold_in(jax.random.fold_in(rng, 6), dim), (blocks,), jnp.float32, smallest / len(cuts), largest / len(cuts))
        factor_of = factor_of * jnp.repeat(jnp.exp(steps), extent[dim] // blocks).reshape((-1,) + (1,) * (len(extent) - 1 - dim))
    return factor_of


def centred(stream_key, shape, spread, bound, cuts=(), held_as=jnp.bfloat16):
    values = spread * jax.random.normal(stream_key, shape, jnp.float32)
    if cuts:
        values = values * steps_of(stream_key, shape, cuts, -0.22, 0.18)
    return jnp.clip(values, -bound, bound).astype(held_as)


def setup_inputs(seed: int = 0) -> dict:
    streams_of = jax.random.split(jax.random.key(seed), 21)
    return {
        "tokens": centred(streams_of[0], (MB, SLOTS, LEN, D), 1.0, 6.0, ((1, 8), (2, 4))),
        "prev_logits": centred(streams_of[1], (MB, SLOTS, H, LEN, LEN), 1.0, 6.0, ((1, 8), (2, 4))),
        "segment_ids": draw_segment_ids(jax.random.fold_in(streams_of[20], 71), 0),
        "query_weight": centred(streams_of[3], (D, HH), D ** -0.5, 0.21875, ((1, 4),)),
        "key_weight": centred(streams_of[4], (D, HH), D ** -0.5, 0.21875, ((1, 4),)),
        "value_weight": centred(streams_of[5], (D, HH), D ** -0.5, 0.21875, ((1, 4),)),
        "query_bias": centred(streams_of[6], (HH,), 0.3, 1.8, ((0, 4),), jnp.float32),
        "value_bias": centred(streams_of[7], (HH,), 0.3, 1.8, ((0, 4),), jnp.float32),
        "output_projection_weight": centred(streams_of[8], (HH, D), (max(HH // 64, 1)) ** -0.5, 1.75, ((0, 4),)),
        "output_bias": centred(streams_of[9], (D,), 0.3, 1.8, (), jnp.float32),
        "first_gain": jnp.clip(1.0 + 0.1 * jax.random.normal(streams_of[10], (D,), jnp.float32), 0.5, 1.5),
        "first_shift": centred(streams_of[11], (D,), 0.3, 1.8, (), jnp.float32),
        "inner_projection_weight": centred(streams_of[12], (D, FF), D ** -0.5, 0.21875, ((1, 4),)),
        "inner_bias": centred(streams_of[13], (FF,), 0.3, 1.8, ((0, 4),), jnp.float32),
        "down_projection_weight": centred(streams_of[14], (FF, D), (FF // 4) ** -0.5, 0.21875, ((0, 4),)),
        "down_bias": centred(streams_of[15], (D,), 0.3, 1.8, (), jnp.float32),
        "second_gain": jnp.clip(1.0 + 0.1 * jax.random.normal(streams_of[16], (D,), jnp.float32), 0.5, 1.5),
        "second_shift": centred(streams_of[17], (D,), 0.3, 1.8, (), jnp.float32),
        "output_cot": centred(streams_of[18], (MB, SLOTS, LEN, D), 1.0, 6.0, ((1, 8), (2, 4))),
        "logit_cot": centred(streams_of[19], (MB, SLOTS, H, LEN, LEN), 0.25, 1.5, ((1, 8), (2, 4))),
    }


@jax.custom_vjp
def low(v):
    return lax.optimization_barrier(v.astype(jnp.bfloat16)).astype(jnp.float32)

@jax.custom_vjp
def low_back(v):
    return v

def low_keep(v):
    return (low(v), None)

def low_pass(kept, grad):
    return (grad,)

def back_keep(v):
    return (v, None)

def back_low(kept, grad):
    return (low(grad),)
low.defvjp(low_keep, low_pass)
low_back.defvjp(back_keep, back_low)
PRECISE = lax.Precision.HIGHEST
EPSILON = 1e-12

def round_both(value_in):
    return low(low_back(value_in))

def norm_rows(values_in, gain_vec, shift_vec):
    row_mean = lax.optimization_barrier(jnp.mean(values_in, -1, keepdims=True))
    centered = values_in - row_mean
    variance = lax.optimization_barrier(jnp.mean(centered * centered, -1, keepdims=True))
    return centered * lax.rsqrt(variance + EPSILON) * gain_vec + shift_vec

def slot_forward(param_set, token_rows, previous, segments):
    query_weight, key_weight, value_weight, query_bias, value_bias, output_projection_weight, output_bias, first_gain, first_shift, inner_projection_weight, inner_bias, down_projection_weight, down_bias, second_gain, second_shift = param_set
    query_rows = round_both(jnp.dot(token_rows, query_weight, precision=PRECISE) + query_bias)
    key_rows = round_both(jnp.dot(token_rows, key_weight, precision=PRECISE))
    value_rows = round_both(jnp.dot(token_rows, value_weight, precision=PRECISE) + value_bias)
    query_heads = query_rows.reshape(LEN, H, HD)
    key_heads = key_rows.reshape(LEN, H, HD)
    value_heads = value_rows.reshape(LEN, H, HD)
    raw_dots = low_back(jnp.einsum('qhe,khe->hqk', query_heads, key_heads, precision=PRECISE))
    scores = raw_dots * (1.0 / math.sqrt(HD)) + previous
    same_doc = (segments[:, None] == segments[None, :])[None]
    masked = jnp.where(same_doc, scores, -1e+30)
    row_top = lax.optimization_barrier(jnp.max(masked, -1, keepdims=True))
    exponent = jnp.exp(masked - row_top)
    soft_probs = round_both(exponent / lax.optimization_barrier(jnp.sum(exponent, -1, keepdims=True)))
    context_vectors = round_both(jnp.einsum('hqk,khe->qhe', soft_probs, value_heads, precision=PRECISE).reshape(LEN, H * HD))
    attended = low_back(jnp.dot(context_vectors, output_projection_weight, precision=PRECISE)) + output_bias
    hidden = norm_rows(token_rows + attended, first_gain, first_shift)
    inner_pre = low_back(jnp.dot(low(hidden), inner_projection_weight, precision=PRECISE)) + inner_bias
    activated = round_both(jax.nn.gelu(inner_pre, approximate=False))
    branch = low_back(jnp.dot(activated, down_projection_weight, precision=PRECISE)) + down_bias
    layer_out = norm_rows(hidden + branch, second_gain, second_shift)
    return (layer_out, scores)

def reference(tokens, prev_logits, segment_ids, query_weight, key_weight, value_weight, query_bias, value_bias, output_projection_weight, output_bias, first_gain, first_shift, inner_projection_weight, inner_bias, down_projection_weight, down_bias, second_gain, second_shift, output_cot, logit_cot):
    params = tuple((argument.astype(jnp.float32) for argument in (query_weight, key_weight, value_weight, query_bias, value_bias, output_projection_weight, output_bias, first_gain, first_shift, inner_projection_weight, inner_bias, down_projection_weight, down_bias, second_gain, second_shift)))
    slot_total = MB * SLOTS

    def flatten(array):
        return array.reshape((slot_total,) + array.shape[2:])

    def slot_step(grad_total, slot_item):
        token_rows, previous, segments, out_cot, score_cot = slot_item

        def forward(param_set, token_in, previous_in):
            return slot_forward(param_set, token_in, previous_in, segments)
        (layer_out, scores), pullback = jax.vjp(forward, params, token_rows.astype(jnp.float32), previous.astype(jnp.float32))
        param_grads, token_grad, previous_grad = pullback((out_cot.astype(jnp.float32), score_cot.astype(jnp.float32)))
        grad_total = jax.tree.map(jnp.add, grad_total, param_grads)
        return (grad_total, (layer_out.astype(jnp.bfloat16), scores.astype(jnp.bfloat16), token_grad, previous_grad))
    zeros = jax.tree.map(jnp.zeros_like, params)
    grad_total, stacked = lax.scan(slot_step, zeros, (flatten(tokens), flatten(prev_logits), flatten(segment_ids), flatten(output_cot), flatten(logit_cot)))
    layer_output = stacked[0].reshape((MB, SLOTS) + stacked[0].shape[1:])
    new_logits = stacked[1].reshape((MB, SLOTS) + stacked[1].shape[1:])
    tokens_grad = stacked[2].reshape((MB, SLOTS) + stacked[2].shape[1:])
    prev_grad = stacked[3].reshape((MB, SLOTS) + stacked[3].shape[1:])
    return (layer_output, new_logits, tokens_grad, prev_grad, grad_total[0], grad_total[1], grad_total[2], grad_total[3], grad_total[4], grad_total[5], grad_total[6], grad_total[7], grad_total[8], grad_total[9], grad_total[10], grad_total[11], grad_total[12], grad_total[13], grad_total[14])
```

```python
import functools
import math

import jax
import jax.numpy as jnp
from jax import lax
from jax.experimental import pallas as pl
from jax.experimental.pallas import tpu as pltpu
from jax.sharding import PartitionSpec as P

EPSILON = 1e-12
MASKED = -1e30
F32 = jnp.float32
BF16 = jnp.bfloat16
VMEM_LIMIT = 56 * 1024 * 1024
ANY = pl.BlockSpec(memory_space=pl.ANY)
SMEM = pl.BlockSpec(memory_space=pltpu.SMEM)


def mm(a, b, ca, cb):
    return lax.dot_general(a, b, (((ca,), (cb,)), ((), ())), preferred_element_type=F32)


def cost(flops, moved, exps=0):
    return pl.CostEstimate(flops=int(flops), bytes_accessed=int(moved), transcendentals=int(exps))


def params():
    return pltpu.CompilerParams(vmem_limit_bytes=VMEM_LIMIT)


def attend_kernel(chunk, heads, size, tok, w, bias, prev, seg_row, seg_col, *refs):
    logits, probs, qkv, ctx, qs, ks, vs, cs = refs[-8:]
    h = pl.program_id(1)
    length = tok.shape[1]
    width = heads * size

    @pl.when(h == 0)
    def _():
        rows = (mm(tok[0], w[...], 1, 0) + bias[...]).astype(BF16)
        qkv[0] = rows
        for i in range(heads):
            at = i * size
            qs[i] = rows[:, at : at + size] * (1.0 / math.sqrt(size))
            ks[i] = rows[:, width + at : width + at + size]
            vs[i] = rows[:, 2 * width + at : 2 * width + at + size]

    k, v = ks[h], vs[h]
    seg_k = seg_row[0]
    for c in range(length // chunk):
        at = pl.ds(c * chunk, chunk)
        scores = mm(qs[h, at, :], k, 1, 1) + prev[0, 0, 0, at, :].astype(F32)
        logits[0, 0, 0, at, :] = scores.astype(BF16)
        masked = jnp.where(seg_col[0, at, :] == seg_k, scores, MASKED)
        exponent = jnp.exp(masked - jnp.max(masked, -1, keepdims=True))
        p = (exponent * (1.0 / jnp.sum(exponent, -1, keepdims=True))).astype(BF16)
        probs[0, 0, at, :] = p
        cs[h, at, :] = mm(p, v, 1, 0).astype(BF16)

    @pl.when(h == heads - 1)
    def _():
        ctx[0] = jnp.concatenate([cs[i] for i in range(heads)], -1)


def attend(b, complete, w_qkv, bias, prev_logits, seg_row, seg_col, logits_in, chunk=128):
    slots, length, width = complete.shape
    heads = prev_logits.shape[2]
    cols = w_qkv.shape[1]
    size = cols // 3 // heads
    big = pl.BlockSpec((1, 1, 1, length, length), lambda s, h: (b, s, h, 0, 0))

    def whole(*shape):
        return pl.BlockSpec(shape, lambda s, h: (0,) * len(shape))

    def slot(*shape):
        return pl.BlockSpec((1,) + shape, lambda s, h: (s,) + (0,) * len(shape))

    args = [complete, w_qkv, bias, prev_logits, seg_row, seg_col]
    in_specs = [
        slot(length, width), whole(width, cols), whole(1, cols), big, slot(1, length),
        slot(length, 1),
    ]
    alias = {}
    if logits_in is not None:
        alias = {len(args): 0}
        args.append(logits_in)
        in_specs.append(ANY)
    n = slots * heads * length * length
    return pl.pallas_call(
        functools.partial(attend_kernel, chunk, heads, size),
        grid=(slots, heads),
        in_specs=in_specs,
        out_specs=[
            big,
            pl.BlockSpec((1, 1, length, length), lambda s, h: (s, h, 0, 0)),
            slot(length, cols),
            slot(length, cols // 3),
        ],
        out_shape=[
            jax.ShapeDtypeStruct(prev_logits.shape, BF16),
            jax.ShapeDtypeStruct((slots, heads, length, length), BF16),
            jax.ShapeDtypeStruct((slots, length, cols), BF16),
            jax.ShapeDtypeStruct((slots, length, cols // 3), BF16),
        ],
        scratch_shapes=[pltpu.VMEM((heads, length, size), BF16)] * 4,
        input_output_aliases=alias,
        compiler_params=params(),
        cost_estimate=cost(n * 1024 + 2 * slots * length * width * cols, n * 6, n),
        name="attend",
    )(*args)


def attend_back_kernel(chunk, heads, size, n_blocks, place, tok, w, qkv, ctx, probs, cot, *refs):
    blocks = refs[:n_blocks]
    acc_in, bias_in = refs[n_blocks : n_blocks + 2]
    prev_grad, back, acc, bias_acc, qs, ks, vs, os, delta, dqkv = refs[-10:]
    s, h = pl.program_id(0), pl.program_id(1)
    length = tok.shape[1]
    width = heads * size
    local = blocks[0].shape[1]

    @pl.when(h == 0)
    def _():
        for j in range(n_blocks):
            at = pl.ds(pl.multiple_of(place[j] * local, local), local)
            for i in range(heads):
                os[i, at, :] = blocks[j][0, :, i * size : (i + 1) * size]
        rows = qkv[0]
        context = ctx[0]
        for i in range(heads):
            at = i * size
            qs[i] = rows[:, at : at + size]
            ks[i] = rows[:, width + at : width + at + size]
            vs[i] = rows[:, 2 * width + at : 2 * width + at + size]
            o = context[:, at : at + size].astype(F32) * os[i].astype(F32)
            delta[i] = jnp.sum(o, -1, keepdims=True)

    k, v = ks[h], vs[h]
    dk_t = dv_t = None
    for c in range(length // chunk):
        at = pl.ds(c * chunk, chunk)
        d_context = os[h, at, :]
        d_probs = mm(d_context, v, 1, 1)
        p = probs[0, 0, at, :]
        d_scores = p.astype(F32) * (d_probs - delta[h, at, :]) + cot[0, 0, 0, at, :].astype(F32)
        prev_grad[0, 0, 0, at, :] = d_scores
        d_dots = (d_scores * (1.0 / math.sqrt(size))).astype(BF16)
        dqkv[h, at, :size] = mm(d_dots, k, 1, 0).astype(BF16)
        part_k = mm(qs[h, at, :], d_dots, 0, 0)
        part_v = mm(d_context, p, 0, 0)
        dk_t = part_k if c == 0 else dk_t + part_k
        dv_t = part_v if c == 0 else dv_t + part_v
    dqkv[h, :, size : 2 * size] = dk_t.T.astype(BF16)
    dqkv[h, :, 2 * size :] = dv_t.T.astype(BF16)

    @pl.when(h == heads - 1)
    def _():
        parts = [dqkv[i] for i in range(heads)]
        d_qkv = jnp.concatenate(
            [part[:, j * size : (j + 1) * size] for j in range(3) for part in parts], -1
        )
        back[0] = mm(d_qkv, w[...], 1, 1).astype(BF16)
        grad = mm(tok[0], d_qkv, 0, 0)
        sums = jnp.sum(d_qkv.astype(F32), 0, keepdims=True)

        @pl.when(s == 0)
        def _():
            acc[...] = acc_in[...] + grad
            bias_acc[...] = bias_in[...] + sums

        @pl.when(s != 0)
        def _():
            acc[...] += grad
            bias_acc[...] += sums


def attend_back(
    b, place, complete, w_qkv, qkv, ctx, probs, logit_cot, blocks, acc, bias_acc, grad_in, chunk=128
):
    slots, length, width = complete.shape
    heads = logit_cot.shape[2]
    cols = w_qkv.shape[1]
    size = cols // 3 // heads
    local = blocks[0].shape[1]
    big = pl.BlockSpec((1, 1, 1, length, length), lambda s, h: (b, s, h, 0, 0))

    def whole(*shape):
        return pl.BlockSpec(shape, lambda s, h: (0,) * len(shape))

    def slot(*shape):
        return pl.BlockSpec((1,) + shape, lambda s, h: (s,) + (0,) * len(shape))

    args = [place, complete, w_qkv, qkv, ctx, probs, logit_cot, *blocks, acc, bias_acc]
    in_specs = [
        SMEM, slot(length, width), whole(width, cols), slot(length, cols),
        slot(length, cols // 3),
        pl.BlockSpec((1, 1, length, length), lambda s, h: (s, h, 0, 0)), big,
        *[slot(local, cols // 3)] * len(blocks), whole(width, cols), whole(8, cols),
    ]
    alias = {}
    if grad_in is not None:
        alias = {len(args): 0}
        args.append(grad_in)
        in_specs.append(ANY)
    n = slots * heads * length * length
    return pl.pallas_call(
        functools.partial(attend_back_kernel, chunk, heads, size, len(blocks)),
        grid=(slots, heads),
        in_specs=in_specs,
        out_specs=[big, slot(length, width), whole(width, cols), whole(8, cols)],
        out_shape=[
            jax.ShapeDtypeStruct(logit_cot.shape, F32),
            jax.ShapeDtypeStruct((slots, length, width), BF16),
            jax.ShapeDtypeStruct((width, cols), F32),
            jax.ShapeDtypeStruct((8, cols), F32),
        ],
        scratch_shapes=[pltpu.VMEM((heads, length, size), BF16)] * 4
        + [pltpu.VMEM((heads, length, 1), F32), pltpu.VMEM((heads, length, 3 * size), BF16)],
        input_output_aliases=alias,
        compiler_params=params(),
        cost_estimate=cost(n * 2048 + 4 * slots * length * width * cols, n * 8),
        name="attend_back",
    )(*args)


def gelu_and_slope(x):
    bell = jnp.exp(-0.5 * x * x)
    t = 1.0 / (1.0 + (0.3275911 * math.sqrt(0.5)) * jnp.abs(x))
    tail = t * (
        0.5 * 0.254829592
        + t * (
            0.5 * -0.284496736
            + t * (0.5 * 1.421413741 + t * (0.5 * -1.453152027 + t * (0.5 * 1.061405429)))
        )
    ) * bell
    phi = jnp.where(x >= 0, 1.0 - tail, tail)
    return x * phi, phi + x * (bell * (1.0 / math.sqrt(2.0 * math.pi)))


def norm_parts(u):
    centered = u - jnp.mean(u, -1, keepdims=True)
    r = lax.rsqrt(jnp.mean(centered * centered, -1, keepdims=True) + EPSILON)
    return centered * r, r


def norm_back(grad, gain, n, r):
    e = grad * gain
    return r * (e - jnp.mean(e, -1, keepdims=True) - n * jnp.mean(e * n, -1, keepdims=True))


def column_sum(u):
    return jnp.sum(u, 0, keepdims=True)


def feed_forward_kernel(n_ctx, n_in, n_down, chunk, refs_in, refs_out, scratch):
    ctx, refs_in = refs_in[:n_ctx], refs_in[n_ctx:]
    in_parts, refs_in = refs_in[:n_in], refs_in[n_in:]
    down_parts, refs_in = refs_in[:n_down], refs_in[n_down:]
    tok, cot, w_out, b_out, g1, s1, b_in, b_down, g2, s2 = refs_in[:10]
    (out, act, branch, inner, low, att, ctx_all, residual, smalls, unit_sums) = refs_out[:10]
    d_ctx = refs_out[10:]
    w_in, w_down, slope, sem = scratch
    units, width = w_in.shape
    span = units // n_in

    copies = []
    for i in range(n_in):
        copies.append(pltpu.make_async_copy(
            in_parts[i].at[pl.ds(0, span)], w_in.at[pl.ds(i * span, span)], sem.at[0, i]))
        copies[-1].start()
    down_copies = []
    for i in range(n_down):
        down_copies.append(pltpu.make_async_copy(
            down_parts[i].at[pl.ds(0, span)], w_down.at[pl.ds(i * span, span)], sem.at[1, i]))
        down_copies[-1].start()

    attended = b_out[...]
    for k in range(n_ctx):
        attended = attended + mm(ctx[k][...], w_out[k], 1, 0)
    ctx_all[0] = jnp.concatenate([c[...] for c in ctx], -1)
    n1, r1 = norm_parts(tok[0].astype(F32) + attended)
    hidden = n1 * g1[...] + s1[...]
    hidden_low = hidden.astype(BF16)
    low[0] = hidden_low
    second = hidden + b_down[...]
    waited = 0
    for j in range(units // chunk):
        at = pl.ds(j * chunk, chunk)
        while waited < n_in and waited * span < (j + 1) * chunk:
            copies[waited].wait()
            down_copies[waited].wait()
            waited += 1
        pre = mm(hidden_low, w_in[at, :], 1, 1) + b_in[:, at]
        activated, grad = gelu_and_slope(pre)
        activated = activated.astype(BF16)
        act[0, :, at] = activated
        slope[:, at] = grad.astype(BF16)
        second = second + mm(activated, w_down[at, :], 1, 0)

    n2, r2 = norm_parts(second)
    out[0] = (n2 * g2[...] + s2[...]).astype(BF16)
    g = cot[0].astype(F32)
    d_second = norm_back(g, g2[...], n2, r2)
    smalls[3:4, :] = column_sum(d_second)
    smalls[4:5, :] = column_sum(g * n2)
    smalls[5:6, :] = column_sum(g)
    d_branch = d_second.astype(BF16)
    branch[0] = d_branch
    d_hidden = d_second
    for j in range(units // chunk):
        at = pl.ds(j * chunk, chunk)
        d_act = mm(d_branch, w_down[at, :], 1, 1)
        d_inner = d_act * slope[:, at].astype(F32)
        unit_sums[:, at] = jnp.broadcast_to(column_sum(d_inner), (8, chunk))
        d_inner = d_inner.astype(BF16)
        inner[0, :, at] = d_inner
        d_hidden = d_hidden + mm(d_inner, w_in[at, :], 1, 0)
    d_residual = norm_back(d_hidden, g1[...], n1, r1)
    residual[0] = d_residual
    smalls[0:1, :] = column_sum(d_residual)
    smalls[1:2, :] = column_sum(d_hidden * n1)
    smalls[2:3, :] = column_sum(d_hidden)
    smalls[6:8, :] = jnp.zeros((2, width), F32)
    d_att = d_residual.astype(BF16)
    att[0] = d_att
    for k in range(n_ctx):
        d_ctx[k][...] = mm(d_att, w_out[k], 1, 1).astype(BF16)


def feed_forward(b, ctx, in_parts, down_parts, tokens, cot, w_out, vectors, joint, chunk=384):
    micro, rows, width = tokens.shape
    b_out, g1, s1, b_in, b_down, g2, s2 = vectors
    units = b_in.shape[1]
    head_width = ctx[0].shape[1]
    n_ctx, n_in, n_down = len(ctx), len(in_parts), len(down_parts)

    def whole(*shape):
        return pl.BlockSpec(shape, lambda i: (0,) * len(shape))

    def part(cols):
        return pl.BlockSpec((1, rows, cols), lambda i: (b, 0, 0))

    args = [*ctx, *in_parts, *down_parts, tokens, cot, w_out, b_out, g1, s1, b_in, b_down, g2, s2]
    in_specs = (
        [whole(rows, head_width)] * n_ctx
        + [ANY] * (n_in + n_down)
        + [part(width)] * 2
        + [whole(n_ctx, head_width, width)]
        + [whole(1, v.shape[1]) for v in vectors]
    )
    joint_cols = [(width, BF16), (units, BF16), (width, BF16), (units, BF16), (width, BF16),
                  (width, BF16), (width, BF16), (width, F32)]
    alias = {}
    if joint is not None:
        for i, array in enumerate(joint):
            alias[len(args)] = i
            args.append(array)
            in_specs.append(ANY)
    n_args = len(args)
    n_out = len(joint_cols) + 2 + n_ctx

    def kernel(*refs):
        feed_forward_kernel(
            n_ctx, n_in, n_down, chunk, refs[: n_args], refs[n_args : n_args + n_out],
            refs[n_args + n_out :],
        )

    outs = pl.pallas_call(
        kernel,
        grid=(1,),
        in_specs=in_specs,
        out_specs=[part(c) for c, _ in joint_cols]
        + [whole(8, width), whole(8, units)]
        + [whole(rows, head_width)] * n_ctx,
        out_shape=[jax.ShapeDtypeStruct((micro, rows, c), t) for c, t in joint_cols]
        + [jax.ShapeDtypeStruct((8, width), F32), jax.ShapeDtypeStruct((8, units), F32)]
        + [jax.ShapeDtypeStruct((rows, head_width), BF16)] * n_ctx,
        scratch_shapes=[
            pltpu.VMEM((units, width), BF16), pltpu.VMEM((units, width), BF16),
            pltpu.VMEM((rows, units), BF16), pltpu.SemaphoreType.DMA((2, max(n_in, n_down))),
        ],
        input_output_aliases=alias,
        compiler_params=params(),
        cost_estimate=cost(
            2 * rows * width * (4 * units + 2 * width), 4 * units * width + 20 * rows * width,
            rows * units,
        ),
        name="feed_forward",
    )(*args)
    n = len(joint_cols)
    return outs[:n], outs[n], outs[n + 1], outs[n + 2 :]


def shift_pairs(mp, k):
    return [(i, (i + k) % mp) for i in range(mp)]


def flip_pairs(dp, bit):
    return [(i, i ^ bit) for i in range(dp)]


def add_low(a, b):
    return (a.astype(F32) + b.astype(F32)).astype(BF16)


def plane_gather(first, second, dp):
    x, y = flip_pairs(dp, 2), flip_pairs(dp, 4)
    a1 = lax.ppermute(first, "dp", x)
    b2 = lax.ppermute(second, "dp", y)
    a2 = lax.ppermute(first, "dp", y)
    b1 = lax.ppermute(second, "dp", x)
    a3 = lax.ppermute(a1, "dp", y)
    b3 = lax.ppermute(b2, "dp", x)
    return [first, a1, a2, a3], [second, b1, b2, b3]


def plane_reduce(first, second, dp):
    x, y = flip_pairs(dp, 2), flip_pairs(dp, 4)
    a3 = lax.ppermute(first[3], "dp", y)
    b3 = lax.ppermute(second[3], "dp", x)
    a2 = lax.ppermute(first[2], "dp", y)
    b1 = lax.ppermute(second[1], "dp", x)
    a1 = lax.ppermute(add_low(first[1], a3), "dp", x)
    b2 = lax.ppermute(add_low(second[2], b3), "dp", y)
    a = first[0].astype(F32) + a1.astype(F32) + a2.astype(F32)
    b = second[0].astype(F32) + b1.astype(F32) + b2.astype(F32)
    return a.astype(BF16), b.astype(BF16)


def reorder(rows, order):
    pick = (order[:, None] == jnp.arange(rows.shape[0])[None, :]).astype(F32)
    return jnp.dot(pick, rows, precision=lax.Precision.HIGHEST)


def on_device(
    tokens,
    prev_logits,
    segment_ids,
    query_weight,
    key_weight,
    value_weight,
    query_bias,
    value_bias,
    output_projection_weight,
    output_bias,
    first_gain,
    first_shift,
    inner_projection_weight,
    inner_bias,
    down_projection_weight,
    down_bias,
    second_gain,
    second_shift,
    output_cot,
    logit_cot,
):
    dp = lax.axis_size("dp")
    mp = lax.axis_size("mp")
    me = lax.axis_index("dp")
    mine = lax.axis_index("mp")
    micro_count, slots, local, width = tokens.shape
    length = prev_logits.shape[3]
    head_width = query_weight.shape[1]
    units = inner_projection_weight.shape[1]
    rows = slots * local
    small_plane = dp == 8
    chips = dp // 2
    core, chip = me % 2, me // 2
    swap = flip_pairs(dp, 1)
    piece = units // dp
    span = mp * piece
    wo_rows = head_width // chips

    def shifted(array, k):
        return lax.ppermute(array, "mp", shift_pairs(mp, k)) if k else array

    complete = [lax.all_gather(tokens[b], "mp", axis=1, tiled=True) for b in range(micro_count)]

    if small_plane:
        start = (core * chips + chip) * piece
        in_piece = lax.dynamic_slice(inner_projection_weight, (0, start), (width, piece)).T
        wo_piece = lax.dynamic_slice(
            output_projection_weight, (chip * wo_rows, 0), (wo_rows, width)
        )
        first_piece = jnp.concatenate([in_piece, wo_piece], 0)
        second_piece = lax.dynamic_slice(down_projection_weight, (start, 0), (piece, width))
        first_z = [shifted(first_piece, k) for k in range(mp)]
        second_z = [shifted(second_piece, k) for k in range(mp)]
        first = jnp.concatenate([a[:piece] for a in first_z] + [a[piece:] for a in first_z], 0)
        second = jnp.concatenate(second_z, 0)
        in_parts, down_parts = plane_gather(first, second, dp)
        w_out = jnp.zeros((mp, chips, wo_rows, width), BF16)
        for o in range(chips):
            block = in_parts[o][span:].reshape(mp, 1, wo_rows, width)
            w_out = lax.dynamic_update_slice(w_out, block, (0, chip ^ o, 0, 0))
        w_out = w_out.reshape(mp, head_width, width)
        in_parts = in_parts + [lax.ppermute(a, "dp", swap) for a in in_parts]
        down_parts = down_parts + [lax.ppermute(a, "dp", swap) for a in down_parts]
        bias_z = jnp.stack([shifted(inner_bias, k) for k in range(mp)]).reshape(-1, piece)
        c_i, o_i, k_i = jnp.meshgrid(
            jnp.arange(2), jnp.arange(chips), jnp.arange(mp), indexing="ij"
        )
        unit_order = ((k_i * 2 + (core ^ c_i)) * chips + (chip ^ o_i)).reshape(-1)
        bias_units = reorder(bias_z, unit_order).reshape(1, -1)
    else:
        in_parts = [lax.all_gather(inner_projection_weight.T, "mp", axis=0, tiled=True)]
        down_parts = [lax.all_gather(down_projection_weight, "mp", axis=0, tiled=True)]
        wo_all = lax.all_gather(output_projection_weight, "mp")
        w_out = jnp.stack(
            [lax.dynamic_index_in_dim(wo_all, (mine - k) % mp, 0, False) for k in range(mp)]
        )
        bias_units = lax.all_gather(inner_bias, "mp").reshape(1, -1)

    w_qkv = jnp.concatenate([query_weight, key_weight, value_weight], 1)
    bias_row = jnp.concatenate([query_bias, jnp.zeros_like(query_bias), value_bias])[None]
    vectors = [
        output_bias[None], first_gain[None], first_shift[None], bias_units, down_bias[None],
        second_gain[None], second_shift[None],
    ]
    own_tokens = tokens.reshape(micro_count, rows, width)
    own_cot = output_cot.reshape(micro_count, rows, width)
    logits = joint = None
    kept = []
    for b in range(micro_count):
        seg = segment_ids[b]
        logits, probs, qkv, ctx = attend(
            b, complete[b], w_qkv, bias_row, prev_logits, seg[:, None, :], seg[:, :, None], logits
        )
        blocks = []
        for k in range(mp):
            at = ((mine + k) % mp) * local
            block = lax.dynamic_slice(ctx, (0, at, 0), (slots, local, head_width))
            blocks.append(shifted(block, k).reshape(rows, head_width))
        joint, small, unit_sums, d_ctx = feed_forward(
            b, blocks, in_parts, down_parts, own_tokens, own_cot, w_out, vectors, joint
        )
        d_blocks = [
            shifted(block, (mp - k) % mp).reshape(slots, local, head_width)
            for k, block in enumerate(d_ctx)
        ]
        kept.append((probs, qkv, ctx, small, unit_sums, d_blocks))
    layer, act, branch, inner, low, att, ctx_all, residual = joint

    def tall(array):
        return array.reshape(micro_count * rows, -1)

    place = jnp.stack([(mine + k) % mp for k in range(mp)]).astype(jnp.int32)
    prev_grad = None
    acc = jnp.zeros((width, 3 * head_width), F32)
    bias_acc = jnp.zeros((8, 3 * head_width), F32)
    token_grads = []
    for b in range(micro_count):
        probs, qkv, ctx, _, _, d_blocks = kept[b]
        prev_grad, back, acc, bias_acc = attend_back(
            b, place, complete[b], w_qkv, qkv, ctx, probs, logit_cot, d_blocks, acc, bias_acc,
            prev_grad,
        )
        back = lax.psum_scatter(back, "mp", scatter_dimension=1, tiled=True)
        token_grads.append(
            residual[b].reshape(slots, local, width) + back.astype(F32)
        )

    g_down = mm(tall(act), tall(branch), 0, 0)
    g_in = mm(tall(inner), tall(low), 0, 0)
    g_out = mm(tall(ctx_all), tall(att), 0, 0)
    unit_total = sum(each[4][0] for each in kept)
    small = sum(each[3] for each in kept)
    if small_plane:
        g_down, g_in, g_out = (g.astype(BF16) for g in (g_down, g_in, g_out))
        half = units * mp // 2
        g_down = add_low(g_down[:half], lax.ppermute(g_down[half:], "dp", swap))
        g_in = add_low(g_in[:half], lax.ppermute(g_in[half:], "dp", swap))
        g_out = add_low(g_out, lax.ppermute(g_out, "dp", swap))
        g_out = g_out.reshape(mp, chips, wo_rows, width)
        first_list, second_list = [], []
        for o in range(chips):
            block = lax.dynamic_index_in_dim(g_out, chip ^ o, 1, False).reshape(-1, width)
            first_list.append(jnp.concatenate([g_in[o * span : (o + 1) * span], block], 0))
            second_list.append(g_down[o * span : (o + 1) * span])
        first, second = plane_reduce(first_list, second_list, dp)
        in_sum = out_sum = down_sum = 0.0
        for k in range(mp):
            send = jnp.concatenate(
                [
                    first[k * piece : (k + 1) * piece],
                    first[span + k * wo_rows : span + (k + 1) * wo_rows],
                    second[k * piece : (k + 1) * piece],
                ],
                0,
            )
            got = shifted(send, (mp - k) % mp).astype(F32)
            in_sum += got[:piece]
            out_sum += got[piece : piece + wo_rows]
            down_sum += got[piece + wo_rows :]
        firsts, seconds = plane_gather(
            jnp.concatenate([in_sum, out_sum], 0).astype(BF16), down_sum.astype(BF16), dp
        )
        in_grad = jnp.zeros((2, chips, piece, width), BF16)
        down_grad = jnp.zeros((2, chips, piece, width), BF16)
        output_weight_grad = jnp.zeros((chips, wo_rows, width), BF16)
        for o in range(chips):
            for c in range(2):
                a = lax.ppermute(firsts[o], "dp", swap) if c else firsts[o]
                d = lax.ppermute(seconds[o], "dp", swap) if c else seconds[o]
                at = (core ^ c, chip ^ o, 0, 0)
                in_grad = lax.dynamic_update_slice(in_grad, a[None, None, :piece], at)
                down_grad = lax.dynamic_update_slice(down_grad, d[None, None], at)
                if c == 0:
                    output_weight_grad = lax.dynamic_update_slice(
                        output_weight_grad, a[None, piece:], (chip ^ o, 0, 0)
                    )
        inner_weight_grad = in_grad.reshape(units, width).astype(F32).T
        down_weight_grad = down_grad.reshape(units, width).astype(F32)
        output_weight_grad = output_weight_grad.reshape(head_width, width).astype(F32)
        c_j, o_j = jnp.meshgrid(jnp.arange(2), jnp.arange(chips), indexing="ij")
        z_j = jnp.arange(mp)[:, None, None]
        back_order = (((core ^ c_j) * chips + (chip ^ o_j)) * mp + (mine - z_j) % mp).reshape(-1)
        unit_total = reorder(unit_total.reshape(-1, piece), back_order).reshape(-1)
    else:
        g_in = lax.psum_scatter(g_in, "mp", scatter_dimension=0, tiled=True)
        inner_weight_grad = lax.psum(g_in, "dp").T
        g_down = lax.psum_scatter(g_down, "mp", scatter_dimension=0, tiled=True)
        down_weight_grad = lax.psum(g_down, "dp")
        g_out = g_out.reshape(mp, head_width, width)
        out_sum = 0.0
        for k in range(mp):
            out_sum += shifted(g_out[k], (mp - k) % mp)
        output_weight_grad = lax.psum(out_sum, "dp")

    vector = jnp.concatenate([small[:6].reshape(-1), unit_total])
    vector = lax.psum(vector, ("dp", "mp"))
    small = vector[: 6 * width].reshape(6, width)
    inner_bias_grad = lax.dynamic_slice(vector, (6 * width + mine * units,), (units,))
    summed = lax.psum(jnp.concatenate([acc, bias_acc], 0), "dp")
    return (
        layer.reshape(tokens.shape),
        logits,
        jnp.stack(token_grads),
        prev_grad,
        summed[:width, :head_width],
        summed[:width, head_width : 2 * head_width],
        summed[:width, 2 * head_width :],
        summed[width, :head_width],
        summed[width, 2 * head_width :],
        output_weight_grad,
        small[0],
        small[1],
        small[2],
        inner_weight_grad,
        inner_bias_grad,
        down_weight_grad,
        small[3],
        small[4],
        small[5],
    )


def solution(mesh):
    rows = P(None, "dp", "mp", None)
    heads = P(None, "dp", "mp", None, None)
    cols, deep, vec, same = P(None, "mp"), P("mp", None), P("mp"), P()
    in_specs = (
        rows, heads, P(None, "dp", None), cols, cols, cols, vec, vec, deep, same, same, same,
        cols, vec, deep, same, same, same, rows, heads,
    )
    out_specs = (
        rows, heads, rows, heads, cols, cols, cols, vec, vec, deep, same, same, same, cols, vec,
        deep, same, same, same,
    )
    return jax.shard_map(
        on_device, mesh=mesh, in_specs=in_specs, out_specs=out_specs, check_vma=False
    )
```

```python
import functools
import math

import jax
import jax.numpy as jnp
from jax import lax
from jax.experimental import pallas as pl
from jax.experimental.pallas import tpu as pltpu
from jax.sharding import PartitionSpec as P

EPSILON = 1e-12
MASKED = -1e30
F32 = jnp.float32
BF16 = jnp.bfloat16
VMEM_LIMIT = 60 * 1024 * 1024
UNROLL = 2
ANY = pl.BlockSpec(memory_space=pl.ANY)
VMEM = pl.BlockSpec(memory_space=pltpu.VMEM)
SMEM = pl.BlockSpec(memory_space=pltpu.SMEM)


def mm(a, b, ca, cb):
    return lax.dot_general(a, b, (((ca,), (cb,)), ((), ())), preferred_element_type=F32)


def cost(flops, moved, exps=0):
    return pl.CostEstimate(flops=int(flops), bytes_accessed=int(moved), transcendentals=int(exps))


def start(src, dst, sem):
    copy = pltpu.make_async_copy(src, dst, sem)
    copy.start()
    return copy

def attend_kernel(b, slots, heads, size, tok, w, bias, prev, seg, *refs):
    logits, probs, qkv, ctx = refs[-17:-13]
    tok_v, prev_v, logits_v, probs_v, qkv_v, ctx_v, w_v, qs, ks, vs = refs[-13:-3]
    sem_in, sem_out, sem_w = refs[-3:]
    length = tok_v.shape[1]
    width = heads * size
    w_in = start(w, w_v, sem_w)
    tok_in, prev_in = [], []
    for s in range(slots):
        tok_in.append(start(tok.at[s], tok_v.at[s], sem_in.at[s, heads]))
        if s == 0:
            prev_in += [start(prev.at[b, s, h], prev_v.at[s, h], sem_in.at[s, h]) for h in range(heads)]
    w_in.wait()
    for s in range(1, slots):
        prev_in += [start(prev.at[b, s, h], prev_v.at[s, h], sem_in.at[s, h]) for h in range(heads)]
    for copy in tok_in:
        copy.wait()

    def project(s, _):
        rows = (mm(tok_v[s], w_v[...], 1, 0) + bias[...]).astype(BF16)
        qkv_v[s] = rows
        start(qkv_v.at[s], qkv.at[s], sem_out.at[s, 2 * heads])
        for h in range(heads):
            at = h * size
            qs[s, h] = rows[:, at : at + size] * (1.0 / math.sqrt(size))
            ks[s, h] = rows[:, width + at : width + at + size]
            vs[s, h] = rows[:, 2 * width + at : 2 * width + at + size]
        return _

    lax.fori_loop(0, slots, project, 0)

    def one_head(i, _):
        s, h = i // heads, lax.rem(i, heads)
        seg_k = seg[b, pl.ds(s, 1), :]
        seg_q = jnp.broadcast_to(seg_k, (8, length)).T[:, :1]
        pltpu.make_async_copy(prev.at[b, s, h], prev_v.at[s, h], sem_in.at[s, h]).wait()
        q, k, v = qs[s, h], ks[s, h], vs[s, h]
        scores = mm(q, k, 1, 1) + prev_v[s, h].astype(F32)
        logits_v[s, h] = scores.astype(BF16)
        start(logits_v.at[s, h], logits.at[b, s, h], sem_out.at[s, h])
        masked = jnp.where(seg_q == seg_k, scores, MASKED)
        exponent = jnp.exp(masked - jnp.max(masked, -1, keepdims=True))
        p = (exponent * (1.0 / jnp.sum(exponent, -1, keepdims=True))).astype(BF16)
        probs_v[s, h] = p
        start(probs_v.at[s, h], probs.at[s, h], sem_out.at[s, heads + h])
        qs[s, h] = mm(p, v, 1, 0).astype(BF16)
        return _

    lax.fori_loop(0, slots * heads, one_head, 0)
    for s in range(slots):
        ctx_v[s] = jnp.concatenate([qs[s, h] for h in range(heads)], -1)
        start(ctx_v.at[s], ctx.at[s], sem_out.at[s, 2 * heads + 1])
    for s in range(slots):
        for h in range(heads):
            pltpu.make_async_copy(logits_v.at[s, h], logits.at[b, s, h], sem_out.at[s, h]).wait()
            pltpu.make_async_copy(probs_v.at[s, h], probs.at[s, h], sem_out.at[s, heads + h]).wait()
        pltpu.make_async_copy(qkv_v.at[s], qkv.at[s], sem_out.at[s, 2 * heads]).wait()
        pltpu.make_async_copy(ctx_v.at[s], ctx.at[s], sem_out.at[s, 2 * heads + 1]).wait()


def attend(b, complete, w_qkv, bias, prev_logits, seg, logits_in):
    slots, length, width = complete.shape
    heads = prev_logits.shape[2]
    cols = w_qkv.shape[1]
    size = cols // 3 // heads
    args = [complete, w_qkv, bias, prev_logits, seg]
    in_specs = [ANY, ANY, VMEM, ANY, VMEM]
    alias = {}
    if logits_in is not None:
        alias = {len(args): 0}
        args.append(logits_in)
        in_specs.append(ANY)
    n = slots * heads * length * length
    square = pltpu.VMEM((slots, heads, length, length), BF16)
    return pl.pallas_call(
        functools.partial(attend_kernel, b, slots, heads, size),
        in_specs=in_specs,
        out_specs=[ANY] * 4,
        out_shape=[
            jax.ShapeDtypeStruct(prev_logits.shape, BF16),
            jax.ShapeDtypeStruct((slots, heads, length, length), BF16),
            jax.ShapeDtypeStruct((slots, length, cols), BF16),
            jax.ShapeDtypeStruct((slots, length, cols // 3), BF16),
        ],
        scratch_shapes=[
            pltpu.VMEM((slots, length, width), BF16), square, square, square,
            pltpu.VMEM((slots, length, cols), BF16), pltpu.VMEM((slots, length, cols // 3), BF16),
            pltpu.VMEM((width, cols), BF16),
            *[pltpu.VMEM((slots, heads, length, size), BF16)] * 3,
            pltpu.SemaphoreType.DMA((slots, heads + 1)),
            pltpu.SemaphoreType.DMA((slots, 2 * heads + 2)), pltpu.SemaphoreType.DMA,
        ],
        input_output_aliases=alias,
        compiler_params=pltpu.CompilerParams(vmem_limit_bytes=VMEM_LIMIT),
        cost_estimate=cost(n * 1024 + 2 * slots * length * width * cols, n * 6, n),
        name="attend",
    )(*args)


def attend_back_kernel(micro, slots, heads, size, n_blocks, place, *refs):
    tok, qkv, ctx, probs = (refs[i * micro : (i + 1) * micro] for i in range(4))
    w, cot, *blocks = refs[4 * micro : 4 * micro + 2 + n_blocks]
    prev_grad, back, acc, bias_acc = refs[-17:-13]
    tok_v, qkv_v, ctx_v, dctx_v, probs_v, cot_v, grad_v, back_v, w_v, parts, deltas = refs[-13:-2]
    sem_in, sem_out = refs[-2:]
    length = tok_v.shape[1]
    width = heads * size
    local = blocks[0].shape[2]
    total = micro * slots
    first, later = [], []
    for s in range(total):
        b, t = divmod(s, slots)
        first += [
            start(qkv[b].at[t], qkv_v.at[s], sem_in.at[s, 0]),
            start(ctx[b].at[t], ctx_v.at[s], sem_in.at[s, 1]),
        ]
        for j in range(n_blocks):
            at = pl.ds(pl.multiple_of(place[j] * local, local), local)
            first.append(start(blocks[j].at[b, t], dctx_v.at[s, at], sem_in.at[s, 3 + j]))
    for s in range(total):
        b, t = divmod(s, slots)
        for h in range(heads):
            start(probs[b].at[t, h], probs_v.at[s, h], sem_in.at[s, 3 + n_blocks + h])
            start(cot.at[b, t, h], cot_v.at[s, h], sem_in.at[s, 3 + n_blocks + heads + h])
    later.append(start(w, w_v, sem_out.at[0, heads]))
    for s in range(total):
        b, t = divmod(s, slots)
        later.append(start(tok[b].at[t], tok_v.at[s], sem_in.at[s, 2]))
    for copy in first:
        copy.wait()

    def split(s, _):
        rows, d_all = qkv_v[s], dctx_v[s]
        product = d_all.astype(F32) * ctx_v[s].astype(F32)
        for h in range(heads):
            at = h * size
            parts[0, s, h] = rows[:, at : at + size]
            parts[1, s, h] = rows[:, width + at : width + at + size]
            parts[2, s, h] = rows[:, 2 * width + at : 2 * width + at + size]
            parts[3, s, h] = d_all[:, at : at + size]
            deltas[s, h] = jnp.sum(product[:, at : at + size], -1, keepdims=True)
        return _

    lax.fori_loop(0, total, split, 0)

    def leave(s, h):
        return pltpu.make_async_copy(
            grad_v.at[s, h], prev_grad.at[s // slots, lax.rem(s, slots), h], sem_out.at[s, h])

    def leave_back(s):
        return pltpu.make_async_copy(
            back_v.at[s], back.at[s // slots, lax.rem(s, slots)], sem_out.at[s, heads + 1])

    def one_head(i, _):
        s, h = i // heads, lax.rem(i, heads)
        pltpu.make_async_copy(
            probs[0].at[0, h], probs_v.at[s, h], sem_in.at[s, 3 + n_blocks + h]).wait()
        pltpu.make_async_copy(
            cot.at[0, 0, h], cot_v.at[s, h], sem_in.at[s, 3 + n_blocks + heads + h]).wait()
        q, k, v, d_context = (parts[j, s, h] for j in range(4))
        p = probs_v[s, h]
        d_scores = p.astype(F32) * (mm(d_context, v, 1, 1) - deltas[s, h]) + cot_v[s, h].astype(F32)
        grad_v[s, h] = d_scores
        leave(s, h).start()
        d_dots = (d_scores * (1.0 / math.sqrt(size))).astype(BF16)
        parts[0, s, h] = mm(d_dots, k, 1, 0).astype(BF16)
        parts[1, s, h] = mm(q, d_dots, 0, 0).T.astype(BF16)
        parts[2, s, h] = mm(d_context, p, 0, 0).T.astype(BF16)
        return _

    lax.fori_loop(0, total * heads, one_head, 0)
    for copy in later:
        copy.wait()
    acc[...] = jnp.zeros_like(acc)
    bias_acc[...] = jnp.zeros_like(bias_acc)

    def finish(s, _):
        d_qkv = jnp.concatenate([parts[j, s, h] for j in range(3) for h in range(heads)], -1)
        back_v[s] = mm(d_qkv, w_v[...], 1, 1).astype(BF16)
        leave_back(s).start()
        acc[...] += mm(tok_v[s], d_qkv, 0, 0)
        bias_acc[...] += jnp.sum(d_qkv.astype(F32), 0, keepdims=True)
        return _

    lax.fori_loop(0, total, finish, 0)
    for s in range(total):
        for h in range(heads):
            leave(s, h).wait()
        leave_back(s).wait()


def attend_back(place, complete, w_qkv, qkv, ctx, probs, logit_cot, blocks):
    micro, slots, heads, length, _ = logit_cot.shape
    width, cols = w_qkv.shape
    size = cols // 3 // heads
    args = [place, *complete, *qkv, *ctx, *probs, w_qkv, logit_cot, *blocks]
    n = micro * slots * heads * length * length
    total = micro * slots
    square = (total, heads, length, length)
    return pl.pallas_call(
        functools.partial(attend_back_kernel, micro, slots, heads, size, len(blocks)),
        in_specs=[SMEM] + [ANY] * (len(args) - 1),
        out_specs=[ANY, ANY, VMEM, VMEM],
        out_shape=[
            jax.ShapeDtypeStruct(logit_cot.shape, F32),
            jax.ShapeDtypeStruct((micro, slots, length, width), BF16),
            jax.ShapeDtypeStruct((width, cols), F32),
            jax.ShapeDtypeStruct((8, cols), F32),
        ],
        scratch_shapes=[
            pltpu.VMEM((total, length, width), BF16), pltpu.VMEM((total, length, cols), BF16),
            pltpu.VMEM((total, length, cols // 3), BF16),
            pltpu.VMEM((total, length, cols // 3), BF16),
            pltpu.VMEM(square, BF16), pltpu.VMEM(square, BF16), pltpu.VMEM(square, F32),
            pltpu.VMEM((total, length, width), BF16), pltpu.VMEM((width, cols), BF16),
            pltpu.VMEM((4, total, heads, length, size), BF16),
            pltpu.VMEM((total, heads, length, 1), F32),
            pltpu.SemaphoreType.DMA((total, 3 + len(blocks) + 2 * heads)),
            pltpu.SemaphoreType.DMA((total, heads + 2)),
        ],
        compiler_params=pltpu.CompilerParams(vmem_limit_bytes=VMEM_LIMIT),
        cost_estimate=cost(n * 2048 + 4 * total * length * width * cols, n * 8),
        name="attend_back",
    )(*args)


def gelu_and_slope(x):
    bell = jnp.exp(-0.5 * x * x)
    t = 1.0 / (1.0 + (0.3275911 * math.sqrt(0.5)) * jnp.abs(x))
    tail = t * (
        0.5 * 0.254829592
        + t * (
            0.5 * -0.284496736
            + t * (0.5 * 1.421413741 + t * (0.5 * -1.453152027 + t * (0.5 * 1.061405429)))
        )
    ) * bell
    phi = jnp.where(x >= 0, 1.0 - tail, tail)
    return x * phi, phi + x * (bell * (1.0 / math.sqrt(2.0 * math.pi)))


def norm_parts(u):
    centered = u - jnp.mean(u, -1, keepdims=True)
    r = lax.rsqrt(jnp.mean(centered * centered, -1, keepdims=True) + EPSILON)
    return centered * r, r


def norm_back(grad, gain, n, r):
    e = grad * gain
    return r * (e - jnp.mean(e, -1, keepdims=True) - n * jnp.mean(e * n, -1, keepdims=True))


def column_sum(u):
    return jnp.sum(u, 0, keepdims=True)


def feed_forward_kernel(micro, n_ctx, intake, place, refs_in, refs_out, scratch):
    ctx, (tok, cot, vectors, *weights) = refs_in[: micro * n_ctx], refs_in[micro * n_ctx :]
    b_out, g1, s1, b_down, g2, s2 = [vectors[i : i + 1, :] for i in range(6)]
    joint, (smalls, unit_sums), d_ctx = refs_out[:8], refs_out[8:10], refs_out[10:]
    slope, total, *held = scratch
    weights_v, held = held[: -14], held[-14:]
    w_out, b_in = weights_v[-2:]
    ctx_v, tok_v, cot_v, d_ctx_v, *joint_v, sem, io_sem = held
    out_v, act_v, branch_v, inner_v, low_v, att_v, all_v, res_v = joint_v
    units, width = slope.shape[1], total.shape[1]
    chunk = width
    head_width = ctx[0].shape[1]

    def leave(i):
        return pltpu.make_async_copy(joint_v[i], joint[i], io_sem.at[1, i])

    first = [start(tok, tok_v, io_sem.at[0, 0])]
    for i, c in enumerate(ctx):
        b, k = divmod(i, n_ctx)
        rows = pl.ds(b * c.shape[0], c.shape[0])
        first.append(start(c, ctx_v.at[k, rows], io_sem.at[3 + b, k]))
    wait_first, wait_units, weights_of = intake(place, weights, weights_v, sem)
    cot_in = start(cot, cot_v, io_sem.at[0, 1])
    for copy in first:
        copy.wait()
    wait_first()
    attended = b_out
    for k in range(n_ctx):
        attended = attended + mm(ctx_v[k], w_out[k].reshape(-1, width)[:head_width], 1, 0)
    all_v[...] = jnp.concatenate([ctx_v[k] for k in range(n_ctx)], -1)
    n1, r1 = norm_parts(tok_v[...].astype(F32) + attended)
    hidden = n1 * g1 + s1
    low_v[...] = hidden.astype(BF16)
    total[...] = hidden + b_down
    leave(4).start()
    leave(6).start()

    def forward(j, _):
        wait_units(j)
        at = pl.ds(pl.multiple_of(j * chunk, chunk), chunk)
        w_in, w_down = weights_of(j)
        pre = mm(low_v[...], w_in, 1, 1) + b_in[:, at]
        activated, grad = gelu_and_slope(pre)
        activated = activated.astype(BF16)
        act_v[:, at] = activated
        slope[:, at] = grad.astype(BF16)
        total[...] += mm(activated, w_down, 1, 0)
        return _

    lax.fori_loop(0, units // chunk, forward, 0, unroll=UNROLL)
    leave(1).start()
    n2, r2 = norm_parts(total[...])
    out_v[...] = (n2 * g2 + s2).astype(BF16)
    leave(0).start()
    cot_in.wait()
    g = cot_v[...].astype(F32)
    d_second = norm_back(g, g2, n2, r2)
    smalls[3:4, :] = column_sum(d_second)
    smalls[4:5, :] = column_sum(g * n2)
    smalls[5:6, :] = column_sum(g)
    branch_v[...] = d_second.astype(BF16)
    leave(2).start()
    total[...] = d_second

    def backward(j, _):
        at = pl.ds(pl.multiple_of(j * chunk, chunk), chunk)
        w_in, w_down = weights_of(j)
        d_act = mm(branch_v[...], w_down, 1, 1)
        d_inner = d_act * slope[:, at].astype(F32)
        unit_sums[:, at] = jnp.broadcast_to(column_sum(d_inner), (8, chunk))
        d_inner = d_inner.astype(BF16)
        inner_v[:, at] = d_inner
        total[...] += mm(d_inner, w_in, 1, 0)
        return _

    lax.fori_loop(0, units // chunk, backward, 0, unroll=UNROLL)
    leave(3).start()
    d_hidden = total[...]
    d_residual = norm_back(d_hidden, g1, n1, r1)
    d_att = d_residual.astype(BF16)
    for k in range(n_ctx):
        d_ctx_v[k] = mm(d_att, w_out[k].reshape(-1, width)[:head_width], 1, 1).astype(BF16)
        start(d_ctx_v.at[k], d_ctx[k], io_sem.at[2, k])
    att_v[...] = d_att
    res_v[...] = d_residual
    leave(5).start()
    leave(7).start()
    smalls[0:1, :] = column_sum(d_residual)
    smalls[1:2, :] = column_sum(d_hidden * n1)
    smalls[2:3, :] = column_sum(d_hidden)
    smalls[6:8, :] = jnp.zeros((2, width), F32)
    for k in range(n_ctx):
        pltpu.make_async_copy(d_ctx_v.at[k], d_ctx[k], io_sem.at[2, k]).wait()
    for i in range(8):
        leave(i).wait()


def relative_intake(place, weights, held, sem):
    own, *parts = weights
    packed, w_out, b_in = held
    n, mp, rows, width = packed.shape
    stages = [parts[j * n : (j + 1) * n] for j in range(len(parts) // n)]
    piece = b_in.shape[1] // (n * mp)
    pieces = 2 * piece

    def copies(i, at, sources):
        last = [pltpu.make_async_copy(
            own.at[at, pl.ds(pieces, rows - pieces)], packed.at[i, 0, pl.ds(pieces, rows - pieces)],
            sem.at[0, i])]
        main = [pltpu.make_async_copy(
            own.at[at, pl.ds(0, pieces)], packed.at[i, 0, pl.ds(0, pieces)], sem.at[1, i])]
        slot = 1
        for j in range(0, len(sources), 2):
            low, high = sources[j], sources[j + 1]
            slots, cut = pl.ds(slot, low.shape[0]), low.shape[1]
            slot += low.shape[0]
            last.append(pltpu.make_async_copy(
                high.at[:, pl.ds(pieces - cut, rows - pieces)],
                packed.at[i, slots, pl.ds(pieces, rows - pieces)], sem.at[2 + j, i]))
            main += [
                pltpu.make_async_copy(low, packed.at[i, slots, pl.ds(0, cut)], sem.at[3 + j, i]),
                pltpu.make_async_copy(
                    high.at[:, pl.ds(0, pieces - cut)],
                    packed.at[i, slots, pl.ds(cut, pieces - cut)], sem.at[6 + j, i]),
            ]
        return last, main

    for which in range(2):
        for i in range(n):
            for copy in copies(i, place[i], [stage[i] for stage in stages])[which]:
                copy.start()
    some = [stage[0] for stage in stages]

    def wait_first():
        for i in range(n):
            for copy in copies(i, 0, some)[0]:
                copy.wait()
            for s in range(mp):
                for j in range(2):
                    w_out[place[n + s], place[i] + n * j] = (
                        packed[i, s, pieces + 16 * j : pieces + 16 * j + 16]
                    )
                row = packed[i, s, pieces + 32 : pieces + 33, :].astype(F32)
                at = (i * mp + s) * piece
                b_in[:, at : at + piece] = (
                    row[:, :piece] + row[:, 128 : 128 + piece] + row[:, 256 : 256 + piece]
                )

    def wait_units(j):
        for half in range(2):
            for copy in copies(2 * j + half, 0, some)[1]:
                copy.wait()

    def units(j):
        at = pl.ds(2 * j, 2)
        return [packed[at, :, lo : lo + piece].reshape(-1, width) for lo in (0, piece)]

    return wait_first, wait_units, units


def whole_intake(place, weights, held, sem):
    w_in, w_down, w_out, b_in = held
    copies = [start(src, dst, sem.at[0, i]) for i, (src, dst) in enumerate(zip(weights, held))]

    def wait_first():
        for copy in copies:
            copy.wait()

    def units(j):
        return w_in[j], w_down[j]

    return wait_first, lambda j: None, units


def feed_forward(ctx, tokens, cot, vectors, place, weights, intake, block):
    rows, width = tokens.shape
    micro, n_ctx = len(ctx), len(ctx[0])
    head_width = ctx[0][0].shape[1]
    units, held_shapes = block
    args = [place, *[c for blocks in ctx for c in blocks], tokens, cot, vectors, *weights]
    in_specs = [SMEM] + [ANY] * (micro * n_ctx + 2) + [VMEM] + [ANY] * len(weights)
    joint_cols = [(width, BF16), (units, BF16), (width, BF16), (units, BF16), (width, BF16),
                  (width, BF16), (n_ctx * head_width, BF16), (width, F32)]
    n_args = len(args)
    n_out = len(joint_cols) + 2 + n_ctx

    def kernel(place, *refs):
        feed_forward_kernel(
            micro, n_ctx, intake, place, refs[: n_args - 1], refs[n_args - 1 : n_args - 1 + n_out],
            refs[n_args - 1 + n_out :],
        )

    heads_block = pltpu.VMEM((n_ctx, rows, head_width), BF16)
    outs = pl.pallas_call(
        kernel,
        in_specs=in_specs,
        out_specs=[ANY] * len(joint_cols) + [VMEM] * 2 + [ANY] * n_ctx,
        out_shape=[jax.ShapeDtypeStruct((rows, c), t) for c, t in joint_cols]
        + [jax.ShapeDtypeStruct((8, width), F32), jax.ShapeDtypeStruct((8, units), F32)]
        + [jax.ShapeDtypeStruct((rows, head_width), BF16)] * n_ctx,
        scratch_shapes=[
            pltpu.VMEM((rows, units), BF16), pltpu.VMEM((rows, width), F32),
            *[pltpu.VMEM(s, BF16) for s in held_shapes], pltpu.VMEM((1, units), F32),
            heads_block, pltpu.VMEM((rows, width), BF16), pltpu.VMEM((rows, width), BF16),
            heads_block, *[pltpu.VMEM((rows, c), t) for c, t in joint_cols],
            pltpu.SemaphoreType.DMA((9, 8)), pltpu.SemaphoreType.DMA((3 + micro, 8)),
        ],
        compiler_params=pltpu.CompilerParams(vmem_limit_bytes=VMEM_LIMIT),
        cost_estimate=cost(
            2 * rows * width * (4 * units + 2 * width), 4 * units * width + 20 * rows * width,
            rows * units,
        ),
        name="feed_forward",
    )(*args)
    n = len(joint_cols)
    return outs[:n], outs[n], outs[n + 1], outs[n + 2 :]


def weight_grad(half, mp, piece, place, act, branch, inner, low, ctx, att, d_out, got):
    rows, width = branch.shape
    span = mp * piece
    n = act.shape[1] // span // 2
    head_width = ctx.shape[1] // mp
    size = 2 * piece + 32
    cut = size // 2
    order = tuple(reversed(range(n)))

    def kernel(place, act, branch, inner, low, *refs):
        given, outs = refs[:2], refs[2:-7]
        act_v, inner_v, branch_v, low_v, got_v, out_v, sem = refs[-7:]
        moving = [start(low, low_v, sem.at[0, 0]), start(branch, branch_v, sem.at[0, 1])]
        loads, stores = {}, []
        for o in order:
            at = pl.ds((half * n + o) * span, span)
            loads[o] = [
                start(inner.at[:, at], inner_v.at[o], sem.at[1, o]),
                start(act.at[:, at], act_v.at[o], sem.at[2, o]),
            ]
            if not half:
                loads[o].append(start(given[1].at[o], got_v.at[o], sem.at[3, o]))
        if half:
            d_out = outs[1]
            d_out[...] = mm(given[0][...], given[1][...], 0, 0)
        else:
            d_out = given[0]
        for copy in moving:
            copy.wait()
        for o in order:
            for copy in loads[o]:
                copy.wait()
            d_in = mm(inner_v[o], low_v[...], 0, 0)
            d_down = mm(act_v[o], branch_v[...], 0, 0)
            first = place[half * n + o]
            second = jnp.minimum(2 * n + first, head_width // 16 - 1)
            for k in range(mp):
                parts = [d_in[k * piece : (k + 1) * piece], d_down[k * piece : (k + 1) * piece]]
                for p in (first, second):
                    at = place[2 * n + k] * head_width + p * 16
                    at = pl.ds(pl.multiple_of(at, 16), 16)
                    parts.append(d_out[at, :])
                row = 0
                for part in parts:
                    at = slice(row, row + part.shape[0])
                    if not half:
                        part = part.astype(BF16).astype(F32) + got_v[o, k, at].astype(F32)
                    out_v[o, k, at] = part.astype(BF16)
                    row += part.shape[0]
            if half:
                stores.append(start(out_v.at[o], outs[0].at[o], sem.at[4, o]))
            else:
                i = 2 * order.index(o)
                stores += [
                    start(out_v.at[o, :, pl.ds(0, cut)], outs[i], sem.at[4, o]),
                    start(out_v.at[o, :, pl.ds(cut, size - cut)], outs[i + 1], sem.at[5, o]),
                ]
        for copy in stores:
            copy.wait()

    last = (ctx.shape[1], width)
    args = [place, act, branch, inner, low]
    if half:
        args += [ctx, att]
        given_specs = [VMEM, VMEM]
        out_specs = [ANY, VMEM]
        out_shape = [
            jax.ShapeDtypeStruct((n, mp, size, width), BF16), jax.ShapeDtypeStruct(last, F32)
        ]
    else:
        args += [d_out, got]
        given_specs = [VMEM, ANY]
        out_specs = [ANY] * (2 * n)
        out_shape = [
            jax.ShapeDtypeStruct((mp, r, width), BF16) for _ in range(n) for r in (cut, size - cut)
        ]
    wide = pltpu.VMEM((n, rows, span), BF16)
    flat = pltpu.VMEM((rows, width), BF16)
    whole = pltpu.VMEM((n, mp, size, width), BF16)
    return pl.pallas_call(
        kernel,
        in_specs=[SMEM] + [ANY] * 4 + given_specs,
        out_specs=out_specs,
        out_shape=out_shape,
        scratch_shapes=[wide, wide, flat, flat, whole, whole, pltpu.SemaphoreType.DMA((6, n))],
        compiler_params=pltpu.CompilerParams(vmem_limit_bytes=VMEM_LIMIT),
        cost_estimate=cost(2 * rows * width * 5 * width, n * mp * width * 500),
        name="weight_grad",
    )(*args)


def joined(body, shapes, *args, name):
    return pl.pallas_call(
        body,
        out_shape=[jax.ShapeDtypeStruct(s, t) for s, t in shapes],
        compiler_params=pltpu.CompilerParams(vmem_limit_bytes=VMEM_LIMIT),
        name=name,
    )(*args)


def hop_sums(a1, a3, b2, b3):
    def hop_sum(a1, a3, b2, b3, a, b):
        a[...] = (a1[...].astype(F32) + a3[...].astype(F32)).astype(BF16)
        b[...] = (b2[...].astype(F32) + b3[...].astype(F32)).astype(BF16)

    shapes = [(a1.shape, BF16), (b2.shape, BF16)]
    return joined(hop_sum, shapes, a1, a3, b2, b3, name="hop_sum")


def plane_sums(here, a0, a1, a2, b0, b1, b2):
    mp, cut, width = a0.shape
    rows = cut + b0.shape[1]

    def plane_sum(here, a0, a1, a2, b0, b1, b2, out):
        for k in range(mp):
            z = here[k]
            for at, parts in ((slice(0, cut), (a0, a1, a2)), (slice(cut, rows), (b0, b1, b2))):
                out[z, at] = sum(p[k].astype(F32) for p in parts).astype(BF16)

    return pl.pallas_call(
        plane_sum,
        in_specs=[SMEM] + [VMEM] * 6,
        out_shape=jax.ShapeDtypeStruct((mp, rows, width), BF16),
        compiler_params=pltpu.CompilerParams(vmem_limit_bytes=VMEM_LIMIT),
        name="plane_sum",
    )(here, a0, a1, a2, b0, b1, b2)


def plane_gather(first, second, dp, between=lambda *arrays: arrays):
    x, y = flip_pairs(dp, 2), flip_pairs(dp, 4)
    a1, b2 = lax.ppermute(first, "dp", x), lax.ppermute(second, "dp", y)
    a2, b1 = lax.ppermute(first, "dp", y), lax.ppermute(second, "dp", x)
    a1, b2 = between(a1, b2)
    a3, b3 = lax.ppermute(a1, "dp", y), lax.ppermute(b2, "dp", x)
    return [first, a1, a2, a3], [second, b1, b2, b3]


def unpack_grads(packed, piece, head_width):
    n, rows, width = packed.shape

    def kernel(packed, d_in, d_down, d_out, pad, wide):
        for p in range(n):
            whole = packed[p].astype(F32)
            wide[p] = whole[:piece]
            d_down[p] = whole[piece : 2 * piece]
            pad[p] = whole[2 * piece : 2 * piece + 16]
            pad[n + p] = whole[2 * piece + 16 :]
        d_out[...] = pad[: head_width // 16]
        d_in[...] = wide[...].reshape(n * piece, width).T

    shapes = [(width, n * piece), (n, piece, width), (head_width // 16, 16, width)]
    return pl.pallas_call(
        kernel,
        out_shape=[jax.ShapeDtypeStruct(s, F32) for s in shapes],
        scratch_shapes=[pltpu.VMEM((2 * n, 16, width), F32), pltpu.VMEM((n, piece, width), F32)],
        compiler_params=pltpu.CompilerParams(vmem_limit_bytes=VMEM_LIMIT),
        name="unpack_grads",
    )(packed)


def shift_pairs(mp, k):
    return [(i, (i + k) % mp) for i in range(mp)]


def relay(array, mp):
    below, above = [array], [array]
    for hop in range(1, mp):
        pairs = [(i, i + 1) for i in range(hop - 1, mp - 1)]
        below.append(lax.ppermute(below[-1], "mp", pairs))
        above.append(lax.ppermute(above[-1], "mp", [(mp - 1 - i, mp - 1 - j) for i, j in pairs]))
    return below[1:], above[1:]


def flip_pairs(dp, bit):
    return [(i, i ^ bit) for i in range(dp)]


def tie(value, *others):
    return lax.optimization_barrier((value, others))[0]


def halves_of(array, core):
    half = array.shape[0] // 2
    return (
        lax.dynamic_slice_in_dim(array, core * half, half),
        lax.dynamic_slice_in_dim(array, (1 - core) * half, half),
    )


def reorder(rows, order):
    pick = (order[:, None] == jnp.arange(rows.shape[0])[None, :]).astype(F32)
    return jnp.dot(pick, rows, precision=lax.Precision.HIGHEST)


def on_device(
    tokens,
    prev_logits,
    segment_ids,
    query_weight,
    key_weight,
    value_weight,
    query_bias,
    value_bias,
    output_projection_weight,
    output_bias,
    first_gain,
    first_shift,
    inner_projection_weight,
    inner_bias,
    down_projection_weight,
    down_bias,
    second_gain,
    second_shift,
    output_cot,
    logit_cot,
):
    dp = lax.axis_size("dp")
    mp = lax.axis_size("mp")
    me = lax.axis_index("dp")
    mine = lax.axis_index("mp")
    micro_count, slots, local, width = tokens.shape
    length = prev_logits.shape[3]
    head_width = query_weight.shape[1]
    units = inner_projection_weight.shape[1]
    rows = slots * local
    packed = dp == 8 and mp == 4 and micro_count == 2 and units // dp == 96 and head_width == 192
    chips = dp // 2
    swap = flip_pairs(dp, 1)
    piece = units // dp

    def shifted(array, k):
        return lax.ppermute(array, "mp", shift_pairs(mp, k)) if k else array

    if packed:
        own_in = inner_projection_weight.T.reshape(dp, piece, width)
        own_down = down_projection_weight.reshape(dp, piece, width)
        own_out = output_projection_weight.reshape(-1, 16, width)
        high = inner_bias.astype(BF16)
        middle = (inner_bias - high.astype(F32)).astype(BF16)
        lowest = (inner_bias - high.astype(F32) - middle.astype(F32)).astype(BF16)
        own_bias = jnp.concatenate(
            [jnp.pad(v.reshape(dp, 1, piece), ((0, 0), (0, 15), (0, 128 - piece)))
             for v in (high, middle, lowest)]
            + [jnp.zeros((dp, 16, width - 3 * 128), BF16)], 2
        )
        own_out = jnp.concatenate([own_out, own_out[: 2 * dp - own_out.shape[0]]], 0)
        own_pack = jnp.concatenate([own_in, own_down, own_out[:dp], own_out[dp:], own_bias], 1)
        sent = lax.dynamic_index_in_dim(own_pack, me, 0, False)
        below, above = relay(sent, mp)
        first_hop = (below[0], above[0])
        from_z = jnp.stack(
            [jnp.where(mine >= k, below[k - 1], above[mp - k - 1]) for k in range(1, mp)]
        )
        k_of = jnp.arange(mp)
        cut = piece + piece // 3
        ff_place = me ^ (jnp.arange(dp) // chips + jnp.arange(dp) % chips * 2)
        ff_place = jnp.concatenate([ff_place, k_of]).astype(jnp.int32)
        intake = relative_intake
        block = (units * mp, [(dp, mp, 2 * piece + 48, width), (mp, 2 * dp, 16, width)])
    else:
        in_all = lax.all_gather(inner_projection_weight.T, "mp", axis=0, tiled=True)
        down_all = lax.all_gather(down_projection_weight, "mp", axis=0, tiled=True)
        wo_all = lax.all_gather(output_projection_weight, "mp")
        wo_all = jnp.stack(
            [lax.dynamic_index_in_dim(wo_all, (mine - k) % mp, 0, False) for k in range(mp)]
        )
        weights = [
            in_all.reshape(-1, width, width), down_all.reshape(-1, width, width), wo_all[:, None],
            lax.all_gather(inner_bias, "mp").reshape(1, -1),
        ]
        ff_place = jnp.zeros((dp,), jnp.int32)
        intake = whole_intake
        first_hop = ()
        square = (units * mp // width, width, width)
        block = (units * mp, [square, square, (mp, 1, head_width, width)])

    def gather_tokens(b, *after):
        return lax.all_gather(tie(tokens[b], *after), "mp", axis=1, tiled=True)

    complete = [gather_tokens(0, *first_hop)]
    for b in range(1, micro_count):
        complete.append(gather_tokens(b, complete[b - 1]))
    w_qkv = jnp.concatenate([query_weight, key_weight, value_weight], 1)
    bias_row = jnp.concatenate([query_bias, jnp.zeros_like(query_bias), value_bias])[None]
    vectors = jnp.stack(
        [output_bias, first_gain, first_shift, down_bias, second_gain, second_shift]
        + [jnp.zeros_like(down_bias)] * 2
    )
    own_tokens = tokens.reshape(-1, width)
    own_cot = output_cot.reshape(-1, width)
    place = jnp.stack([(mine + k) % mp for k in range(mp)]).astype(jnp.int32)
    logits = None

    def attend_fully(b, logits):
        logits, probs, qkv, ctx = attend(
            b, complete[b], w_qkv, bias_row, prev_logits, segment_ids, logits
        )
        blocks = []
        for k in range(mp):
            at = ((mine + k) % mp) * local
            part = lax.dynamic_slice(ctx, (0, at, 0), (slots, local, head_width))
            blocks.append(shifted(part, k).reshape(rows, head_width))
        return logits, (probs, qkv, ctx), blocks

    def to_heads(d_ctx):
        return [
            shifted(part, (mp - k) % mp).reshape(micro_count, slots, local, head_width)
            for k, part in enumerate(d_ctx)
        ]

    kept, blocks = [], []
    for b in range(micro_count):
        logits, each, ctx_blocks = attend_fully(b, logits)
        kept.append(each)
        blocks.append(ctx_blocks)
        if packed and b == 0:
            firsts, seconds = plane_gather(
                from_z[:, :cut], from_z[:, cut:], dp, lambda *arrays: tie(arrays, each[2])
            )
            firsts, seconds, blocks[0], complete[1] = lax.optimization_barrier(
                (firsts, seconds, blocks[0], complete[1])
            )
            weights = [own_pack]
            for group in (firsts, seconds):
                weights += group + [lax.ppermute(a, "dp", swap) for a in group]
    blocks = lax.optimization_barrier(blocks)
    joint, small, unit_sums, d_ctx = feed_forward(
        blocks, own_tokens, own_cot, vectors, ff_place, weights, intake, block
    )
    d_blocks = to_heads(d_ctx)
    layer, act, branch, inner, low, att, ctx_all, residual = joint

    def back_through(*after):
        d_blocks[0] = tie(d_blocks[0], *after)
        probs, qkv, ctx = zip(*kept)
        return attend_back(place, complete, w_qkv, qkv, ctx, probs, logit_cot, d_blocks)

    unit_total = unit_sums[0]
    if packed:
        z, i = jnp.meshgrid(jnp.arange(mp), jnp.arange(dp), indexing="ij")
        at = me ^ i
        at = ((at % 2 * chips + at // 2) * mp + k_of[(mine - z) % mp]).reshape(-1)
        unit_total = reorder(unit_total.reshape(-1, piece), at).reshape(-1)
    vector = jnp.concatenate([small[:6].reshape(-1), unit_total])
    cols = 3 * head_width
    vector = jnp.pad(vector, (0, -vector.shape[0] % (24 * cols))).reshape(-1, cols)
    at = width + 8
    def joint_grads(*after):
        return tie(jnp.concatenate([acc, bias_acc, vector], 0), *after)

    if packed:
        pairs = [act, branch, inner, low, ctx_all, att]
        other, d_out = weight_grad(1, mp, piece, ff_place, *pairs, None, None)
        got = lax.ppermute(other, "dp", swap)
        prev_grad, back, acc, bias_acc = back_through(d_out)
        got, prev_grad = lax.optimization_barrier((got, prev_grad))
        sums = weight_grad(0, mp, piece, ff_place, *pairs, d_out, got)
        cut = 2 * piece + 32 >> 1
        x, y = flip_pairs(dp, 2), flip_pairs(dp, 4)
        a3, b3, a2, b2, a1, b1, a0, b0 = sums
        a3, b3 = lax.ppermute(a3, "dp", y), lax.ppermute(b3, "dp", x)
        a2, b1 = lax.ppermute(a2, "dp", y), lax.ppermute(b1, "dp", x)
        a1, b2 = hop_sums(a1, a3, b2, b3)
        a1, b2 = lax.ppermute(a1, "dp", x), lax.ppermute(b2, "dp", y)
        back = lax.psum_scatter(back, "mp", scatter_dimension=2, tiled=True)
        a0, back = lax.optimization_barrier((a0, back))
        total = plane_sums(((mine - k_of) % mp).astype(jnp.int32), a0, a1, a2, b0, b1, b2)
        scattered = lax.psum_scatter(total, "mp", scatter_dimension=0)
        keep, send = halves_of(joint_grads(total), me % 2)
        keep = keep + lax.ppermute(send, "dp", swap)
        quarter = keep.shape[0] // 2
        top, low_part = keep[:quarter], keep[quarter:]
        top, low_part = (
            top + lax.ppermute(top, "dp", x), low_part + lax.ppermute(low_part, "dp", y)
        )
        top, low_part = (
            top + lax.ppermute(top, "dp", y), low_part + lax.ppermute(low_part, "dp", x)
        )
        keep = jnp.concatenate([top, low_part], 0)
        scattered, keep = lax.optimization_barrier((scattered, keep))
        gathered = lax.all_gather(scattered, "dp")
        other = lax.ppermute(keep, "dp", swap)
        summed = jnp.where(
            me % 2 == 0, jnp.concatenate([keep, other], 0), jnp.concatenate([other, keep], 0)
        )
        vector = summed[at:]
        for bit in (1, 2):
            vector += lax.ppermute(vector, "mp", flip_pairs(mp, bit))
        d_in, d_down, d_out = unpack_grads(gathered, piece, head_width)
        inner_weight_grad = d_in
        down_weight_grad = d_down.reshape(units, width)
        output_weight_grad = d_out.reshape(head_width, width)
    else:
        g_down = mm(act, branch, 0, 0)
        g_in = mm(inner, low, 0, 0)
        g_out = mm(ctx_all, att, 0, 0)
        vector = lax.psum(vector, "mp")
        prev_grad, back, acc, bias_acc = back_through()
        summed = lax.psum(joint_grads(), "dp")
        vector = summed[at:]
        back = lax.psum_scatter(back, "mp", scatter_dimension=2, tiled=True)
        g_in = lax.psum_scatter(g_in, "mp", scatter_dimension=0, tiled=True)
        inner_weight_grad = lax.psum(g_in, "dp").T
        g_down = lax.psum_scatter(g_down, "mp", scatter_dimension=0, tiled=True)
        down_weight_grad = lax.psum(g_down, "dp")
        g_out = g_out.reshape(mp, head_width, width)
        out_sum = 0.0
        for k in range(mp):
            out_sum += shifted(g_out[k], (mp - k) % mp)
        output_weight_grad = lax.psum(out_sum, "dp")
    token_grads = residual.reshape(tokens.shape) + back.astype(F32)
    vector = vector.reshape(-1)
    small = vector[: 6 * width].reshape(6, width)
    unit_total = vector[6 * width : 6 * width + units * mp]
    inner_bias_grad = lax.dynamic_index_in_dim(unit_total.reshape(mp, units), mine, 0, False)
    return (
        layer.reshape(tokens.shape),
        logits,
        token_grads,
        prev_grad,
        summed[:width, :head_width],
        summed[:width, head_width : 2 * head_width],
        summed[:width, 2 * head_width :],
        summed[width, :head_width],
        summed[width, 2 * head_width :],
        output_weight_grad,
        small[0],
        small[1],
        small[2],
        inner_weight_grad,
        inner_bias_grad,
        down_weight_grad,
        small[3],
        small[4],
        small[5],
    )


def solution(mesh):
    rows = P(None, "dp", "mp", None)
    heads = P(None, "dp", "mp", None, None)
    cols, deep, vec, same = P(None, "mp"), P("mp", None), P("mp"), P()
    in_specs = (
        rows, heads, P(None, "dp", None), cols, cols, cols, vec, vec, deep, same, same, same,
        cols, vec, deep, same, same, same, rows, heads,
    )
    out_specs = (
        rows, heads, rows, heads, cols, cols, cols, vec, vec, deep, same, same, same, cols, vec,
        deep, same, same, same,
    )
    return jax.shard_map(
        on_device, mesh=mesh, in_specs=in_specs, out_specs=out_specs, check_vma=False
    )
```

```python
import functools
import math

import jax
import jax.numpy as jnp
from jax import lax
from jax.experimental import pallas as pl
from jax.experimental.pallas import tpu as pltpu
from jax.sharding import PartitionSpec as P

EPSILON = 1e-12
MASKED = -1e30
F32 = jnp.float32
BF16 = jnp.bfloat16
VMEM_LIMIT = 60 * 1024 * 1024
UNROLL = 2
ANY = pl.BlockSpec(memory_space=pl.ANY)
VMEM = pl.BlockSpec(memory_space=pltpu.VMEM)
SMEM = pl.BlockSpec(memory_space=pltpu.SMEM)


def mm(a, b, ca, cb):
    return lax.dot_general(a, b, (((ca,), (cb,)), ((), ())), preferred_element_type=F32)


def cost(flops, moved, exps=0):
    return pl.CostEstimate(flops=int(flops), bytes_accessed=int(moved), transcendentals=int(exps))


def start(src, dst, sem):
    copy = pltpu.make_async_copy(src, dst, sem)
    copy.start()
    return copy

def attend_kernel(b, slots, heads, size, tok, w, bias, prev, seg, *refs):
    logits, probs, qkv, ctx = refs[-17:-13]
    tok_v, prev_v, logits_v, probs_v, qkv_v, ctx_v, w_v, qs, ks, vs = refs[-13:-3]
    sem_in, sem_out, sem_w = refs[-3:]
    length = tok_v.shape[1]
    width = heads * size
    w_in = start(w, w_v, sem_w)
    tok_in, prev_in = [], []
    for s in range(slots):
        tok_in.append(start(tok.at[s], tok_v.at[s], sem_in.at[s, heads]))
        if s == 0:
            prev_in += [start(prev.at[b, s, h], prev_v.at[s, h], sem_in.at[s, h]) for h in range(heads)]
    w_in.wait()
    for s in range(1, slots):
        prev_in += [start(prev.at[b, s, h], prev_v.at[s, h], sem_in.at[s, h]) for h in range(heads)]
    for copy in tok_in:
        copy.wait()

    def project(s, _):
        rows = (mm(tok_v[s], w_v[...], 1, 0) + bias[...]).astype(BF16)
        qkv_v[s] = rows
        start(qkv_v.at[s], qkv.at[s], sem_out.at[s, 2 * heads])
        for h in range(heads):
            at = h * size
            qs[s, h] = rows[:, at : at + size] * (1.0 / math.sqrt(size))
            ks[s, h] = rows[:, width + at : width + at + size]
            vs[s, h] = rows[:, 2 * width + at : 2 * width + at + size]
        return _

    lax.fori_loop(0, slots, project, 0)

    def one_head(i, _):
        s, h = i // heads, lax.rem(i, heads)
        seg_k = seg[b, pl.ds(s, 1), :]
        seg_q = jnp.broadcast_to(seg_k, (8, length)).T[:, :1]
        pltpu.make_async_copy(prev.at[b, s, h], prev_v.at[s, h], sem_in.at[s, h]).wait()
        q, k, v = qs[s, h], ks[s, h], vs[s, h]
        scores = mm(q, k, 1, 1) + prev_v[s, h].astype(F32)
        logits_v[s, h] = scores.astype(BF16)
        start(logits_v.at[s, h], logits.at[b, s, h], sem_out.at[s, h])
        masked = jnp.where(seg_q == seg_k, scores, MASKED)
        exponent = jnp.exp(masked - jnp.max(masked, -1, keepdims=True))
        p = (exponent * (1.0 / jnp.sum(exponent, -1, keepdims=True))).astype(BF16)
        probs_v[s, h] = p
        start(probs_v.at[s, h], probs.at[s, h], sem_out.at[s, heads + h])
        qs[s, h] = mm(p, v, 1, 0).astype(BF16)
        return _

    lax.fori_loop(0, slots * heads, one_head, 0)
    for s in range(slots):
        ctx_v[s] = jnp.concatenate([qs[s, h] for h in range(heads)], -1)
        start(ctx_v.at[s], ctx.at[s], sem_out.at[s, 2 * heads + 1])
    for s in range(slots):
        for h in range(heads):
            pltpu.make_async_copy(logits_v.at[s, h], logits.at[b, s, h], sem_out.at[s, h]).wait()
            pltpu.make_async_copy(probs_v.at[s, h], probs.at[s, h], sem_out.at[s, heads + h]).wait()
        pltpu.make_async_copy(qkv_v.at[s], qkv.at[s], sem_out.at[s, 2 * heads]).wait()
        pltpu.make_async_copy(ctx_v.at[s], ctx.at[s], sem_out.at[s, 2 * heads + 1]).wait()


def attend(b, complete, w_qkv, bias, prev_logits, seg, logits_in):
    slots, length, width = complete.shape
    heads = prev_logits.shape[2]
    cols = w_qkv.shape[1]
    size = cols // 3 // heads
    args = [complete, w_qkv, bias, prev_logits, seg]
    in_specs = [ANY, ANY, VMEM, ANY, VMEM]
    alias = {}
    if logits_in is not None:
        alias = {len(args): 0}
        args.append(logits_in)
        in_specs.append(ANY)
    n = slots * heads * length * length
    square = pltpu.VMEM((slots, heads, length, length), BF16)
    return pl.pallas_call(
        functools.partial(attend_kernel, b, slots, heads, size),
        in_specs=in_specs,
        out_specs=[ANY] * 4,
        out_shape=[
            jax.ShapeDtypeStruct(prev_logits.shape, BF16),
            jax.ShapeDtypeStruct((slots, heads, length, length), BF16),
            jax.ShapeDtypeStruct((slots, length, cols), BF16),
            jax.ShapeDtypeStruct((slots, length, cols // 3), BF16),
        ],
        scratch_shapes=[
            pltpu.VMEM((slots, length, width), BF16), square, square, square,
            pltpu.VMEM((slots, length, cols), BF16), pltpu.VMEM((slots, length, cols // 3), BF16),
            pltpu.VMEM((width, cols), BF16),
            *[pltpu.VMEM((slots, heads, length, size), BF16)] * 3,
            pltpu.SemaphoreType.DMA((slots, heads + 1)),
            pltpu.SemaphoreType.DMA((slots, 2 * heads + 2)), pltpu.SemaphoreType.DMA,
        ],
        input_output_aliases=alias,
        compiler_params=pltpu.CompilerParams(vmem_limit_bytes=VMEM_LIMIT),
        cost_estimate=cost(n * 1024 + 2 * slots * length * width * cols, n * 6, n),
        name="attend",
    )(*args)


def attend_back_kernel(micro, slots, heads, size, n_blocks, place, *refs):
    tok, qkv, ctx, probs = (refs[i * micro : (i + 1) * micro] for i in range(4))
    w, cot, *blocks = refs[4 * micro : 4 * micro + 2 + n_blocks]
    prev_grad, acc, bias_acc, *backs = refs[-16 - micro : -13]
    tok_v, qkv_v, ctx_v, dctx_v, probs_v, cot_v, grad_v, back_v, w_v, parts, deltas = refs[-13:-2]
    sem_in, sem_out = refs[-2:]
    length = tok_v.shape[1]
    width = heads * size
    local = blocks[0].shape[2]
    total = micro * slots
    first, later = [], []
    for s in range(total):
        b, t = divmod(s, slots)
        first += [
            start(qkv[b].at[t], qkv_v.at[s], sem_in.at[s, 0]),
            start(ctx[b].at[t], ctx_v.at[s], sem_in.at[s, 1]),
        ]
        for j in range(n_blocks):
            at = pl.ds(pl.multiple_of(place[j] * local, local), local)
            first.append(start(blocks[j].at[b, t], dctx_v.at[s, at], sem_in.at[s, 3 + j]))
    for s in range(total):
        b, t = divmod(s, slots)
        for h in range(heads):
            start(probs[b].at[t, h], probs_v.at[s, h], sem_in.at[s, 3 + n_blocks + h])
            start(cot.at[b, t, h], cot_v.at[s, h], sem_in.at[s, 3 + n_blocks + heads + h])
    later.append(start(w, w_v, sem_out.at[0, heads]))
    for s in range(total):
        b, t = divmod(s, slots)
        later.append(start(tok[b].at[t], tok_v.at[s], sem_in.at[s, 2]))
    for copy in first:
        copy.wait()

    def split(s, _):
        rows, d_all = qkv_v[s], dctx_v[s]
        product = d_all.astype(F32) * ctx_v[s].astype(F32)
        for h in range(heads):
            at = h * size
            parts[0, s, h] = rows[:, at : at + size]
            parts[1, s, h] = rows[:, width + at : width + at + size]
            parts[2, s, h] = rows[:, 2 * width + at : 2 * width + at + size]
            parts[3, s, h] = d_all[:, at : at + size]
            deltas[s, h] = jnp.sum(product[:, at : at + size], -1, keepdims=True)
        return _

    lax.fori_loop(0, total, split, 0)

    def leave(s, h):
        return pltpu.make_async_copy(
            grad_v.at[s, h], prev_grad.at[s // slots, lax.rem(s, slots), h], sem_out.at[s, h])

    def leave_back(s, b):
        return pltpu.make_async_copy(
            back_v.at[s], backs[b].at[lax.rem(s, slots)], sem_out.at[s, heads + 1])

    def one_head(i, _):
        s, h = i // heads, lax.rem(i, heads)
        pltpu.make_async_copy(
            probs[0].at[0, h], probs_v.at[s, h], sem_in.at[s, 3 + n_blocks + h]).wait()
        pltpu.make_async_copy(
            cot.at[0, 0, h], cot_v.at[s, h], sem_in.at[s, 3 + n_blocks + heads + h]).wait()
        q, k, v, d_context = (parts[j, s, h] for j in range(4))
        p = probs_v[s, h]
        d_scores = p.astype(F32) * (mm(d_context, v, 1, 1) - deltas[s, h]) + cot_v[s, h].astype(F32)
        grad_v[s, h] = d_scores
        leave(s, h).start()
        d_dots = (d_scores * (1.0 / math.sqrt(size))).astype(BF16)
        parts[0, s, h] = mm(d_dots, k, 1, 0).astype(BF16)
        parts[1, s, h] = mm(q, d_dots, 0, 0).T.astype(BF16)
        parts[2, s, h] = mm(d_context, p, 0, 0).T.astype(BF16)
        return _

    lax.fori_loop(0, total * heads, one_head, 0)
    for copy in later:
        copy.wait()
    acc[...] = jnp.zeros_like(acc)
    bias_acc[...] = jnp.zeros_like(bias_acc)

    def finish(s, _):
        d_qkv = jnp.concatenate([parts[j, s, h] for j in range(3) for h in range(heads)], -1)
        back_v[s] = mm(d_qkv, w_v[...], 1, 1).astype(BF16)
        for b in range(micro):
            pl.when(s // slots == b)(leave_back(s, b).start)
        acc[...] += mm(tok_v[s], d_qkv, 0, 0)
        bias_acc[...] += jnp.sum(d_qkv.astype(F32), 0, keepdims=True)
        return _

    lax.fori_loop(0, total, finish, 0)
    for s in range(total):
        for h in range(heads):
            leave(s, h).wait()
        leave_back(s, 0).wait()


def attend_back(place, complete, w_qkv, qkv, ctx, probs, logit_cot, blocks):
    micro, slots, heads, length, _ = logit_cot.shape
    width, cols = w_qkv.shape
    size = cols // 3 // heads
    args = [place, *complete, *qkv, *ctx, *probs, w_qkv, logit_cot, *blocks]
    n = micro * slots * heads * length * length
    total = micro * slots
    square = (total, heads, length, length)
    return pl.pallas_call(
        functools.partial(attend_back_kernel, micro, slots, heads, size, len(blocks)),
        in_specs=[SMEM] + [ANY] * (len(args) - 1),
        out_specs=[ANY, VMEM, VMEM] + [ANY] * micro,
        out_shape=[
            jax.ShapeDtypeStruct(logit_cot.shape, F32),
            jax.ShapeDtypeStruct((width, cols), F32),
            jax.ShapeDtypeStruct((8, cols), F32),
        ]
        + [jax.ShapeDtypeStruct((slots, length, width), BF16)] * micro,
        scratch_shapes=[
            pltpu.VMEM((total, length, width), BF16), pltpu.VMEM((total, length, cols), BF16),
            pltpu.VMEM((total, length, cols // 3), BF16),
            pltpu.VMEM((total, length, cols // 3), BF16),
            pltpu.VMEM(square, BF16), pltpu.VMEM(square, BF16), pltpu.VMEM(square, F32),
            pltpu.VMEM((total, length, width), BF16), pltpu.VMEM((width, cols), BF16),
            pltpu.VMEM((4, total, heads, length, size), BF16),
            pltpu.VMEM((total, heads, length, 1), F32),
            pltpu.SemaphoreType.DMA((total, 3 + len(blocks) + 2 * heads)),
            pltpu.SemaphoreType.DMA((total, heads + 2)),
        ],
        compiler_params=pltpu.CompilerParams(vmem_limit_bytes=VMEM_LIMIT),
        cost_estimate=cost(n * 2048 + 4 * total * length * width * cols, n * 8),
        name="attend_back",
    )(*args)


def gelu_and_slope(x):
    bell = jnp.exp(-0.5 * x * x)
    t = 1.0 / (1.0 + (0.3275911 * math.sqrt(0.5)) * jnp.abs(x))
    tail = t * (
        0.5 * 0.254829592
        + t * (
            0.5 * -0.284496736
            + t * (0.5 * 1.421413741 + t * (0.5 * -1.453152027 + t * (0.5 * 1.061405429)))
        )
    ) * bell
    phi = jnp.where(x >= 0, 1.0 - tail, tail)
    return x * phi, phi + x * (bell * (1.0 / math.sqrt(2.0 * math.pi)))


def norm_parts(u):
    centered = u - jnp.mean(u, -1, keepdims=True)
    r = lax.rsqrt(jnp.mean(centered * centered, -1, keepdims=True) + EPSILON)
    return centered * r, r


def norm_back(grad, gain, n, r):
    e = grad * gain
    return r * (e - jnp.mean(e, -1, keepdims=True) - n * jnp.mean(e * n, -1, keepdims=True))


def column_sum(u):
    return jnp.sum(u, 0, keepdims=True)


def feed_forward_kernel(micro, n_ctx, intake, place, refs_in, refs_out, scratch):
    ctx, (tok, cot, vectors, *weights) = refs_in[: micro * n_ctx], refs_in[micro * n_ctx :]
    b_out, g1, s1, b_down, g2, s2 = [vectors[i : i + 1, :] for i in range(6)]
    joint, (smalls, unit_sums), d_ctx = refs_out[:8], refs_out[8:10], refs_out[10:]
    slope, total, *held = scratch
    weights_v, held = held[: -14], held[-14:]
    w_out, b_in = weights_v[-2:]
    ctx_v, tok_v, cot_v, d_ctx_v, *joint_v, sem, io_sem = held
    out_v, act_v, branch_v, inner_v, low_v, att_v, all_v, res_v = joint_v
    units, width = slope.shape[1], total.shape[1]
    chunk = width
    head_width = ctx[0].shape[1]

    def leave(i):
        return pltpu.make_async_copy(joint_v[i], joint[i], io_sem.at[1, i])

    first = [start(tok, tok_v, io_sem.at[0, 0])]
    for i, c in enumerate(ctx):
        b, k = divmod(i, n_ctx)
        rows = pl.ds(b * c.shape[0], c.shape[0])
        first.append(start(c, ctx_v.at[k, rows], io_sem.at[3 + b, k]))
    wait_first, wait_units, weights_of = intake(place, weights, weights_v, sem)
    cot_in = start(cot, cot_v, io_sem.at[0, 1])
    for copy in first:
        copy.wait()
    wait_first()
    attended = b_out
    for k in range(n_ctx):
        attended = attended + mm(ctx_v[k], w_out[k].reshape(-1, width)[:head_width], 1, 0)
    all_v[...] = jnp.concatenate([ctx_v[k] for k in range(n_ctx)], -1)
    n1, r1 = norm_parts(tok_v[...].astype(F32) + attended)
    hidden = n1 * g1 + s1
    low_v[...] = hidden.astype(BF16)
    total[...] = hidden + b_down
    leave(4).start()
    leave(6).start()

    def forward(j, _):
        wait_units(j)
        at = pl.ds(pl.multiple_of(j * chunk, chunk), chunk)
        w_in, w_down = weights_of(j)
        pre = mm(low_v[...], w_in, 1, 1) + b_in[:, at]
        activated, grad = gelu_and_slope(pre)
        activated = activated.astype(BF16)
        act_v[:, at] = activated
        slope[:, at] = grad.astype(BF16)
        total[...] += mm(activated, w_down, 1, 0)
        return _

    lax.fori_loop(0, units // chunk, forward, 0, unroll=UNROLL)
    leave(1).start()
    n2, r2 = norm_parts(total[...])
    out_v[...] = (n2 * g2 + s2).astype(BF16)
    leave(0).start()
    cot_in.wait()
    g = cot_v[...].astype(F32)
    d_second = norm_back(g, g2, n2, r2)
    smalls[3:4, :] = column_sum(d_second)
    smalls[4:5, :] = column_sum(g * n2)
    smalls[5:6, :] = column_sum(g)
    branch_v[...] = d_second.astype(BF16)
    leave(2).start()
    total[...] = d_second

    def backward(j, _):
        at = pl.ds(pl.multiple_of(j * chunk, chunk), chunk)
        w_in, w_down = weights_of(j)
        d_act = mm(branch_v[...], w_down, 1, 1)
        d_inner = d_act * slope[:, at].astype(F32)
        unit_sums[:, at] = jnp.broadcast_to(column_sum(d_inner), (8, chunk))
        d_inner = d_inner.astype(BF16)
        inner_v[:, at] = d_inner
        total[...] += mm(d_inner, w_in, 1, 0)
        return _

    lax.fori_loop(0, units // chunk, backward, 0, unroll=UNROLL)
    leave(3).start()
    d_hidden = total[...]
    d_residual = norm_back(d_hidden, g1, n1, r1)
    d_att = d_residual.astype(BF16)
    for k in range(n_ctx):
        d_ctx_v[k] = mm(d_att, w_out[k].reshape(-1, width)[:head_width], 1, 1).astype(BF16)
        start(d_ctx_v.at[k], d_ctx[k], io_sem.at[2, k])
    att_v[...] = d_att
    res_v[...] = d_residual
    leave(5).start()
    leave(7).start()
    smalls[0:1, :] = column_sum(d_residual)
    smalls[1:2, :] = column_sum(d_hidden * n1)
    smalls[2:3, :] = column_sum(d_hidden)
    smalls[6:8, :] = jnp.zeros((2, width), F32)
    for k in range(n_ctx):
        pltpu.make_async_copy(d_ctx_v.at[k], d_ctx[k], io_sem.at[2, k]).wait()
    for i in range(8):
        leave(i).wait()


def relative_intake(place, weights, held, sem):
    own, *parts = weights
    packed, w_out, b_in = held
    n, mp, rows, width = packed.shape
    stages = [parts[j * n : (j + 1) * n] for j in range(len(parts) // n)]
    piece = b_in.shape[1] // (n * mp)
    pieces = 2 * piece

    def copies(i, at, sources):
        last = [pltpu.make_async_copy(
            own.at[at, pl.ds(pieces, rows - pieces)], packed.at[i, 0, pl.ds(pieces, rows - pieces)],
            sem.at[0, i])]
        main = [pltpu.make_async_copy(
            own.at[at, pl.ds(0, pieces)], packed.at[i, 0, pl.ds(0, pieces)], sem.at[1, i])]
        slot = 1
        for j in range(0, len(sources), 2):
            low, high = sources[j], sources[j + 1]
            slots, cut = pl.ds(slot, low.shape[0]), low.shape[1]
            slot += low.shape[0]
            last.append(pltpu.make_async_copy(
                high.at[:, pl.ds(pieces - cut, rows - pieces)],
                packed.at[i, slots, pl.ds(pieces, rows - pieces)], sem.at[2 + j, i]))
            main += [
                pltpu.make_async_copy(low, packed.at[i, slots, pl.ds(0, cut)], sem.at[3 + j, i]),
                pltpu.make_async_copy(
                    high.at[:, pl.ds(0, pieces - cut)],
                    packed.at[i, slots, pl.ds(cut, pieces - cut)], sem.at[6 + j, i]),
            ]
        return last, main

    for which in range(2):
        for i in range(n):
            for copy in copies(i, place[i], [stage[i] for stage in stages])[which]:
                copy.start()
    some = [stage[0] for stage in stages]

    def wait_first():
        for i in range(n):
            for copy in copies(i, 0, some)[0]:
                copy.wait()
            for s in range(mp):
                for j in range(2):
                    w_out[place[n + s], place[i] + n * j] = (
                        packed[i, s, pieces + 16 * j : pieces + 16 * j + 16]
                    )
                row = packed[i, s, pieces + 32 : pieces + 33, :].astype(F32)
                at = (i * mp + s) * piece
                b_in[:, at : at + piece] = (
                    row[:, :piece] + row[:, 128 : 128 + piece] + row[:, 256 : 256 + piece]
                )

    def wait_units(j):
        for half in range(2):
            for copy in copies(2 * j + half, 0, some)[1]:
                copy.wait()

    def units(j):
        at = pl.ds(2 * j, 2)
        return [packed[at, :, lo : lo + piece].reshape(-1, width) for lo in (0, piece)]

    return wait_first, wait_units, units


def whole_intake(place, weights, held, sem):
    w_in, w_down, w_out, b_in = held
    copies = [start(src, dst, sem.at[0, i]) for i, (src, dst) in enumerate(zip(weights, held))]

    def wait_first():
        for copy in copies:
            copy.wait()

    def units(j):
        return w_in[j], w_down[j]

    return wait_first, lambda j: None, units


def feed_forward(ctx, tokens, cot, vectors, place, weights, intake, block):
    rows, width = tokens.shape
    micro, n_ctx = len(ctx), len(ctx[0])
    head_width = ctx[0][0].shape[1]
    units, held_shapes = block
    args = [place, *[c for blocks in ctx for c in blocks], tokens, cot, vectors, *weights]
    in_specs = [SMEM] + [ANY] * (micro * n_ctx + 2) + [VMEM] + [ANY] * len(weights)
    joint_cols = [(width, BF16), (units, BF16), (width, BF16), (units, BF16), (width, BF16),
                  (width, BF16), (n_ctx * head_width, BF16), (width, F32)]
    n_args = len(args)
    n_out = len(joint_cols) + 2 + n_ctx

    def kernel(place, *refs):
        feed_forward_kernel(
            micro, n_ctx, intake, place, refs[: n_args - 1], refs[n_args - 1 : n_args - 1 + n_out],
            refs[n_args - 1 + n_out :],
        )

    heads_block = pltpu.VMEM((n_ctx, rows, head_width), BF16)
    outs = pl.pallas_call(
        kernel,
        in_specs=in_specs,
        out_specs=[ANY] * len(joint_cols) + [VMEM] * 2 + [ANY] * n_ctx,
        out_shape=[jax.ShapeDtypeStruct((rows, c), t) for c, t in joint_cols]
        + [jax.ShapeDtypeStruct((8, width), F32), jax.ShapeDtypeStruct((8, units), F32)]
        + [jax.ShapeDtypeStruct((rows, head_width), BF16)] * n_ctx,
        scratch_shapes=[
            pltpu.VMEM((rows, units), BF16), pltpu.VMEM((rows, width), F32),
            *[pltpu.VMEM(s, BF16) for s in held_shapes], pltpu.VMEM((1, units), F32),
            heads_block, pltpu.VMEM((rows, width), BF16), pltpu.VMEM((rows, width), BF16),
            heads_block, *[pltpu.VMEM((rows, c), t) for c, t in joint_cols],
            pltpu.SemaphoreType.DMA((9, 8)), pltpu.SemaphoreType.DMA((3 + micro, 8)),
        ],
        compiler_params=pltpu.CompilerParams(vmem_limit_bytes=VMEM_LIMIT),
        cost_estimate=cost(
            2 * rows * width * (4 * units + 2 * width), 4 * units * width + 20 * rows * width,
            rows * units,
        ),
        name="feed_forward",
    )(*args)
    n = len(joint_cols)
    return outs[:n], outs[n], outs[n + 1], outs[n + 2 :]


def weight_grad(half, mp, piece, place, act, branch, inner, low, ctx, att, d_out, got):
    rows, width = branch.shape
    span = mp * piece
    n = act.shape[1] // span // 2
    head_width = ctx.shape[1] // mp
    size = 2 * piece + 32
    cut = size // 2
    order = tuple(reversed(range(n)))

    def kernel(place, act, branch, inner, low, *refs):
        given, outs = refs[:2], refs[2:-7]
        act_v, inner_v, branch_v, low_v, got_v, out_v, sem = refs[-7:]
        moving = [start(low, low_v, sem.at[0, 0]), start(branch, branch_v, sem.at[0, 1])]
        loads, stores = {}, []
        for o in order:
            at = pl.ds((half * n + o) * span, span)
            loads[o] = [
                start(inner.at[:, at], inner_v.at[o], sem.at[1, o]),
                start(act.at[:, at], act_v.at[o], sem.at[2, o]),
            ]
            if not half:
                loads[o].append(start(given[1].at[o], got_v.at[o], sem.at[3, o]))
        if half:
            d_out = outs[1]
            d_out[...] = mm(given[0][...], given[1][...], 0, 0)
        else:
            d_out = given[0]
        for copy in moving:
            copy.wait()
        for o in order:
            for copy in loads[o]:
                copy.wait()
            d_in = mm(inner_v[o], low_v[...], 0, 0)
            d_down = mm(act_v[o], branch_v[...], 0, 0)
            first = place[half * n + o]
            second = jnp.minimum(2 * n + first, head_width // 16 - 1)
            for k in range(mp):
                parts = [d_in[k * piece : (k + 1) * piece], d_down[k * piece : (k + 1) * piece]]
                for p in (first, second):
                    at = place[2 * n + k] * head_width + p * 16
                    at = pl.ds(pl.multiple_of(at, 16), 16)
                    parts.append(d_out[at, :])
                row = 0
                for part in parts:
                    at = slice(row, row + part.shape[0])
                    if not half:
                        part = part.astype(BF16).astype(F32) + got_v[o, k, at].astype(F32)
                    out_v[o, k, at] = part.astype(BF16)
                    row += part.shape[0]
            if half:
                stores.append(start(out_v.at[o], outs[0].at[o], sem.at[4, o]))
            else:
                i = 2 * order.index(o)
                stores += [
                    start(out_v.at[o, :, pl.ds(0, cut)], outs[i], sem.at[4, o]),
                    start(out_v.at[o, :, pl.ds(cut, size - cut)], outs[i + 1], sem.at[5, o]),
                ]
        for copy in stores:
            copy.wait()

    last = (ctx.shape[1], width)
    args = [place, act, branch, inner, low]
    if half:
        args += [ctx, att]
        given_specs = [VMEM, VMEM]
        out_specs = [ANY, VMEM]
        out_shape = [
            jax.ShapeDtypeStruct((n, mp, size, width), BF16), jax.ShapeDtypeStruct(last, F32)
        ]
    else:
        args += [d_out, got]
        given_specs = [VMEM, ANY]
        out_specs = [ANY] * (2 * n)
        out_shape = [
            jax.ShapeDtypeStruct((mp, r, width), BF16) for _ in range(n) for r in (cut, size - cut)
        ]
    wide = pltpu.VMEM((n, rows, span), BF16)
    flat = pltpu.VMEM((rows, width), BF16)
    whole = pltpu.VMEM((n, mp, size, width), BF16)
    return pl.pallas_call(
        kernel,
        in_specs=[SMEM] + [ANY] * 4 + given_specs,
        out_specs=out_specs,
        out_shape=out_shape,
        scratch_shapes=[wide, wide, flat, flat, whole, whole, pltpu.SemaphoreType.DMA((6, n))],
        compiler_params=pltpu.CompilerParams(vmem_limit_bytes=VMEM_LIMIT),
        cost_estimate=cost(2 * rows * width * 5 * width, n * mp * width * 500),
        name="weight_grad",
    )(*args)


def joined(body, shapes, *args, name):
    return pl.pallas_call(
        body,
        out_shape=[jax.ShapeDtypeStruct(s, t) for s, t in shapes],
        compiler_params=pltpu.CompilerParams(vmem_limit_bytes=VMEM_LIMIT),
        name=name,
    )(*args)


def hop_sums(a1, a3, b2, b3):
    def hop_sum(a1, a3, b2, b3, a, b):
        a[...] = (a1[...].astype(F32) + a3[...].astype(F32)).astype(BF16)
        b[...] = (b2[...].astype(F32) + b3[...].astype(F32)).astype(BF16)

    shapes = [(a1.shape, BF16), (b2.shape, BF16)]
    return joined(hop_sum, shapes, a1, a3, b2, b3, name="hop_sum")


def plane_sums(here, a0, a1, a2, b0, b1, b2):
    mp, cut, width = a0.shape
    rows = cut + b0.shape[1]

    def plane_sum(here, a0, a1, a2, b0, b1, b2, out):
        for k in range(mp):
            z = here[k]
            for at, parts in ((slice(0, cut), (a0, a1, a2)), (slice(cut, rows), (b0, b1, b2))):
                out[z, at] = sum(p[k].astype(F32) for p in parts).astype(BF16)

    return pl.pallas_call(
        plane_sum,
        in_specs=[SMEM] + [VMEM] * 6,
        out_shape=jax.ShapeDtypeStruct((mp, rows, width), BF16),
        compiler_params=pltpu.CompilerParams(vmem_limit_bytes=VMEM_LIMIT),
        name="plane_sum",
    )(here, a0, a1, a2, b0, b1, b2)


def plane_gather(first, second, dp, between=lambda *arrays: arrays):
    x, y = flip_pairs(dp, 2), flip_pairs(dp, 4)
    a1, b2 = lax.ppermute(first, "dp", x), lax.ppermute(second, "dp", y)
    a2, b1 = lax.ppermute(first, "dp", y), lax.ppermute(second, "dp", x)
    a1, b2 = between(a1, b2)
    a3, b3 = lax.ppermute(a1, "dp", y), lax.ppermute(b2, "dp", x)
    return [first, a1, a2, a3], [second, b1, b2, b3]


def gather_grads(place, units, piece, head_width, firsts, seconds):
    n = len(firsts)
    cut, width = firsts[0].shape
    rows = cut + seconds[0].shape[0]

    def kernel(place, *refs):
        parts, (d_in, d_down, d_out) = refs[: 2 * n], refs[2 * n : 2 * n + 3]
        pad, wide = refs[-2:]
        for i in range(n):
            p = place[i]
            whole = jnp.concatenate([parts[i][...], parts[n + i][...]], 0).astype(F32)
            wide[p] = whole[:piece]
            d_down[p] = whole[piece : 2 * piece]
            pad[p] = whole[2 * piece : 2 * piece + 16]
            pad[n + p] = whole[2 * piece + 16 :]
        d_out[...] = pad[: head_width // 16]
        d_in[...] = wide[...].reshape(n * piece, width).T

    vmem = [VMEM] * (2 * n)
    shapes = [(width, n * piece), (n, piece, width), (head_width // 16, 16, width)]
    return pl.pallas_call(
        kernel,
        in_specs=[SMEM] + vmem,
        out_shape=[jax.ShapeDtypeStruct(s, F32) for s in shapes],
        scratch_shapes=[pltpu.VMEM((2 * n, 16, width), F32), pltpu.VMEM((n, piece, width), F32)],
        compiler_params=pltpu.CompilerParams(vmem_limit_bytes=VMEM_LIMIT),
        name="gather_grads",
    )(place, *firsts, *seconds)


def shift_pairs(mp, k):
    return [(i, (i + k) % mp) for i in range(mp)]


def relay(array, mp):
    below, above = [array], [array]
    for hop in range(1, mp):
        pairs = [(i, i + 1) for i in range(hop - 1, mp - 1)]
        below.append(lax.ppermute(below[-1], "mp", pairs))
        above.append(lax.ppermute(above[-1], "mp", [(mp - 1 - i, mp - 1 - j) for i, j in pairs]))
    return below[1:], above[1:]


def flip_pairs(dp, bit):
    return [(i, i ^ bit) for i in range(dp)]


def tie(value, *others):
    return lax.optimization_barrier((value, others))[0]


def halves_of(array, core):
    half = array.shape[0] // 2
    return (
        lax.dynamic_slice_in_dim(array, core * half, half),
        lax.dynamic_slice_in_dim(array, (1 - core) * half, half),
    )


def reorder(rows, order):
    pick = (order[:, None] == jnp.arange(rows.shape[0])[None, :]).astype(F32)
    return jnp.dot(pick, rows, precision=lax.Precision.HIGHEST)


def on_device(
    tokens,
    prev_logits,
    segment_ids,
    query_weight,
    key_weight,
    value_weight,
    query_bias,
    value_bias,
    output_projection_weight,
    output_bias,
    first_gain,
    first_shift,
    inner_projection_weight,
    inner_bias,
    down_projection_weight,
    down_bias,
    second_gain,
    second_shift,
    output_cot,
    logit_cot,
):
    dp = lax.axis_size("dp")
    mp = lax.axis_size("mp")
    me = lax.axis_index("dp")
    mine = lax.axis_index("mp")
    micro_count, slots, local, width = tokens.shape
    length = prev_logits.shape[3]
    head_width = query_weight.shape[1]
    units = inner_projection_weight.shape[1]
    rows = slots * local
    packed = dp == 8 and mp == 4 and micro_count == 2 and units // dp == 96 and head_width == 192
    chips = dp // 2
    swap = flip_pairs(dp, 1)
    piece = units // dp

    def shifted(array, k):
        return lax.ppermute(array, "mp", shift_pairs(mp, k)) if k else array

    if packed:
        own_in = inner_projection_weight.T.reshape(dp, piece, width)
        own_down = down_projection_weight.reshape(dp, piece, width)
        own_out = output_projection_weight.reshape(-1, 16, width)
        high = inner_bias.astype(BF16)
        middle = (inner_bias - high.astype(F32)).astype(BF16)
        lowest = (inner_bias - high.astype(F32) - middle.astype(F32)).astype(BF16)
        own_bias = jnp.concatenate(
            [jnp.pad(v.reshape(dp, 1, piece), ((0, 0), (0, 15), (0, 128 - piece)))
             for v in (high, middle, lowest)]
            + [jnp.zeros((dp, 16, width - 3 * 128), BF16)], 2
        )
        own_out = jnp.concatenate([own_out, own_out[: 2 * dp - own_out.shape[0]]], 0)
        own_pack = jnp.concatenate([own_in, own_down, own_out[:dp], own_out[dp:], own_bias], 1)
        sent = lax.dynamic_index_in_dim(own_pack, me, 0, False)
        below, above = relay(sent, mp)
        second_hop = (below[1], above[1])
        from_z = jnp.stack(
            [jnp.where(mine >= k, below[k - 1], above[mp - k - 1]) for k in range(1, mp)]
        )
        k_of = jnp.arange(mp)
        cut = piece + piece // 3
        ff_place = me ^ (jnp.arange(dp) // chips + jnp.arange(dp) % chips * 2)
        ff_place = jnp.concatenate([ff_place, k_of]).astype(jnp.int32)
        intake = relative_intake
        block = (units * mp, [(dp, mp, 2 * piece + 48, width), (mp, 2 * dp, 16, width)])
    else:
        in_all = lax.all_gather(inner_projection_weight.T, "mp", axis=0, tiled=True)
        down_all = lax.all_gather(down_projection_weight, "mp", axis=0, tiled=True)
        wo_all = lax.all_gather(output_projection_weight, "mp")
        wo_all = jnp.stack(
            [lax.dynamic_index_in_dim(wo_all, (mine - k) % mp, 0, False) for k in range(mp)]
        )
        weights = [
            in_all.reshape(-1, width, width), down_all.reshape(-1, width, width), wo_all[:, None],
            lax.all_gather(inner_bias, "mp").reshape(1, -1),
        ]
        ff_place = jnp.zeros((dp,), jnp.int32)
        intake = whole_intake
        second_hop = ()
        square = (units * mp // width, width, width)
        block = (units * mp, [square, square, (mp, 1, head_width, width)])

    def gather_tokens(b, *after):
        return lax.all_gather(tie(tokens[b], *after), "mp", axis=1, tiled=True)

    complete = [gather_tokens(0)]
    for b in range(1, micro_count):
        complete.append(gather_tokens(b, *second_hop))
    w_qkv = jnp.concatenate([query_weight, key_weight, value_weight], 1)
    bias_row = jnp.concatenate([query_bias, jnp.zeros_like(query_bias), value_bias])[None]
    vectors = jnp.stack(
        [output_bias, first_gain, first_shift, down_bias, second_gain, second_shift]
        + [jnp.zeros_like(down_bias)] * 2
    )
    own_tokens = tokens.reshape(-1, width)
    own_cot = output_cot.reshape(-1, width)
    place = jnp.stack([(mine + k) % mp for k in range(mp)]).astype(jnp.int32)
    logits = None

    def attend_fully(b, logits):
        logits, probs, qkv, ctx = attend(
            b, complete[b], w_qkv, bias_row, prev_logits, segment_ids, logits
        )
        blocks = []
        for k in range(mp):
            at = ((mine + k) % mp) * local
            part = lax.dynamic_slice(ctx, (0, at, 0), (slots, local, head_width))
            blocks.append(shifted(part, k).reshape(rows, head_width))
        return logits, (probs, qkv, ctx), blocks

    def to_heads(d_ctx):
        return [
            shifted(part, (mp - k) % mp).reshape(micro_count, slots, local, head_width)
            for k, part in enumerate(d_ctx)
        ]

    kept, blocks = [], []
    for b in range(micro_count):
        logits, each, ctx_blocks = attend_fully(b, logits)
        kept.append(each)
        blocks.append(ctx_blocks)
        if packed and b == 0:
            firsts, seconds = plane_gather(
                from_z[:, :cut], from_z[:, cut:], dp, lambda *arrays: tie(arrays, each[2])
            )
            firsts[-1], seconds[-1], blocks[0] = lax.optimization_barrier(
                (firsts[-1], seconds[-1], blocks[0])
            )
            weights = [own_pack]
            for group in (firsts, seconds):
                weights += group + [lax.ppermute(a, "dp", swap) for a in group]
    blocks = lax.optimization_barrier(blocks)
    joint, small, unit_sums, d_ctx = feed_forward(
        blocks, own_tokens, own_cot, vectors, ff_place, weights, intake, block
    )
    d_blocks = to_heads(d_ctx)
    layer, act, branch, inner, low, att, ctx_all, residual = joint

    def back_through(*after):
        d_blocks[0] = tie(d_blocks[0], *after)
        probs, qkv, ctx = zip(*kept)
        return attend_back(place, complete, w_qkv, qkv, ctx, probs, logit_cot, d_blocks)

    unit_total = unit_sums[0]
    if packed:
        z, i = jnp.meshgrid(jnp.arange(mp), jnp.arange(dp), indexing="ij")
        at = me ^ i
        at = ((at % 2 * chips + at // 2) * mp + k_of[(mine - z) % mp]).reshape(-1)
        unit_total = reorder(unit_total.reshape(-1, piece), at).reshape(-1)
    vector = jnp.concatenate([small[:6].reshape(-1), unit_total])
    cols = 3 * head_width
    vector = jnp.pad(vector, (0, -vector.shape[0] % (24 * cols))).reshape(-1, cols)
    at = width + 8
    def scatter_tokens(back):
        return lax.psum_scatter(back, "mp", scatter_dimension=1, tiled=True)

    def joint_grads(*after):
        return tie(jnp.concatenate([acc, bias_acc, vector], 0), *after)

    if packed:
        pairs = [act, branch, inner, low, ctx_all, att]
        other, d_out = weight_grad(1, mp, piece, ff_place, *pairs, None, None)
        got = lax.ppermute(other, "dp", swap)
        sums = weight_grad(0, mp, piece, ff_place, *pairs, d_out, got)
        prev_grad, acc, bias_acc, *backs = back_through(sums)
        cut = 2 * piece + 32 >> 1
        x, y = flip_pairs(dp, 2), flip_pairs(dp, 4)
        a3, b3, a2, b2, a1, b1, a0, b0 = sums
        a3, b3 = lax.ppermute(a3, "dp", y), lax.ppermute(b3, "dp", x)
        a2, b1 = lax.ppermute(a2, "dp", y), lax.ppermute(b1, "dp", x)
        a1, a2, b1, prev_grad = lax.optimization_barrier((a1, a2, b1, prev_grad))
        a1, b2 = hop_sums(a1, a3, b2, b3)
        backs[0] = tie(backs[0], a1)
        a1, b2 = lax.ppermute(a1, "dp", x), lax.ppermute(b2, "dp", y)
        total = plane_sums(((mine - k_of) % mp).astype(jnp.int32), a0, a1, a2, b0, b1, b2)
        backs[0] = scatter_tokens(backs[0])
        backs[0], total = lax.optimization_barrier((backs[0], total))
        scattered = lax.psum_scatter(total, "mp", scatter_dimension=0)
        backs[1:] = [scatter_tokens(tie(back, scattered)) for back in backs[1:]]
        keep, send = halves_of(joint_grads(total), me % 2)
        keep = keep + lax.ppermute(send, "dp", swap)
        quarter = keep.shape[0] // 2
        top, low_part = keep[:quarter], keep[quarter:]
        top, low_part = (
            top + lax.ppermute(top, "dp", x), low_part + lax.ppermute(low_part, "dp", y)
        )
        top, low_part = (
            top + lax.ppermute(top, "dp", y), low_part + lax.ppermute(low_part, "dp", x)
        )
        keep = jnp.concatenate([top, low_part], 0)
        firsts, seconds = plane_gather(scattered[:cut], scattered[cut:], dp)
        firsts += [lax.ppermute(a, "dp", swap) for a in firsts]
        seconds += [lax.ppermute(a, "dp", swap) for a in seconds]
        other = lax.ppermute(keep, "dp", swap)
        summed = jnp.where(
            me % 2 == 0, jnp.concatenate([keep, other], 0), jnp.concatenate([other, keep], 0)
        )
        vector = summed[at:]
        for bit in (1, 2):
            vector += lax.ppermute(vector, "mp", flip_pairs(mp, bit))
        firsts[-1], vector = lax.optimization_barrier((firsts[-1], vector))
        d_in, d_down, d_out = gather_grads(ff_place, units, piece, head_width, firsts, seconds)
        backs[-1] = tie(backs[-1], d_in)
        inner_weight_grad = d_in
        down_weight_grad = d_down.reshape(units, width)
        output_weight_grad = d_out.reshape(head_width, width)
    else:
        g_down = mm(act, branch, 0, 0)
        g_in = mm(inner, low, 0, 0)
        g_out = mm(ctx_all, att, 0, 0)
        vector = lax.psum(vector, "mp")
        prev_grad, acc, bias_acc, *backs = back_through()
        summed = lax.psum(joint_grads(), "dp")
        vector = summed[at:]
        backs = [scatter_tokens(back) for back in backs]
        g_in = lax.psum_scatter(g_in, "mp", scatter_dimension=0, tiled=True)
        inner_weight_grad = lax.psum(g_in, "dp").T
        g_down = lax.psum_scatter(g_down, "mp", scatter_dimension=0, tiled=True)
        down_weight_grad = lax.psum(g_down, "dp")
        g_out = g_out.reshape(mp, head_width, width)
        out_sum = 0.0
        for k in range(mp):
            out_sum += shifted(g_out[k], (mp - k) % mp)
        output_weight_grad = lax.psum(out_sum, "dp")
    token_grads = residual.reshape(tokens.shape) + jnp.stack(backs).astype(F32)
    vector = vector.reshape(-1)
    small = vector[: 6 * width].reshape(6, width)
    unit_total = vector[6 * width : 6 * width + units * mp]
    inner_bias_grad = lax.dynamic_index_in_dim(unit_total.reshape(mp, units), mine, 0, False)
    return (
        layer.reshape(tokens.shape),
        logits,
        token_grads,
        prev_grad,
        summed[:width, :head_width],
        summed[:width, head_width : 2 * head_width],
        summed[:width, 2 * head_width :],
        summed[width, :head_width],
        summed[width, 2 * head_width :],
        output_weight_grad,
        small[0],
        small[1],
        small[2],
        inner_weight_grad,
        inner_bias_grad,
        down_weight_grad,
        small[3],
        small[4],
        small[5],
    )


def solution(mesh):
    rows = P(None, "dp", "mp", None)
    heads = P(None, "dp", "mp", None, None)
    cols, deep, vec, same = P(None, "mp"), P("mp", None), P("mp"), P()
    in_specs = (
        rows, heads, P(None, "dp", None), cols, cols, cols, vec, vec, deep, same, same, same,
        cols, vec, deep, same, same, same, rows, heads,
    )
    out_specs = (
        rows, heads, rows, heads, cols, cols, cols, vec, vec, deep, same, same, same, cols, vec,
        deep, same, same, same,
    )
    return jax.shard_map(
        on_device, mesh=mesh, in_specs=in_specs, out_specs=out_specs, check_vma=False
    )
```

```python
import functools
import math

import jax
import jax.numpy as jnp
from jax import lax
from jax.experimental import pallas as pl
from jax.experimental.pallas import tpu as pltpu
from jax.sharding import PartitionSpec as P

EPSILON = 1e-12
MASKED = -1e30
F32 = jnp.float32
BF16 = jnp.bfloat16
VMEM_LIMIT = 60 * 1024 * 1024
UNROLL = 2
ANY = pl.BlockSpec(memory_space=pl.ANY)
VMEM = pl.BlockSpec(memory_space=pltpu.VMEM)
SMEM = pl.BlockSpec(memory_space=pltpu.SMEM)


def mm(a, b, ca, cb):
    return lax.dot_general(a, b, (((ca,), (cb,)), ((), ())), preferred_element_type=F32)


def cost(flops, moved, exps=0):
    return pl.CostEstimate(flops=int(flops), bytes_accessed=int(moved), transcendentals=int(exps))


def start(src, dst, sem):
    copy = pltpu.make_async_copy(src, dst, sem)
    copy.start()
    return copy

def attend_kernel(b, slots, heads, size, tok, w, bias, prev, seg, *refs):
    logits, probs, qkv, ctx = refs[-17:-13]
    tok_v, prev_v, logits_v, probs_v, qkv_v, ctx_v, w_v, qs, ks, vs = refs[-13:-3]
    sem_in, sem_out, sem_w = refs[-3:]
    length = tok_v.shape[1]
    width = heads * size
    w_in = start(w, w_v, sem_w)
    tok_in, prev_in = [], []
    for s in range(slots):
        tok_in.append(start(tok.at[s], tok_v.at[s], sem_in.at[s, heads]))
        if s == 0:
            prev_in += [start(prev.at[b, s, h], prev_v.at[s, h], sem_in.at[s, h]) for h in range(heads)]
    w_in.wait()
    for s in range(1, slots):
        prev_in += [start(prev.at[b, s, h], prev_v.at[s, h], sem_in.at[s, h]) for h in range(heads)]
    for copy in tok_in:
        copy.wait()

    def project(s, _):
        rows = (mm(tok_v[s], w_v[...], 1, 0) + bias[...]).astype(BF16)
        qkv_v[s] = rows
        start(qkv_v.at[s], qkv.at[s], sem_out.at[s, 2 * heads])
        for h in range(heads):
            at = h * size
            qs[s, h] = rows[:, at : at + size] * (1.0 / math.sqrt(size))
            ks[s, h] = rows[:, width + at : width + at + size]
            vs[s, h] = rows[:, 2 * width + at : 2 * width + at + size]
        return _

    lax.fori_loop(0, slots, project, 0)

    def one_head(i, _):
        s, h = i // heads, lax.rem(i, heads)
        seg_k = seg[b, pl.ds(s, 1), :]
        seg_q = jnp.broadcast_to(seg_k, (8, length)).T[:, :1]
        pltpu.make_async_copy(prev.at[b, s, h], prev_v.at[s, h], sem_in.at[s, h]).wait()
        q, k, v = qs[s, h], ks[s, h], vs[s, h]
        scores = mm(q, k, 1, 1) + prev_v[s, h].astype(F32)
        logits_v[s, h] = scores.astype(BF16)
        start(logits_v.at[s, h], logits.at[b, s, h], sem_out.at[s, h])
        masked = jnp.where(seg_q == seg_k, scores, MASKED)
        exponent = jnp.exp(masked - jnp.max(masked, -1, keepdims=True))
        p = (exponent * (1.0 / jnp.sum(exponent, -1, keepdims=True))).astype(BF16)
        probs_v[s, h] = p
        start(probs_v.at[s, h], probs.at[s, h], sem_out.at[s, heads + h])
        qs[s, h] = mm(p, v, 1, 0).astype(BF16)
        return _

    lax.fori_loop(0, slots * heads, one_head, 0)
    for s in range(slots):
        ctx_v[s] = jnp.concatenate([qs[s, h] for h in range(heads)], -1)
        start(ctx_v.at[s], ctx.at[s], sem_out.at[s, 2 * heads + 1])
    for s in range(slots):
        for h in range(heads):
            pltpu.make_async_copy(logits_v.at[s, h], logits.at[b, s, h], sem_out.at[s, h]).wait()
            pltpu.make_async_copy(probs_v.at[s, h], probs.at[s, h], sem_out.at[s, heads + h]).wait()
        pltpu.make_async_copy(qkv_v.at[s], qkv.at[s], sem_out.at[s, 2 * heads]).wait()
        pltpu.make_async_copy(ctx_v.at[s], ctx.at[s], sem_out.at[s, 2 * heads + 1]).wait()


def attend(b, complete, w_qkv, bias, prev_logits, seg, logits_in):
    slots, length, width = complete.shape
    heads = prev_logits.shape[2]
    cols = w_qkv.shape[1]
    size = cols // 3 // heads
    args = [complete, w_qkv, bias, prev_logits, seg]
    in_specs = [ANY, ANY, VMEM, ANY, VMEM]
    alias = {}
    if logits_in is not None:
        alias = {len(args): 0}
        args.append(logits_in)
        in_specs.append(ANY)
    n = slots * heads * length * length
    square = pltpu.VMEM((slots, heads, length, length), BF16)
    return pl.pallas_call(
        functools.partial(attend_kernel, b, slots, heads, size),
        in_specs=in_specs,
        out_specs=[ANY] * 4,
        out_shape=[
            jax.ShapeDtypeStruct(prev_logits.shape, BF16),
            jax.ShapeDtypeStruct((slots, heads, length, length), BF16),
            jax.ShapeDtypeStruct((slots, length, cols), BF16),
            jax.ShapeDtypeStruct((slots, length, cols // 3), BF16),
        ],
        scratch_shapes=[
            pltpu.VMEM((slots, length, width), BF16), square, square, square,
            pltpu.VMEM((slots, length, cols), BF16), pltpu.VMEM((slots, length, cols // 3), BF16),
            pltpu.VMEM((width, cols), BF16),
            *[pltpu.VMEM((slots, heads, length, size), BF16)] * 3,
            pltpu.SemaphoreType.DMA((slots, heads + 1)),
            pltpu.SemaphoreType.DMA((slots, 2 * heads + 2)), pltpu.SemaphoreType.DMA,
        ],
        input_output_aliases=alias,
        compiler_params=pltpu.CompilerParams(vmem_limit_bytes=VMEM_LIMIT),
        cost_estimate=cost(n * 1024 + 2 * slots * length * width * cols, n * 6, n),
        name="attend",
    )(*args)


def attend_back_kernel(micro, slots, heads, size, n_blocks, place, *refs):
    tok, qkv, ctx, probs = (refs[i * micro : (i + 1) * micro] for i in range(4))
    w, cot, *blocks = refs[4 * micro : 4 * micro + 2 + n_blocks]
    prev_grad, acc, bias_acc, *backs = refs[-16 - micro : -13]
    tok_v, qkv_v, ctx_v, dctx_v, probs_v, cot_v, grad_v, back_v, w_v, parts, deltas = refs[-13:-2]
    sem_in, sem_out = refs[-2:]
    length = tok_v.shape[1]
    width = heads * size
    local = blocks[0].shape[2]
    total = micro * slots
    first, later = [], []
    for s in range(total):
        b, t = divmod(s, slots)
        first += [
            start(qkv[b].at[t], qkv_v.at[s], sem_in.at[s, 0]),
            start(ctx[b].at[t], ctx_v.at[s], sem_in.at[s, 1]),
        ]
        for j in range(n_blocks):
            at = pl.ds(pl.multiple_of(place[j] * local, local), local)
            first.append(start(blocks[j].at[b, t], dctx_v.at[s, at], sem_in.at[s, 3 + j]))
    for s in range(total):
        b, t = divmod(s, slots)
        for h in range(heads):
            start(probs[b].at[t, h], probs_v.at[s, h], sem_in.at[s, 3 + n_blocks + h])
            start(cot.at[b, t, h], cot_v.at[s, h], sem_in.at[s, 3 + n_blocks + heads + h])
    later.append(start(w, w_v, sem_out.at[0, heads]))
    for s in range(total):
        b, t = divmod(s, slots)
        later.append(start(tok[b].at[t], tok_v.at[s], sem_in.at[s, 2]))
    for copy in first:
        copy.wait()

    def split(s, _):
        rows, d_all = qkv_v[s], dctx_v[s]
        product = d_all.astype(F32) * ctx_v[s].astype(F32)
        for h in range(heads):
            at = h * size
            parts[0, s, h] = rows[:, at : at + size]
            parts[1, s, h] = rows[:, width + at : width + at + size]
            parts[2, s, h] = rows[:, 2 * width + at : 2 * width + at + size]
            parts[3, s, h] = d_all[:, at : at + size]
            deltas[s, h] = jnp.sum(product[:, at : at + size], -1, keepdims=True)
        return _

    lax.fori_loop(0, total, split, 0)

    def leave(s, h):
        return pltpu.make_async_copy(
            grad_v.at[s, h], prev_grad.at[s // slots, lax.rem(s, slots), h], sem_out.at[s, h])

    def leave_back(s, b):
        return pltpu.make_async_copy(
            back_v.at[s], backs[b].at[lax.rem(s, slots)], sem_out.at[s, heads + 1])

    def one_head(i, _):
        s, h = i // heads, lax.rem(i, heads)
        pltpu.make_async_copy(
            probs[0].at[0, h], probs_v.at[s, h], sem_in.at[s, 3 + n_blocks + h]).wait()
        pltpu.make_async_copy(
            cot.at[0, 0, h], cot_v.at[s, h], sem_in.at[s, 3 + n_blocks + heads + h]).wait()
        q, k, v, d_context = (parts[j, s, h] for j in range(4))
        p = probs_v[s, h]
        d_scores = p.astype(F32) * (mm(d_context, v, 1, 1) - deltas[s, h]) + cot_v[s, h].astype(F32)
        grad_v[s, h] = d_scores
        leave(s, h).start()
        d_dots = (d_scores * (1.0 / math.sqrt(size))).astype(BF16)
        parts[0, s, h] = mm(d_dots, k, 1, 0).astype(BF16)
        parts[1, s, h] = mm(q, d_dots, 0, 0).T.astype(BF16)
        parts[2, s, h] = mm(d_context, p, 0, 0).T.astype(BF16)
        return _

    lax.fori_loop(0, total * heads, one_head, 0)
    for copy in later:
        copy.wait()
    acc[...] = jnp.zeros_like(acc)
    bias_acc[...] = jnp.zeros_like(bias_acc)

    def finish(s, _):
        d_qkv = jnp.concatenate([parts[j, s, h] for j in range(3) for h in range(heads)], -1)
        back_v[s] = mm(d_qkv, w_v[...], 1, 1).astype(BF16)
        for b in range(micro):
            pl.when(s // slots == b)(leave_back(s, b).start)
        acc[...] += mm(tok_v[s], d_qkv, 0, 0)
        bias_acc[...] += jnp.sum(d_qkv.astype(F32), 0, keepdims=True)
        return _

    lax.fori_loop(0, total, finish, 0)
    for s in range(total):
        for h in range(heads):
            leave(s, h).wait()
        leave_back(s, 0).wait()


def attend_back(place, complete, w_qkv, qkv, ctx, probs, logit_cot, blocks):
    micro, slots, heads, length, _ = logit_cot.shape
    width, cols = w_qkv.shape
    size = cols // 3 // heads
    args = [place, *complete, *qkv, *ctx, *probs, w_qkv, logit_cot, *blocks]
    n = micro * slots * heads * length * length
    total = micro * slots
    square = (total, heads, length, length)
    return pl.pallas_call(
        functools.partial(attend_back_kernel, micro, slots, heads, size, len(blocks)),
        in_specs=[SMEM] + [ANY] * (len(args) - 1),
        out_specs=[ANY, VMEM, VMEM] + [ANY] * micro,
        out_shape=[
            jax.ShapeDtypeStruct(logit_cot.shape, F32),
            jax.ShapeDtypeStruct((width, cols), F32),
            jax.ShapeDtypeStruct((8, cols), F32),
        ]
        + [jax.ShapeDtypeStruct((slots, length, width), BF16)] * micro,
        scratch_shapes=[
            pltpu.VMEM((total, length, width), BF16), pltpu.VMEM((total, length, cols), BF16),
            pltpu.VMEM((total, length, cols // 3), BF16),
            pltpu.VMEM((total, length, cols // 3), BF16),
            pltpu.VMEM(square, BF16), pltpu.VMEM(square, BF16), pltpu.VMEM(square, F32),
            pltpu.VMEM((total, length, width), BF16), pltpu.VMEM((width, cols), BF16),
            pltpu.VMEM((4, total, heads, length, size), BF16),
            pltpu.VMEM((total, heads, length, 1), F32),
            pltpu.SemaphoreType.DMA((total, 3 + len(blocks) + 2 * heads)),
            pltpu.SemaphoreType.DMA((total, heads + 2)),
        ],
        compiler_params=pltpu.CompilerParams(vmem_limit_bytes=VMEM_LIMIT),
        cost_estimate=cost(n * 2048 + 4 * total * length * width * cols, n * 8),
        name="attend_back",
    )(*args)


def gelu_and_slope(x):
    bell = jnp.exp(-0.5 * x * x)
    t = 1.0 / (1.0 + (0.3275911 * math.sqrt(0.5)) * jnp.abs(x))
    tail = t * (
        0.5 * 0.254829592
        + t * (
            0.5 * -0.284496736
            + t * (0.5 * 1.421413741 + t * (0.5 * -1.453152027 + t * (0.5 * 1.061405429)))
        )
    ) * bell
    phi = jnp.where(x >= 0, 1.0 - tail, tail)
    return x * phi, phi + x * (bell * (1.0 / math.sqrt(2.0 * math.pi)))


def norm_parts(u):
    centered = u - jnp.mean(u, -1, keepdims=True)
    r = lax.rsqrt(jnp.mean(centered * centered, -1, keepdims=True) + EPSILON)
    return centered * r, r


def norm_back(grad, gain, n, r):
    e = grad * gain
    return r * (e - jnp.mean(e, -1, keepdims=True) - n * jnp.mean(e * n, -1, keepdims=True))


def column_sum(u):
    return jnp.sum(u, 0, keepdims=True)


def feed_forward_kernel(micro, n_ctx, intake, place, refs_in, refs_out, scratch):
    ctx, (tok, cot, vectors, *weights) = refs_in[: micro * n_ctx], refs_in[micro * n_ctx :]
    b_out, g1, s1, b_down, g2, s2 = [vectors[i : i + 1, :] for i in range(6)]
    joint, (smalls, unit_sums) = refs_out[:8], refs_out[8:10]
    d_ctx, other = refs_out[10 : 10 + n_ctx], refs_out[10 + n_ctx :] or None
    if other:
        scratch, other_scratch = scratch[:-2], scratch[-2:]
    slope, total, *held = scratch
    weights_v, held = held[: -14], held[-14:]
    w_out, b_in = weights_v[-2:]
    ctx_v, tok_v, cot_v, d_ctx_v, *joint_v, sem, io_sem = held
    out_v, act_v, branch_v, inner_v, low_v, att_v, all_v, res_v = joint_v
    units, width = slope.shape[1], total.shape[1]
    chunk = width
    head_width = ctx[0].shape[1]

    def leave(i):
        return pltpu.make_async_copy(joint_v[i], joint[i], io_sem.at[1, i])

    first = [start(tok, tok_v, io_sem.at[0, 0])]
    for i, c in enumerate(ctx):
        b, k = divmod(i, n_ctx)
        rows = pl.ds(b * c.shape[0], c.shape[0])
        first.append(start(c, ctx_v.at[k, rows], io_sem.at[3 + b, k]))
    wait_first, wait_units, weights_of = intake(place, weights, weights_v, sem)
    cot_in = start(cot, cot_v, io_sem.at[0, 1])
    for copy in first:
        copy.wait()
    wait_first()
    attended = b_out
    for k in range(n_ctx):
        attended = attended + mm(ctx_v[k], w_out[k].reshape(-1, width)[:head_width], 1, 0)
    all_v[...] = jnp.concatenate([ctx_v[k] for k in range(n_ctx)], -1)
    n1, r1 = norm_parts(tok_v[...].astype(F32) + attended)
    hidden = n1 * g1 + s1
    low_v[...] = hidden.astype(BF16)
    total[...] = hidden + b_down
    leave(4).start()
    leave(6).start()

    def forward(j, _):
        wait_units(j)
        at = pl.ds(pl.multiple_of(j * chunk, chunk), chunk)
        w_in, w_down = weights_of(j)
        pre = mm(low_v[...], w_in, 1, 1) + b_in[:, at]
        activated, grad = gelu_and_slope(pre)
        activated = activated.astype(BF16)
        act_v[:, at] = activated
        slope[:, at] = grad.astype(BF16)
        total[...] += mm(activated, w_down, 1, 0)
        return _

    lax.fori_loop(0, units // chunk, forward, 0, unroll=UNROLL)
    leave(1).start()
    n2, r2 = norm_parts(total[...])
    out_v[...] = (n2 * g2 + s2).astype(BF16)
    leave(0).start()
    cot_in.wait()
    g = cot_v[...].astype(F32)
    d_second = norm_back(g, g2, n2, r2)
    smalls[3:4, :] = column_sum(d_second)
    smalls[4:5, :] = column_sum(g * n2)
    smalls[5:6, :] = column_sum(g)
    branch_v[...] = d_second.astype(BF16)
    leave(2).start()
    total[...] = d_second

    def backward(j, _):
        at = pl.ds(pl.multiple_of(j * chunk, chunk), chunk)
        w_in, w_down = weights_of(j)
        d_act = mm(branch_v[...], w_down, 1, 1)
        d_inner = d_act * slope[:, at].astype(F32)
        unit_sums[:, at] = jnp.broadcast_to(column_sum(d_inner), (8, chunk))
        d_inner = d_inner.astype(BF16)
        inner_v[:, at] = d_inner
        total[...] += mm(d_inner, w_in, 1, 0)
        return _

    lax.fori_loop(0, units // chunk, backward, 0, unroll=UNROLL)
    leave(3).start()
    d_hidden = total[...]
    d_residual = norm_back(d_hidden, g1, n1, r1)
    d_att = d_residual.astype(BF16)
    for k in range(n_ctx):
        d_ctx_v[k] = mm(d_att, w_out[k].reshape(-1, width)[:head_width], 1, 1).astype(BF16)
        start(d_ctx_v.at[k], d_ctx[k], io_sem.at[2, k])
    att_v[...] = d_att
    res_v[...] = d_residual
    leave(5).start()
    leave(7).start()
    smalls[0:1, :] = column_sum(d_residual)
    smalls[1:2, :] = column_sum(d_hidden * n1)
    smalls[2:3, :] = column_sum(d_hidden)
    smalls[6:8, :] = jnp.zeros((2, width), F32)
    if other is not None:
        grads, d_out = other
        other_v, other_sem = other_scratch
        n, mp, size, _ = other_v.shape
        piece = (size - 32) // 2
        span = mp * piece
        d_out[...] = mm(all_v[...], att_v[...], 0, 0)
        for o in reversed(range(n)):
            at = slice((n + o) * span, (n + o + 1) * span)
            fill_block(
                other_v, o, mm(inner_v[:, at], low_v[...], 0, 0),
                mm(act_v[:, at], branch_v[...], 0, 0), d_out, piece, place[n + o],
                2 * n + place[n + o], lambda k: place[2 * n + k],
            )
            start(other_v.at[o], grads.at[o], other_sem.at[o])
        for o in range(n):
            pltpu.make_async_copy(other_v.at[o], grads.at[o], other_sem.at[o]).wait()
    for k in range(n_ctx):
        pltpu.make_async_copy(d_ctx_v.at[k], d_ctx[k], io_sem.at[2, k]).wait()
    for i in range(8):
        leave(i).wait()


def relative_intake(place, weights, held, sem):
    own, *parts = weights
    packed, w_out, b_in = held
    n, mp, rows, width = packed.shape
    stages = [parts[j * n : (j + 1) * n] for j in range(len(parts) // n)]
    piece = b_in.shape[1] // (n * mp)
    pieces = 2 * piece

    def copies(i, at, sources):
        last = [pltpu.make_async_copy(
            own.at[at, pl.ds(pieces, rows - pieces)], packed.at[i, 0, pl.ds(pieces, rows - pieces)],
            sem.at[0, i])]
        main = [pltpu.make_async_copy(
            own.at[at, pl.ds(0, pieces)], packed.at[i, 0, pl.ds(0, pieces)], sem.at[1, i])]
        slot = 1
        for j in range(0, len(sources), 2):
            low, high = sources[j], sources[j + 1]
            slots, cut = pl.ds(slot, low.shape[0]), low.shape[1]
            slot += low.shape[0]
            last.append(pltpu.make_async_copy(
                high.at[:, pl.ds(pieces - cut, rows - pieces)],
                packed.at[i, slots, pl.ds(pieces, rows - pieces)], sem.at[2 + j, i]))
            main += [
                pltpu.make_async_copy(low, packed.at[i, slots, pl.ds(0, cut)], sem.at[3 + j, i]),
                pltpu.make_async_copy(
                    high.at[:, pl.ds(0, pieces - cut)],
                    packed.at[i, slots, pl.ds(cut, pieces - cut)], sem.at[6 + j, i]),
            ]
        return last, main

    for which in range(2):
        for i in range(n):
            for copy in copies(i, place[i], [stage[i] for stage in stages])[which]:
                copy.start()
    some = [stage[0] for stage in stages]

    def wait_first():
        for i in range(n):
            for copy in copies(i, 0, some)[0]:
                copy.wait()
            for s in range(mp):
                for j in range(2):
                    w_out[place[n + s], place[i] + n * j] = (
                        packed[i, s, pieces + 16 * j : pieces + 16 * j + 16]
                    )
                row = packed[i, s, pieces + 32 : pieces + 33, :].astype(F32)
                at = (i * mp + s) * piece
                b_in[:, at : at + piece] = (
                    row[:, :piece] + row[:, 128 : 128 + piece] + row[:, 256 : 256 + piece]
                )

    def wait_units(j):
        for half in range(2):
            for copy in copies(2 * j + half, 0, some)[1]:
                copy.wait()

    def units(j):
        at = pl.ds(2 * j, 2)
        return [packed[at, :, lo : lo + piece].reshape(-1, width) for lo in (0, piece)]

    return wait_first, wait_units, units


def whole_intake(place, weights, held, sem):
    w_in, w_down, w_out, b_in = held
    copies = [start(src, dst, sem.at[0, i]) for i, (src, dst) in enumerate(zip(weights, held))]

    def wait_first():
        for copy in copies:
            copy.wait()

    def units(j):
        return w_in[j], w_down[j]

    return wait_first, lambda j: None, units


def feed_forward(ctx, tokens, cot, vectors, place, weights, intake, block, grads):
    rows, width = tokens.shape
    micro, n_ctx = len(ctx), len(ctx[0])
    head_width = ctx[0][0].shape[1]
    units, held_shapes = block
    args = [place, *[c for blocks in ctx for c in blocks], tokens, cot, vectors, *weights]
    in_specs = [SMEM] + [ANY] * (micro * n_ctx + 2) + [VMEM] + [ANY] * len(weights)
    joint_cols = [(width, BF16), (units, BF16), (width, BF16), (units, BF16), (width, BF16),
                  (width, BF16), (n_ctx * head_width, BF16), (width, F32)]
    n_args = len(args)
    n_out = len(joint_cols) + 2 + n_ctx + 2 * len(grads)
    context = n_ctx * head_width

    def kernel(place, *refs):
        feed_forward_kernel(
            micro, n_ctx, intake, place, refs[: n_args - 1], refs[n_args - 1 : n_args - 1 + n_out],
            refs[n_args - 1 + n_out :],
        )

    heads_block = pltpu.VMEM((n_ctx, rows, head_width), BF16)
    outs = pl.pallas_call(
        kernel,
        in_specs=in_specs,
        out_specs=[ANY] * len(joint_cols) + [VMEM] * 2 + [ANY] * n_ctx + [ANY, VMEM] * len(grads),
        out_shape=[jax.ShapeDtypeStruct((rows, c), t) for c, t in joint_cols]
        + [jax.ShapeDtypeStruct((8, width), F32), jax.ShapeDtypeStruct((8, units), F32)]
        + [jax.ShapeDtypeStruct((rows, head_width), BF16)] * n_ctx
        + [jax.ShapeDtypeStruct(s, t) for g in grads for s, t in ((g, BF16), ((context, width), F32))],
        scratch_shapes=[
            pltpu.VMEM((rows, units), BF16), pltpu.VMEM((rows, width), F32),
            *[pltpu.VMEM(s, BF16) for s in held_shapes], pltpu.VMEM((1, units), F32),
            heads_block, pltpu.VMEM((rows, width), BF16), pltpu.VMEM((rows, width), BF16),
            heads_block, *[pltpu.VMEM((rows, c), t) for c, t in joint_cols],
            pltpu.SemaphoreType.DMA((9, 8)), pltpu.SemaphoreType.DMA((3 + micro, 8)),
        ]
        + [s for g in grads for s in (pltpu.VMEM(g, BF16), pltpu.SemaphoreType.DMA((g[0],)))],
        compiler_params=pltpu.CompilerParams(vmem_limit_bytes=VMEM_LIMIT),
        cost_estimate=cost(
            2 * rows * width * (4 * units + 2 * width), 4 * units * width + 20 * rows * width,
            rows * units,
        ),
        name="feed_forward",
    )(*args)
    n = len(joint_cols)
    return outs[:n], outs[n], outs[n + 1], outs[n + 2 : n + 2 + n_ctx], outs[n + 2 + n_ctx :]


def fill_block(out, o, d_in, d_down, d_out, piece, first, spare, place_of, got=None):
    mp = out.shape[1]
    head_width = d_out.shape[0] // mp
    for k in range(mp):
        parts = [d_in[k * piece : (k + 1) * piece], d_down[k * piece : (k + 1) * piece]]
        for p in (first, jnp.minimum(spare, head_width // 16 - 1)):
            at = pl.ds(pl.multiple_of(place_of(k) * head_width + p * 16, 16), 16)
            parts.append(d_out[at, :])
        row = 0
        for part in parts:
            at = slice(row, row + part.shape[0])
            if got is not None:
                part = part.astype(BF16).astype(F32) + got[o, k, at].astype(F32)
            out[o, k, at] = part.astype(BF16)
            row += part.shape[0]


def weight_grad(mp, piece, place, act, branch, inner, low, d_out, got):
    rows, width = branch.shape
    span = mp * piece
    n = act.shape[1] // span // 2
    size = 2 * piece + 32
    cut = size // 2
    order = tuple(reversed(range(n)))

    def kernel(place, act, branch, inner, low, d_out, got, *refs):
        outs, (act_v, inner_v, branch_v, low_v, got_v, out_v, sem) = refs[:-7], refs[-7:]
        moving = [start(low, low_v, sem.at[0, 0]), start(branch, branch_v, sem.at[0, 1])]
        loads, stores = {}, []
        for o in order:
            at = pl.ds(o * span, span)
            loads[o] = [
                start(inner.at[:, at], inner_v.at[o], sem.at[1, o]),
                start(act.at[:, at], act_v.at[o], sem.at[2, o]),
                start(got.at[o], got_v.at[o], sem.at[3, o]),
            ]
        for copy in moving:
            copy.wait()
        for i, o in enumerate(order):
            for copy in loads[o]:
                copy.wait()
            fill_block(
                out_v, o, mm(inner_v[o], low_v[...], 0, 0), mm(act_v[o], branch_v[...], 0, 0),
                d_out, piece, place[o], 2 * n + place[o], lambda k: place[2 * n + k], got_v,
            )
            stores += [
                start(out_v.at[o, :, pl.ds(0, cut)], outs[2 * i], sem.at[4, o]),
                start(out_v.at[o, :, pl.ds(cut, size - cut)], outs[2 * i + 1], sem.at[5, o]),
            ]
        for copy in stores:
            copy.wait()

    wide = pltpu.VMEM((n, rows, span), BF16)
    flat = pltpu.VMEM((rows, width), BF16)
    whole = pltpu.VMEM((n, mp, size, width), BF16)
    return pl.pallas_call(
        kernel,
        in_specs=[SMEM] + [ANY] * 4 + [VMEM, ANY],
        out_specs=[ANY] * (2 * n),
        out_shape=[
            jax.ShapeDtypeStruct((mp, r, width), BF16) for _ in range(n) for r in (cut, size - cut)
        ],
        scratch_shapes=[wide, wide, flat, flat, whole, whole, pltpu.SemaphoreType.DMA((6, n))],
        compiler_params=pltpu.CompilerParams(vmem_limit_bytes=VMEM_LIMIT),
        cost_estimate=cost(2 * rows * width * 5 * width, n * mp * width * 500),
        name="weight_grad",
    )(place, act, branch, inner, low, d_out, got)


def joined(body, shapes, *args, name):
    return pl.pallas_call(
        body,
        out_shape=[jax.ShapeDtypeStruct(s, t) for s, t in shapes],
        compiler_params=pltpu.CompilerParams(vmem_limit_bytes=VMEM_LIMIT),
        name=name,
    )(*args)


def hop_sums(a1, a3, b2, b3):
    def hop_sum(a1, a3, b2, b3, a, b):
        a[...] = (a1[...].astype(F32) + a3[...].astype(F32)).astype(BF16)
        b[...] = (b2[...].astype(F32) + b3[...].astype(F32)).astype(BF16)

    shapes = [(a1.shape, BF16), (b2.shape, BF16)]
    return joined(hop_sum, shapes, a1, a3, b2, b3, name="hop_sum")


def plane_sums(here, a0, a1, a2, b0, b1, b2):
    mp, cut, width = a0.shape
    rows = cut + b0.shape[1]

    def plane_sum(here, a0, a1, a2, b0, b1, b2, out):
        for k in range(mp):
            z = here[k]
            for at, parts in ((slice(0, cut), (a0, a1, a2)), (slice(cut, rows), (b0, b1, b2))):
                out[z, at] = sum(p[k].astype(F32) for p in parts).astype(BF16)

    return pl.pallas_call(
        plane_sum,
        in_specs=[SMEM] + [VMEM] * 6,
        out_shape=jax.ShapeDtypeStruct((mp, rows, width), BF16),
        compiler_params=pltpu.CompilerParams(vmem_limit_bytes=VMEM_LIMIT),
        name="plane_sum",
    )(here, a0, a1, a2, b0, b1, b2)


def plane_gather(first, second, dp, between=lambda *arrays: arrays):
    x, y = flip_pairs(dp, 2), flip_pairs(dp, 4)
    a1, b2 = lax.ppermute(first, "dp", x), lax.ppermute(second, "dp", y)
    a2, b1 = lax.ppermute(first, "dp", y), lax.ppermute(second, "dp", x)
    a1, b2 = between(a1, b2)
    a3, b3 = lax.ppermute(a1, "dp", y), lax.ppermute(b2, "dp", x)
    return [first, a1, a2, a3], [second, b1, b2, b3]


def gather_grads(place, units, piece, head_width, firsts, seconds):
    n = len(firsts)
    cut, width = firsts[0].shape
    rows = cut + seconds[0].shape[0]

    def kernel(place, *refs):
        parts, (d_in, d_down, d_out) = refs[: 2 * n], refs[2 * n : 2 * n + 3]
        pad, wide = refs[-2:]
        for i in range(n):
            p = place[i]
            whole = jnp.concatenate([parts[i][...], parts[n + i][...]], 0).astype(F32)
            wide[p] = whole[:piece]
            d_down[p] = whole[piece : 2 * piece]
            pad[p] = whole[2 * piece : 2 * piece + 16]
            pad[n + p] = whole[2 * piece + 16 :]
        d_out[...] = pad[: head_width // 16]
        d_in[...] = wide[...].reshape(n * piece, width).T

    vmem = [VMEM] * (2 * n)
    shapes = [(width, n * piece), (n, piece, width), (head_width // 16, 16, width)]
    return pl.pallas_call(
        kernel,
        in_specs=[SMEM] + vmem,
        out_shape=[jax.ShapeDtypeStruct(s, F32) for s in shapes],
        scratch_shapes=[pltpu.VMEM((2 * n, 16, width), F32), pltpu.VMEM((n, piece, width), F32)],
        compiler_params=pltpu.CompilerParams(vmem_limit_bytes=VMEM_LIMIT),
        name="gather_grads",
    )(place, *firsts, *seconds)


def shift_pairs(mp, k):
    return [(i, (i + k) % mp) for i in range(mp)]


def relay(array, mp):
    below, above = [array], [array]
    for hop in range(1, mp):
        pairs = [(i, i + 1) for i in range(hop - 1, mp - 1)]
        below.append(lax.ppermute(below[-1], "mp", pairs))
        above.append(lax.ppermute(above[-1], "mp", [(mp - 1 - i, mp - 1 - j) for i, j in pairs]))
    return below[1:], above[1:]


def flip_pairs(dp, bit):
    return [(i, i ^ bit) for i in range(dp)]


def tie(value, *others):
    return lax.optimization_barrier((value, others))[0]


def halves_of(array, core):
    half = array.shape[0] // 2
    return (
        lax.dynamic_slice_in_dim(array, core * half, half),
        lax.dynamic_slice_in_dim(array, (1 - core) * half, half),
    )


def reorder(rows, order):
    pick = (order[:, None] == jnp.arange(rows.shape[0])[None, :]).astype(F32)
    return jnp.dot(pick, rows, precision=lax.Precision.HIGHEST)


def on_device(
    tokens,
    prev_logits,
    segment_ids,
    query_weight,
    key_weight,
    value_weight,
    query_bias,
    value_bias,
    output_projection_weight,
    output_bias,
    first_gain,
    first_shift,
    inner_projection_weight,
    inner_bias,
    down_projection_weight,
    down_bias,
    second_gain,
    second_shift,
    output_cot,
    logit_cot,
):
    dp = lax.axis_size("dp")
    mp = lax.axis_size("mp")
    me = lax.axis_index("dp")
    mine = lax.axis_index("mp")
    micro_count, slots, local, width = tokens.shape
    length = prev_logits.shape[3]
    head_width = query_weight.shape[1]
    units = inner_projection_weight.shape[1]
    rows = slots * local
    packed = dp == 8 and mp == 4 and micro_count == 2 and units // dp == 96 and head_width == 192
    chips = dp // 2
    swap = flip_pairs(dp, 1)
    piece = units // dp

    def shifted(array, k):
        return lax.ppermute(array, "mp", shift_pairs(mp, k)) if k else array

    if packed:
        own_in = inner_projection_weight.T.reshape(dp, piece, width)
        own_down = down_projection_weight.reshape(dp, piece, width)
        own_out = output_projection_weight.reshape(-1, 16, width)
        high = inner_bias.astype(BF16)
        middle = (inner_bias - high.astype(F32)).astype(BF16)
        lowest = (inner_bias - high.astype(F32) - middle.astype(F32)).astype(BF16)
        own_bias = jnp.concatenate(
            [jnp.pad(v.reshape(dp, 1, piece), ((0, 0), (0, 15), (0, 128 - piece)))
             for v in (high, middle, lowest)]
            + [jnp.zeros((dp, 16, width - 3 * 128), BF16)], 2
        )
        own_out = jnp.concatenate([own_out, own_out[: 2 * dp - own_out.shape[0]]], 0)
        own_pack = jnp.concatenate([own_in, own_down, own_out[:dp], own_out[dp:], own_bias], 1)
        sent = lax.dynamic_index_in_dim(own_pack, me, 0, False)
        below, above = relay(sent, mp)
        second_hop = (below[1], above[1])
        from_z = jnp.stack(
            [jnp.where(mine >= k, below[k - 1], above[mp - k - 1]) for k in range(1, mp)]
        )
        k_of = jnp.arange(mp)
        cut = piece + piece // 3
        ff_place = me ^ (jnp.arange(dp) // chips + jnp.arange(dp) % chips * 2)
        ff_place = jnp.concatenate([ff_place, k_of]).astype(jnp.int32)
        intake = relative_intake
        block = (units * mp, [(dp, mp, 2 * piece + 48, width), (mp, 2 * dp, 16, width)])
    else:
        in_all = lax.all_gather(inner_projection_weight.T, "mp", axis=0, tiled=True)
        down_all = lax.all_gather(down_projection_weight, "mp", axis=0, tiled=True)
        wo_all = lax.all_gather(output_projection_weight, "mp")
        wo_all = jnp.stack(
            [lax.dynamic_index_in_dim(wo_all, (mine - k) % mp, 0, False) for k in range(mp)]
        )
        weights = [
            in_all.reshape(-1, width, width), down_all.reshape(-1, width, width), wo_all[:, None],
            lax.all_gather(inner_bias, "mp").reshape(1, -1),
        ]
        ff_place = jnp.zeros((dp,), jnp.int32)
        intake = whole_intake
        second_hop = ()
        square = (units * mp // width, width, width)
        block = (units * mp, [square, square, (mp, 1, head_width, width)])

    def gather_tokens(b, *after):
        return lax.all_gather(tie(tokens[b], *after), "mp", axis=1, tiled=True)

    complete = [gather_tokens(0)]
    for b in range(1, micro_count):
        complete.append(gather_tokens(b, *second_hop))
    w_qkv = jnp.concatenate([query_weight, key_weight, value_weight], 1)
    bias_row = jnp.concatenate([query_bias, jnp.zeros_like(query_bias), value_bias])[None]
    vectors = jnp.stack(
        [output_bias, first_gain, first_shift, down_bias, second_gain, second_shift]
        + [jnp.zeros_like(down_bias)] * 2
    )
    own_tokens = tokens.reshape(-1, width)
    own_cot = output_cot.reshape(-1, width)
    place = jnp.stack([(mine + k) % mp for k in range(mp)]).astype(jnp.int32)
    logits = None

    def attend_fully(b, logits):
        logits, probs, qkv, ctx = attend(
            b, complete[b], w_qkv, bias_row, prev_logits, segment_ids, logits
        )
        blocks = []
        for k in range(mp):
            at = ((mine + k) % mp) * local
            part = lax.dynamic_slice(ctx, (0, at, 0), (slots, local, head_width))
            blocks.append(shifted(part, k).reshape(rows, head_width))
        return logits, (probs, qkv, ctx), blocks

    def to_heads(d_ctx):
        return [
            shifted(part, (mp - k) % mp).reshape(micro_count, slots, local, head_width)
            for k, part in enumerate(d_ctx)
        ]

    kept, blocks = [], []
    for b in range(micro_count):
        logits, each, ctx_blocks = attend_fully(b, logits)
        kept.append(each)
        blocks.append(ctx_blocks)
        if packed and b == 0:
            firsts, seconds = plane_gather(
                from_z[:, :cut], from_z[:, cut:], dp, lambda *arrays: tie(arrays, each[2])
            )
            firsts[-1], seconds[-1], blocks[0] = lax.optimization_barrier(
                (firsts[-1], seconds[-1], blocks[0])
            )
            weights = [own_pack]
            for group in (firsts, seconds):
                weights += group + [lax.ppermute(a, "dp", swap) for a in group]
    blocks = lax.optimization_barrier(blocks)
    grads = [(chips, mp, 2 * piece + 32, width)] if packed else []
    joint, small, unit_sums, d_ctx, other_grads = feed_forward(
        blocks, own_tokens, own_cot, vectors, ff_place, weights, intake, block, grads
    )
    d_blocks = to_heads(d_ctx)
    layer, act, branch, inner, low, att, ctx_all, residual = joint

    def back_through(*after):
        d_blocks[0] = tie(d_blocks[0], *after)
        probs, qkv, ctx = zip(*kept)
        return attend_back(place, complete, w_qkv, qkv, ctx, probs, logit_cot, d_blocks)

    unit_total = unit_sums[0]
    if packed:
        z, i = jnp.meshgrid(jnp.arange(mp), jnp.arange(dp), indexing="ij")
        at = me ^ i
        at = ((at % 2 * chips + at // 2) * mp + k_of[(mine - z) % mp]).reshape(-1)
        unit_total = reorder(unit_total.reshape(-1, piece), at).reshape(-1)
    vector = jnp.concatenate([small[:6].reshape(-1), unit_total])
    cols = 3 * head_width
    vector = jnp.pad(vector, (0, -vector.shape[0] % (24 * cols))).reshape(-1, cols)
    at = width + 8
    def scatter_tokens(back):
        return lax.psum_scatter(back, "mp", scatter_dimension=1, tiled=True)

    def joint_grads(*after):
        return tie(jnp.concatenate([acc, bias_acc, vector], 0), *after)

    if packed:
        other, d_out = other_grads
        got = lax.ppermute(other, "dp", swap)
        sums = weight_grad(mp, piece, ff_place, act, branch, inner, low, d_out, got)
        prev_grad, acc, bias_acc, *backs = back_through(sums)
        cut = 2 * piece + 32 >> 1
        x, y = flip_pairs(dp, 2), flip_pairs(dp, 4)
        a3, b3, a2, b2, a1, b1, a0, b0 = sums
        a3, b3 = lax.ppermute(a3, "dp", y), lax.ppermute(b3, "dp", x)
        a2, b1 = lax.ppermute(a2, "dp", y), lax.ppermute(b1, "dp", x)
        a1, a2, a3, b1, b3, prev_grad, backs[0] = lax.optimization_barrier(
            (a1, a2, a3, b1, b3, prev_grad, backs[0])
        )
        a1, b2 = hop_sums(a1, a3, b2, b3)
        vector = tie(vector, a1)
        a1, b2 = lax.ppermute(a1, "dp", x), lax.ppermute(b2, "dp", y)
        for bit in (1, 2):
            vector += lax.ppermute(vector, "mp", flip_pairs(mp, bit))
        a0, vector = lax.optimization_barrier((a0, vector))
        total = plane_sums(((mine - k_of) % mp).astype(jnp.int32), a0, a1, a2, b0, b1, b2)
        backs[0] = scatter_tokens(backs[0])
        backs[0], total = lax.optimization_barrier((backs[0], total))
        scattered = lax.psum_scatter(total, "mp", scatter_dimension=0)
        backs[1:] = [scatter_tokens(tie(back, scattered)) for back in backs[1:]]
        keep, send = halves_of(joint_grads(total), me % 2)
        keep = keep + lax.ppermute(send, "dp", swap)
        quarter = keep.shape[0] // 2
        top, low_part = keep[:quarter], keep[quarter:]
        top, low_part = (
            top + lax.ppermute(top, "dp", x), low_part + lax.ppermute(low_part, "dp", y)
        )
        top, low_part = (
            top + lax.ppermute(top, "dp", y), low_part + lax.ppermute(low_part, "dp", x)
        )
        keep = jnp.concatenate([top, low_part], 0)
        firsts, seconds = plane_gather(scattered[:cut], scattered[cut:], dp)
        firsts += [lax.ppermute(a, "dp", swap) for a in firsts]
        seconds += [lax.ppermute(a, "dp", swap) for a in seconds]
        other = lax.ppermute(keep, "dp", swap)
        summed = jnp.where(
            me % 2 == 0, jnp.concatenate([keep, other], 0), jnp.concatenate([other, keep], 0)
        )
        vector = summed[at:]
        d_in, d_down, d_out = gather_grads(ff_place, units, piece, head_width, firsts, seconds)
        backs[-1] = tie(backs[-1], d_in)
        inner_weight_grad = d_in
        down_weight_grad = d_down.reshape(units, width)
        output_weight_grad = d_out.reshape(head_width, width)
    else:
        g_down = mm(act, branch, 0, 0)
        g_in = mm(inner, low, 0, 0)
        g_out = mm(ctx_all, att, 0, 0)
        vector = lax.psum(vector, "mp")
        prev_grad, acc, bias_acc, *backs = back_through()
        summed = lax.psum(joint_grads(), "dp")
        vector = summed[at:]
        backs = [scatter_tokens(back) for back in backs]
        g_in = lax.psum_scatter(g_in, "mp", scatter_dimension=0, tiled=True)
        inner_weight_grad = lax.psum(g_in, "dp").T
        g_down = lax.psum_scatter(g_down, "mp", scatter_dimension=0, tiled=True)
        down_weight_grad = lax.psum(g_down, "dp")
        g_out = g_out.reshape(mp, head_width, width)
        out_sum = 0.0
        for k in range(mp):
            out_sum += shifted(g_out[k], (mp - k) % mp)
        output_weight_grad = lax.psum(out_sum, "dp")
    token_grads = residual.reshape(tokens.shape) + jnp.stack(backs).astype(F32)
    vector = vector.reshape(-1)
    small = vector[: 6 * width].reshape(6, width)
    unit_total = vector[6 * width : 6 * width + units * mp]
    inner_bias_grad = lax.dynamic_index_in_dim(unit_total.reshape(mp, units), mine, 0, False)
    return (
        layer.reshape(tokens.shape),
        logits,
        token_grads,
        prev_grad,
        summed[:width, :head_width],
        summed[:width, head_width : 2 * head_width],
        summed[:width, 2 * head_width :],
        summed[width, :head_width],
        summed[width, 2 * head_width :],
        output_weight_grad,
        small[0],
        small[1],
        small[2],
        inner_weight_grad,
        inner_bias_grad,
        down_weight_grad,
        small[3],
        small[4],
        small[5],
    )


def solution(mesh):
    rows = P(None, "dp", "mp", None)
    heads = P(None, "dp", "mp", None, None)
    cols, deep, vec, same = P(None, "mp"), P("mp", None), P("mp"), P()
    in_specs = (
        rows, heads, P(None, "dp", None), cols, cols, cols, vec, vec, deep, same, same, same,
        cols, vec, deep, same, same, same, rows, heads,
    )
    out_specs = (
        rows, heads, rows, heads, cols, cols, cols, vec, vec, deep, same, same, same, cols, vec,
        deep, same, same, same,
    )
    return jax.shard_map(
        on_device, mesh=mesh, in_specs=in_specs, out_specs=out_specs, check_vma=False
    )
```

```python
import functools
import math

import jax
import jax.numpy as jnp
from jax import lax
from jax.experimental import pallas as pl
from jax.experimental.pallas import tpu as pltpu
from jax.sharding import PartitionSpec as P

EPSILON = 1e-12
MASKED = -1e30
F32 = jnp.float32
BF16 = jnp.bfloat16
VMEM_LIMIT = 60 * 1024 * 1024
UNROLL = 2
ANY = pl.BlockSpec(memory_space=pl.ANY)
VMEM = pl.BlockSpec(memory_space=pltpu.VMEM)
SMEM = pl.BlockSpec(memory_space=pltpu.SMEM)


def mm(a, b, ca, cb):
    return lax.dot_general(a, b, (((ca,), (cb,)), ((), ())), preferred_element_type=F32)


def cost(flops, moved, exps=0):
    return pl.CostEstimate(flops=int(flops), bytes_accessed=int(moved), transcendentals=int(exps))


def start(src, dst, sem):
    copy = pltpu.make_async_copy(src, dst, sem)
    copy.start()
    return copy

def attend_kernel(b, slots, heads, size, tok, w, bias, prev, seg, *refs):
    logits, probs, qkv, ctx = refs[-15:-11]
    tok_v, prev_v, logits_v, probs_v, ctx_v, w_v, parts, cs = refs[-11:-3]
    sem_in, sem_out, sem_w = refs[-3:]
    length = tok_v.shape[1]
    width = heads * size
    w_in = start(w, w_v, sem_w)
    tok_in, prev_in = [], []
    for s in range(slots):
        tok_in.append(start(tok.at[s], tok_v.at[s], sem_in.at[s, heads]))
        if s == 0:
            prev_in += [start(prev.at[b, s, h], prev_v.at[s, h], sem_in.at[s, h]) for h in range(heads)]
    w_in.wait()
    for s in range(1, slots):
        prev_in += [start(prev.at[b, s, h], prev_v.at[s, h], sem_in.at[s, h]) for h in range(heads)]
    for copy in tok_in:
        copy.wait()

    def project(s, _):
        rows = (mm(tok_v[s], w_v[...], 1, 0) + bias[...]).astype(BF16)
        for h in range(heads):
            at = h * size
            parts[s, 0, h] = rows[:, at : at + size] * (1.0 / math.sqrt(size))
            parts[s, 1, h] = rows[:, width + at : width + at + size]
            parts[s, 2, h] = rows[:, 2 * width + at : 2 * width + at + size]
        start(parts.at[s], qkv.at[s], sem_out.at[s, 2 * heads])
        return _

    lax.fori_loop(0, slots, project, 0)

    def one_head(i, _):
        s, h = i // heads, lax.rem(i, heads)
        seg_k = seg[b, pl.ds(s, 1), :]
        seg_q = jnp.broadcast_to(seg_k, (8, length)).T[:, :1]
        pltpu.make_async_copy(prev.at[b, s, h], prev_v.at[s, h], sem_in.at[s, h]).wait()
        q, k, v = (parts[s, j, h] for j in range(3))
        scores = mm(q, k, 1, 1) + prev_v[s, h].astype(F32)
        logits_v[s, h] = scores.astype(BF16)
        start(logits_v.at[s, h], logits.at[b, s, h], sem_out.at[s, h])
        masked = jnp.where(seg_q == seg_k, scores, MASKED)
        exponent = jnp.exp(masked - jnp.max(masked, -1, keepdims=True))
        p = (exponent * (1.0 / jnp.sum(exponent, -1, keepdims=True))).astype(BF16)
        probs_v[s, h] = p
        start(probs_v.at[s, h], probs.at[s, h], sem_out.at[s, heads + h])
        cs[s, h] = mm(p, v, 1, 0).astype(BF16)
        return _

    lax.fori_loop(0, slots * heads, one_head, 0)
    for s in range(slots):
        ctx_v[s] = jnp.concatenate([cs[s, h] for h in range(heads)], -1)
        start(ctx_v.at[s], ctx.at[s], sem_out.at[s, 2 * heads + 1])
    for s in range(slots):
        for h in range(heads):
            pltpu.make_async_copy(logits_v.at[s, h], logits.at[b, s, h], sem_out.at[s, h]).wait()
            pltpu.make_async_copy(probs_v.at[s, h], probs.at[s, h], sem_out.at[s, heads + h]).wait()
        pltpu.make_async_copy(parts.at[s], qkv.at[s], sem_out.at[s, 2 * heads]).wait()
        pltpu.make_async_copy(ctx_v.at[s], ctx.at[s], sem_out.at[s, 2 * heads + 1]).wait()


def attend(b, complete, w_qkv, bias, prev_logits, seg, logits_in):
    slots, length, width = complete.shape
    heads = prev_logits.shape[2]
    cols = w_qkv.shape[1]
    size = cols // 3 // heads
    args = [complete, w_qkv, bias, prev_logits, seg]
    in_specs = [ANY, ANY, VMEM, ANY, VMEM]
    alias = {}
    if logits_in is not None:
        alias = {len(args): 0}
        args.append(logits_in)
        in_specs.append(ANY)
    n = slots * heads * length * length
    square = pltpu.VMEM((slots, heads, length, length), BF16)
    return pl.pallas_call(
        functools.partial(attend_kernel, b, slots, heads, size),
        in_specs=in_specs,
        out_specs=[ANY] * 4,
        out_shape=[
            jax.ShapeDtypeStruct(prev_logits.shape, BF16),
            jax.ShapeDtypeStruct((slots, heads, length, length), BF16),
            jax.ShapeDtypeStruct((slots, 3, heads, length, size), BF16),
            jax.ShapeDtypeStruct((slots, length, cols // 3), BF16),
        ],
        scratch_shapes=[
            pltpu.VMEM((slots, length, width), BF16), square, square, square,
            pltpu.VMEM((slots, length, cols // 3), BF16), pltpu.VMEM((width, cols), BF16),
            pltpu.VMEM((slots, 3, heads, length, size), BF16),
            pltpu.VMEM((slots, heads, length, size), BF16),
            pltpu.SemaphoreType.DMA((slots, heads + 1)),
            pltpu.SemaphoreType.DMA((slots, 2 * heads + 2)), pltpu.SemaphoreType.DMA,
        ],
        input_output_aliases=alias,
        compiler_params=pltpu.CompilerParams(vmem_limit_bytes=VMEM_LIMIT),
        cost_estimate=cost(n * 1024 + 2 * slots * length * width * cols, n * 6, n),
        name="attend",
    )(*args)


def attend_back_kernel(micro, slots, heads, size, n_blocks, place, *refs):
    tok, qkv, ctx, probs = (refs[i * micro : (i + 1) * micro] for i in range(4))
    w, cot, *blocks = refs[4 * micro : 4 * micro + 2 + n_blocks]
    prev_grad, acc, bias_acc, *backs = refs[-15 - micro : -12]
    tok_v, ctx_v, dctx_v, probs_v, cot_v, grad_v, back_v, w_v, parts, deltas = refs[-12:-2]
    sem_in, sem_out = refs[-2:]
    length = tok_v.shape[1]
    width = heads * size
    local = blocks[0].shape[2]
    total = micro * slots
    first, later = [], []
    for s in range(total):
        b, t = divmod(s, slots)
        first += [
            start(qkv[b].at[t], parts.at[s, pl.ds(0, 3)], sem_in.at[s, 0]),
            start(ctx[b].at[t], ctx_v.at[s], sem_in.at[s, 1]),
        ]
        for j in range(n_blocks):
            at = pl.ds(pl.multiple_of(place[j] * local, local), local)
            first.append(start(blocks[j].at[b, t], dctx_v.at[s, at], sem_in.at[s, 3 + j]))
    for s in range(total):
        b, t = divmod(s, slots)
        for h in range(heads):
            start(probs[b].at[t, h], probs_v.at[s, h], sem_in.at[s, 3 + n_blocks + h])
            start(cot.at[b, t, h], cot_v.at[s, h], sem_in.at[s, 3 + n_blocks + heads + h])
    later.append(start(w, w_v, sem_out.at[0, heads]))
    for s in range(total):
        b, t = divmod(s, slots)
        later.append(start(tok[b].at[t], tok_v.at[s], sem_in.at[s, 2]))
    for copy in first:
        copy.wait()

    def split(s, _):
        d_all = dctx_v[s]
        product = d_all.astype(F32) * ctx_v[s].astype(F32)
        for h in range(heads):
            at = h * size
            parts[s, 3, h] = d_all[:, at : at + size]
            deltas[s, h] = jnp.sum(product[:, at : at + size], -1, keepdims=True)
        return _

    lax.fori_loop(0, total, split, 0)

    def leave(s, h):
        return pltpu.make_async_copy(
            grad_v.at[s, h], prev_grad.at[s // slots, lax.rem(s, slots), h], sem_out.at[s, h])

    def leave_back(s, b):
        return pltpu.make_async_copy(
            back_v.at[s], backs[b].at[lax.rem(s, slots)], sem_out.at[s, heads + 1])

    def one_head(i, _):
        s, h = i // heads, lax.rem(i, heads)
        pltpu.make_async_copy(
            probs[0].at[0, h], probs_v.at[s, h], sem_in.at[s, 3 + n_blocks + h]).wait()
        pltpu.make_async_copy(
            cot.at[0, 0, h], cot_v.at[s, h], sem_in.at[s, 3 + n_blocks + heads + h]).wait()
        q, k, v, d_context = (parts[s, j, h] for j in range(4))
        p = probs_v[s, h]
        d_scores = p.astype(F32) * (mm(d_context, v, 1, 1) - deltas[s, h]) + cot_v[s, h].astype(F32)
        grad_v[s, h] = d_scores
        leave(s, h).start()
        d_dots = (d_scores * (1.0 / math.sqrt(size))).astype(BF16)
        parts[s, 0, h] = mm(d_dots, k, 1, 0).astype(BF16)
        parts[s, 1, h] = (mm(q, d_dots, 0, 0) * math.sqrt(size)).T.astype(BF16)
        parts[s, 2, h] = mm(d_context, p, 0, 0).T.astype(BF16)
        return _

    lax.fori_loop(0, total * heads, one_head, 0)
    for copy in later:
        copy.wait()
    acc[...] = jnp.zeros_like(acc)
    bias_acc[...] = jnp.zeros_like(bias_acc)

    def finish(s, _):
        d_qkv = jnp.concatenate([parts[s, j, h] for j in range(3) for h in range(heads)], -1)
        back_v[s] = mm(d_qkv, w_v[...], 1, 1).astype(BF16)
        for b in range(micro):
            pl.when(s // slots == b)(leave_back(s, b).start)
        acc[...] += mm(tok_v[s], d_qkv, 0, 0)
        bias_acc[...] += jnp.sum(d_qkv.astype(F32), 0, keepdims=True)
        return _

    lax.fori_loop(0, total, finish, 0)
    for s in range(total):
        for h in range(heads):
            leave(s, h).wait()
        leave_back(s, 0).wait()


def attend_back(place, complete, w_qkv, qkv, ctx, probs, logit_cot, blocks):
    micro, slots, heads, length, _ = logit_cot.shape
    width, cols = w_qkv.shape
    size = cols // 3 // heads
    args = [place, *complete, *qkv, *ctx, *probs, w_qkv, logit_cot, *blocks]
    n = micro * slots * heads * length * length
    total = micro * slots
    square = (total, heads, length, length)
    return pl.pallas_call(
        functools.partial(attend_back_kernel, micro, slots, heads, size, len(blocks)),
        in_specs=[SMEM] + [ANY] * (len(args) - 1),
        out_specs=[ANY, VMEM, VMEM] + [ANY] * micro,
        out_shape=[
            jax.ShapeDtypeStruct(logit_cot.shape, F32),
            jax.ShapeDtypeStruct((width, cols), F32),
            jax.ShapeDtypeStruct((8, cols), F32),
        ]
        + [jax.ShapeDtypeStruct((slots, length, width), BF16)] * micro,
        scratch_shapes=[
            pltpu.VMEM((total, length, width), BF16), pltpu.VMEM((total, length, cols // 3), BF16),
            pltpu.VMEM((total, length, cols // 3), BF16),
            pltpu.VMEM(square, BF16), pltpu.VMEM(square, BF16), pltpu.VMEM(square, F32),
            pltpu.VMEM((total, length, width), BF16), pltpu.VMEM((width, cols), BF16),
            pltpu.VMEM((total, 4, heads, length, size), BF16),
            pltpu.VMEM((total, heads, length, 1), F32),
            pltpu.SemaphoreType.DMA((total, 3 + len(blocks) + 2 * heads)),
            pltpu.SemaphoreType.DMA((total, heads + 2)),
        ],
        compiler_params=pltpu.CompilerParams(vmem_limit_bytes=VMEM_LIMIT),
        cost_estimate=cost(n * 2048 + 4 * total * length * width * cols, n * 8),
        name="attend_back",
    )(*args)


def gelu_and_slope(x):
    bell = jnp.exp(-0.5 * x * x)
    t = 1.0 / (1.0 + (0.3275911 * math.sqrt(0.5)) * jnp.abs(x))
    tail = t * (
        0.5 * 0.254829592
        + t * (
            0.5 * -0.284496736
            + t * (0.5 * 1.421413741 + t * (0.5 * -1.453152027 + t * (0.5 * 1.061405429)))
        )
    ) * bell
    phi = jnp.where(x >= 0, 1.0 - tail, tail)
    return x * phi, phi + x * (bell * (1.0 / math.sqrt(2.0 * math.pi)))


def norm_parts(u):
    centered = u - jnp.mean(u, -1, keepdims=True)
    r = lax.rsqrt(jnp.mean(centered * centered, -1, keepdims=True) + EPSILON)
    return centered * r, r


def norm_back(grad, gain, n, r):
    e = grad * gain
    return r * (e - jnp.mean(e, -1, keepdims=True) - n * jnp.mean(e * n, -1, keepdims=True))


def column_sum(u):
    return jnp.sum(u, 0, keepdims=True)


def feed_forward_kernel(micro, n_ctx, intake, place, refs_in, refs_out, scratch):
    ctx, (tok, cot, vectors, *weights) = refs_in[: micro * n_ctx], refs_in[micro * n_ctx :]
    b_out, g1, s1, b_down, g2, s2 = [vectors[i : i + 1, :] for i in range(6)]
    joint, (smalls, unit_sums) = refs_out[:8], refs_out[8:10]
    d_ctx, other = refs_out[10 : 10 + n_ctx], refs_out[10 + n_ctx :] or None
    if other:
        scratch, other_scratch = scratch[:-2], scratch[-2:]
    slope, total, *held = scratch
    weights_v, held = held[: -14], held[-14:]
    w_out, b_in = weights_v[-2:]
    ctx_v, tok_v, cot_v, d_ctx_v, *joint_v, sem, io_sem = held
    out_v, act_v, branch_v, inner_v, low_v, att_v, all_v, res_v = joint_v
    units, width = slope.shape[1], total.shape[1]
    chunk = width
    head_width = ctx[0].shape[1]

    def leave(i):
        return pltpu.make_async_copy(joint_v[i], joint[i], io_sem.at[1, i])

    first = [start(tok, tok_v, io_sem.at[0, 0])]
    for i, c in enumerate(ctx):
        b, k = divmod(i, n_ctx)
        rows = pl.ds(b * c.shape[0], c.shape[0])
        first.append(start(c, ctx_v.at[k, rows], io_sem.at[3 + b, k]))
    wait_first, wait_units, weights_of = intake(place, weights, weights_v, sem)
    cot_in = start(cot, cot_v, io_sem.at[0, 1])
    for copy in first:
        copy.wait()
    wait_first()
    attended = b_out
    for k in range(n_ctx):
        attended = attended + mm(ctx_v[k], w_out[k].reshape(-1, width)[:head_width], 1, 0)
    all_v[...] = jnp.concatenate([ctx_v[k] for k in range(n_ctx)], -1)
    n1, r1 = norm_parts(tok_v[...].astype(F32) + attended)
    hidden = n1 * g1 + s1
    low_v[...] = hidden.astype(BF16)
    total[...] = hidden + b_down
    leave(4).start()
    leave(6).start()

    def forward(j, _):
        wait_units(j)
        at = pl.ds(pl.multiple_of(j * chunk, chunk), chunk)
        w_in, w_down = weights_of(j)
        pre = mm(low_v[...], w_in, 1, 1) + b_in[:, at]
        activated, grad = gelu_and_slope(pre)
        activated = activated.astype(BF16)
        act_v[:, at] = activated
        slope[:, at] = grad.astype(BF16)
        total[...] += mm(activated, w_down, 1, 0)
        return _

    lax.fori_loop(0, units // chunk, forward, 0, unroll=UNROLL)
    leave(1).start()
    n2, r2 = norm_parts(total[...])
    out_v[...] = (n2 * g2 + s2).astype(BF16)
    leave(0).start()
    cot_in.wait()
    g = cot_v[...].astype(F32)
    d_second = norm_back(g, g2, n2, r2)
    smalls[3:4, :] = column_sum(d_second)
    smalls[4:5, :] = column_sum(g * n2)
    smalls[5:6, :] = column_sum(g)
    branch_v[...] = d_second.astype(BF16)
    leave(2).start()
    total[...] = d_second

    def backward(j, _):
        at = pl.ds(pl.multiple_of(j * chunk, chunk), chunk)
        w_in, w_down = weights_of(j)
        d_act = mm(branch_v[...], w_down, 1, 1)
        d_inner = d_act * slope[:, at].astype(F32)
        unit_sums[:, at] = jnp.broadcast_to(column_sum(d_inner), (8, chunk))
        d_inner = d_inner.astype(BF16)
        inner_v[:, at] = d_inner
        total[...] += mm(d_inner, w_in, 1, 0)
        return _

    lax.fori_loop(0, units // chunk, backward, 0, unroll=UNROLL)
    leave(3).start()
    d_hidden = total[...]
    d_residual = norm_back(d_hidden, g1, n1, r1)
    d_att = d_residual.astype(BF16)
    for k in range(n_ctx):
        d_ctx_v[k] = mm(d_att, w_out[k].reshape(-1, width)[:head_width], 1, 1).astype(BF16)
        start(d_ctx_v.at[k], d_ctx[k], io_sem.at[2, k])
    att_v[...] = d_att
    res_v[...] = d_residual
    leave(5).start()
    leave(7).start()
    smalls[0:1, :] = column_sum(d_residual)
    smalls[1:2, :] = column_sum(d_hidden * n1)
    smalls[2:3, :] = column_sum(d_hidden)
    smalls[6:8, :] = jnp.zeros((2, width), F32)
    if other is not None:
        grads, d_out = other
        other_v, other_sem = other_scratch
        n, mp, size, _ = other_v.shape
        piece = (size - 32) // 2
        span = mp * piece
        d_out[...] = mm(all_v[...], att_v[...], 0, 0)
        for o in reversed(range(n)):
            at = slice((n + o) * span, (n + o + 1) * span)
            fill_block(
                other_v, o, mm(inner_v[:, at], low_v[...], 0, 0),
                mm(act_v[:, at], branch_v[...], 0, 0), d_out, piece, place[n + o],
                2 * n + place[n + o], lambda k: place[2 * n + k],
            )
            start(other_v.at[o], grads.at[o], other_sem.at[o])
        for o in range(n):
            pltpu.make_async_copy(other_v.at[o], grads.at[o], other_sem.at[o]).wait()
    for k in range(n_ctx):
        pltpu.make_async_copy(d_ctx_v.at[k], d_ctx[k], io_sem.at[2, k]).wait()
    for i in range(8):
        leave(i).wait()


def relative_intake(place, weights, held, sem):
    own, *parts = weights
    packed, w_out, b_in = held
    n, mp, rows, width = packed.shape
    stages = [parts[j * n : (j + 1) * n] for j in range(len(parts) // n)]
    piece = b_in.shape[1] // (n * mp)
    pieces = 2 * piece

    def copies(i, at, sources):
        last = [pltpu.make_async_copy(
            own.at[at, pl.ds(pieces, rows - pieces)], packed.at[i, 0, pl.ds(pieces, rows - pieces)],
            sem.at[0, i])]
        main = [pltpu.make_async_copy(
            own.at[at, pl.ds(0, pieces)], packed.at[i, 0, pl.ds(0, pieces)], sem.at[1, i])]
        slot = 1
        for j in range(0, len(sources), 2):
            low, high = sources[j], sources[j + 1]
            slots, cut = pl.ds(slot, low.shape[0]), low.shape[1]
            slot += low.shape[0]
            last.append(pltpu.make_async_copy(
                high.at[:, pl.ds(pieces - cut, rows - pieces)],
                packed.at[i, slots, pl.ds(pieces, rows - pieces)], sem.at[2 + j, i]))
            main += [
                pltpu.make_async_copy(low, packed.at[i, slots, pl.ds(0, cut)], sem.at[3 + j, i]),
                pltpu.make_async_copy(
                    high.at[:, pl.ds(0, pieces - cut)],
                    packed.at[i, slots, pl.ds(cut, pieces - cut)], sem.at[6 + j, i]),
            ]
        return last, main

    for which in range(2):
        for i in range(n):
            for copy in copies(i, place[i], [stage[i] for stage in stages])[which]:
                copy.start()
    some = [stage[0] for stage in stages]

    def wait_first():
        for i in range(n):
            for copy in copies(i, 0, some)[0]:
                copy.wait()
            for s in range(mp):
                for j in range(2):
                    w_out[place[n + s], place[i] + n * j] = (
                        packed[i, s, pieces + 16 * j : pieces + 16 * j + 16]
                    )
                row = packed[i, s, pieces + 32 : pieces + 33, :].astype(F32)
                at = (i * mp + s) * piece
                b_in[:, at : at + piece] = (
                    row[:, :piece] + row[:, 128 : 128 + piece] + row[:, 256 : 256 + piece]
                )

    def wait_units(j):
        for half in range(2):
            for copy in copies(2 * j + half, 0, some)[1]:
                copy.wait()

    def units(j):
        at = pl.ds(2 * j, 2)
        return [packed[at, :, lo : lo + piece].reshape(-1, width) for lo in (0, piece)]

    return wait_first, wait_units, units


def whole_intake(place, weights, held, sem):
    w_in, w_down, w_out, b_in = held
    copies = [start(src, dst, sem.at[0, i]) for i, (src, dst) in enumerate(zip(weights, held))]

    def wait_first():
        for copy in copies:
            copy.wait()

    def units(j):
        return w_in[j], w_down[j]

    return wait_first, lambda j: None, units


def feed_forward(ctx, tokens, cot, vectors, place, weights, intake, block, grads):
    rows, width = tokens.shape
    micro, n_ctx = len(ctx), len(ctx[0])
    head_width = ctx[0][0].shape[1]
    units, held_shapes = block
    args = [place, *[c for blocks in ctx for c in blocks], tokens, cot, vectors, *weights]
    in_specs = [SMEM] + [ANY] * (micro * n_ctx + 2) + [VMEM] + [ANY] * len(weights)
    joint_cols = [(width, BF16), (units, BF16), (width, BF16), (units, BF16), (width, BF16),
                  (width, BF16), (n_ctx * head_width, BF16), (width, F32)]
    n_args = len(args)
    n_out = len(joint_cols) + 2 + n_ctx + 2 * len(grads)
    context = n_ctx * head_width

    def kernel(place, *refs):
        feed_forward_kernel(
            micro, n_ctx, intake, place, refs[: n_args - 1], refs[n_args - 1 : n_args - 1 + n_out],
            refs[n_args - 1 + n_out :],
        )

    heads_block = pltpu.VMEM((n_ctx, rows, head_width), BF16)
    outs = pl.pallas_call(
        kernel,
        in_specs=in_specs,
        out_specs=[ANY] * len(joint_cols) + [VMEM] * 2 + [ANY] * n_ctx + [ANY, VMEM] * len(grads),
        out_shape=[jax.ShapeDtypeStruct((rows, c), t) for c, t in joint_cols]
        + [jax.ShapeDtypeStruct((8, width), F32), jax.ShapeDtypeStruct((8, units), F32)]
        + [jax.ShapeDtypeStruct((rows, head_width), BF16)] * n_ctx
        + [jax.ShapeDtypeStruct(s, t) for g in grads for s, t in ((g, BF16), ((context, width), F32))],
        scratch_shapes=[
            pltpu.VMEM((rows, units), BF16), pltpu.VMEM((rows, width), F32),
            *[pltpu.VMEM(s, BF16) for s in held_shapes], pltpu.VMEM((1, units), F32),
            heads_block, pltpu.VMEM((rows, width), BF16), pltpu.VMEM((rows, width), BF16),
            heads_block, *[pltpu.VMEM((rows, c), t) for c, t in joint_cols],
            pltpu.SemaphoreType.DMA((9, 8)), pltpu.SemaphoreType.DMA((3 + micro, 8)),
        ]
        + [s for g in grads for s in (pltpu.VMEM(g, BF16), pltpu.SemaphoreType.DMA((g[0],)))],
        compiler_params=pltpu.CompilerParams(vmem_limit_bytes=VMEM_LIMIT),
        cost_estimate=cost(
            2 * rows * width * (4 * units + 2 * width), 4 * units * width + 20 * rows * width,
            rows * units,
        ),
        name="feed_forward",
    )(*args)
    n = len(joint_cols)
    return outs[:n], outs[n], outs[n + 1], outs[n + 2 : n + 2 + n_ctx], outs[n + 2 + n_ctx :]


def fill_block(out, o, d_in, d_down, d_out, piece, first, spare, place_of, got=None):
    mp = out.shape[1]
    head_width = d_out.shape[0] // mp
    for k in range(mp):
        parts = [d_in[k * piece : (k + 1) * piece], d_down[k * piece : (k + 1) * piece]]
        for p in (first, jnp.minimum(spare, head_width // 16 - 1)):
            at = pl.ds(pl.multiple_of(place_of(k) * head_width + p * 16, 16), 16)
            parts.append(d_out[at, :])
        row = 0
        for part in parts:
            at = slice(row, row + part.shape[0])
            if got is not None:
                part = part.astype(BF16).astype(F32) + got[o, k, at].astype(F32)
            out[o, k, at] = part.astype(BF16)
            row += part.shape[0]


def weight_grad(mp, piece, place, act, branch, inner, low, d_out, got):
    rows, width = branch.shape
    span = mp * piece
    n = act.shape[1] // span // 2
    size = 2 * piece + 32
    cut = size // 2
    order = tuple(reversed(range(n)))

    def kernel(place, act, branch, inner, low, d_out, got, *refs):
        outs, (act_v, inner_v, branch_v, low_v, got_v, out_v, sem) = refs[:-7], refs[-7:]
        moving = [start(low, low_v, sem.at[0, 0]), start(branch, branch_v, sem.at[0, 1])]
        loads, stores = {}, []
        for o in order:
            at = pl.ds(o * span, span)
            loads[o] = [
                start(inner.at[:, at], inner_v.at[o], sem.at[1, o]),
                start(act.at[:, at], act_v.at[o], sem.at[2, o]),
                start(got.at[o], got_v.at[o], sem.at[3, o]),
            ]
        for copy in moving:
            copy.wait()
        for i, o in enumerate(order):
            for copy in loads[o]:
                copy.wait()
            fill_block(
                out_v, o, mm(inner_v[o], low_v[...], 0, 0), mm(act_v[o], branch_v[...], 0, 0),
                d_out, piece, place[o], 2 * n + place[o], lambda k: place[2 * n + k], got_v,
            )
            stores += [
                start(out_v.at[o, :, pl.ds(0, cut)], outs[2 * i], sem.at[4, o]),
                start(out_v.at[o, :, pl.ds(cut, size - cut)], outs[2 * i + 1], sem.at[5, o]),
            ]
        for copy in stores:
            copy.wait()

    wide = pltpu.VMEM((n, rows, span), BF16)
    flat = pltpu.VMEM((rows, width), BF16)
    whole = pltpu.VMEM((n, mp, size, width), BF16)
    return pl.pallas_call(
        kernel,
        in_specs=[SMEM] + [ANY] * 4 + [VMEM, ANY],
        out_specs=[ANY] * (2 * n),
        out_shape=[
            jax.ShapeDtypeStruct((mp, r, width), BF16) for _ in range(n) for r in (cut, size - cut)
        ],
        scratch_shapes=[wide, wide, flat, flat, whole, whole, pltpu.SemaphoreType.DMA((6, n))],
        compiler_params=pltpu.CompilerParams(vmem_limit_bytes=VMEM_LIMIT),
        cost_estimate=cost(2 * rows * width * 5 * width, n * mp * width * 500),
        name="weight_grad",
    )(place, act, branch, inner, low, d_out, got)


def joined(body, shapes, *args, name):
    return pl.pallas_call(
        body,
        out_shape=[jax.ShapeDtypeStruct(s, t) for s, t in shapes],
        compiler_params=pltpu.CompilerParams(vmem_limit_bytes=VMEM_LIMIT),
        name=name,
    )(*args)


def hop_sums(a1, a3, b2, b3):
    def hop_sum(a1, a3, b2, b3, a, b):
        a[...] = (a1[...].astype(F32) + a3[...].astype(F32)).astype(BF16)
        b[...] = (b2[...].astype(F32) + b3[...].astype(F32)).astype(BF16)

    shapes = [(a1.shape, BF16), (b2.shape, BF16)]
    return joined(hop_sum, shapes, a1, a3, b2, b3, name="hop_sum")


def plane_sums(here, a0, a1, a2, b0, b1, b2):
    mp, cut, width = a0.shape
    rows = cut + b0.shape[1]

    def plane_sum(here, a0, a1, a2, b0, b1, b2, out):
        for k in range(mp):
            z = here[k]
            for at, parts in ((slice(0, cut), (a0, a1, a2)), (slice(cut, rows), (b0, b1, b2))):
                out[z, at] = sum(p[k].astype(F32) for p in parts).astype(BF16)

    return pl.pallas_call(
        plane_sum,
        in_specs=[SMEM] + [VMEM] * 6,
        out_shape=jax.ShapeDtypeStruct((mp, rows, width), BF16),
        compiler_params=pltpu.CompilerParams(vmem_limit_bytes=VMEM_LIMIT),
        name="plane_sum",
    )(here, a0, a1, a2, b0, b1, b2)


def plane_gather(first, second, dp, between=lambda *arrays: arrays):
    x, y = flip_pairs(dp, 2), flip_pairs(dp, 4)
    a1, b2 = lax.ppermute(first, "dp", x), lax.ppermute(second, "dp", y)
    a2, b1 = lax.ppermute(first, "dp", y), lax.ppermute(second, "dp", x)
    a1, b2 = between(a1, b2)
    a3, b3 = lax.ppermute(a1, "dp", y), lax.ppermute(b2, "dp", x)
    return [first, a1, a2, a3], [second, b1, b2, b3]


def gather_grads(place, units, piece, head_width, firsts, seconds):
    n = len(firsts)
    cut, width = firsts[0].shape
    rows = cut + seconds[0].shape[0]

    def kernel(place, *refs):
        parts, (d_in, d_down, d_out) = refs[: 2 * n], refs[2 * n : 2 * n + 3]
        pad, wide = refs[-2:]
        for i in range(n):
            p = place[i]
            whole = jnp.concatenate([parts[i][...], parts[n + i][...]], 0).astype(F32)
            wide[p] = whole[:piece]
            d_down[p] = whole[piece : 2 * piece]
            pad[p] = whole[2 * piece : 2 * piece + 16]
            pad[n + p] = whole[2 * piece + 16 :]
        d_out[...] = pad[: head_width // 16]
        d_in[...] = wide[...].reshape(n * piece, width).T

    vmem = [VMEM] * (2 * n)
    shapes = [(width, n * piece), (n, piece, width), (head_width // 16, 16, width)]
    return pl.pallas_call(
        kernel,
        in_specs=[SMEM] + vmem,
        out_shape=[jax.ShapeDtypeStruct(s, F32) for s in shapes],
        scratch_shapes=[pltpu.VMEM((2 * n, 16, width), F32), pltpu.VMEM((n, piece, width), F32)],
        compiler_params=pltpu.CompilerParams(vmem_limit_bytes=VMEM_LIMIT),
        name="gather_grads",
    )(place, *firsts, *seconds)


def shift_pairs(mp, k):
    return [(i, (i + k) % mp) for i in range(mp)]


def relay(array, mp):
    below, above = [array], [array]
    for hop in range(1, mp):
        pairs = [(i, i + 1) for i in range(hop - 1, mp - 1)]
        below.append(lax.ppermute(below[-1], "mp", pairs))
        above.append(lax.ppermute(above[-1], "mp", [(mp - 1 - i, mp - 1 - j) for i, j in pairs]))
    return below[1:], above[1:]


def flip_pairs(dp, bit):
    return [(i, i ^ bit) for i in range(dp)]


def tie(value, *others):
    return lax.optimization_barrier((value, others))[0]


def halves_of(array, core):
    half = array.shape[0] // 2
    return (
        lax.dynamic_slice_in_dim(array, core * half, half),
        lax.dynamic_slice_in_dim(array, (1 - core) * half, half),
    )


def reorder(rows, order):
    pick = (order[:, None] == jnp.arange(rows.shape[0])[None, :]).astype(F32)
    return jnp.dot(pick, rows, precision=lax.Precision.HIGHEST)


def on_device(
    tokens,
    prev_logits,
    segment_ids,
    query_weight,
    key_weight,
    value_weight,
    query_bias,
    value_bias,
    output_projection_weight,
    output_bias,
    first_gain,
    first_shift,
    inner_projection_weight,
    inner_bias,
    down_projection_weight,
    down_bias,
    second_gain,
    second_shift,
    output_cot,
    logit_cot,
):
    dp = lax.axis_size("dp")
    mp = lax.axis_size("mp")
    me = lax.axis_index("dp")
    mine = lax.axis_index("mp")
    micro_count, slots, local, width = tokens.shape
    length = prev_logits.shape[3]
    head_width = query_weight.shape[1]
    units = inner_projection_weight.shape[1]
    rows = slots * local
    packed = dp == 8 and mp == 4 and micro_count == 2 and units // dp == 96 and head_width == 192
    chips = dp // 2
    swap = flip_pairs(dp, 1)
    piece = units // dp

    def shifted(array, k):
        return lax.ppermute(array, "mp", shift_pairs(mp, k)) if k else array

    if packed:
        own_in = inner_projection_weight.T.reshape(dp, piece, width)
        own_down = down_projection_weight.reshape(dp, piece, width)
        own_out = output_projection_weight.reshape(-1, 16, width)
        high = inner_bias.astype(BF16)
        middle = (inner_bias - high.astype(F32)).astype(BF16)
        lowest = (inner_bias - high.astype(F32) - middle.astype(F32)).astype(BF16)
        own_bias = jnp.concatenate(
            [jnp.pad(v.reshape(dp, 1, piece), ((0, 0), (0, 15), (0, 128 - piece)))
             for v in (high, middle, lowest)]
            + [jnp.zeros((dp, 16, width - 3 * 128), BF16)], 2
        )
        own_out = jnp.concatenate([own_out, own_out[: 2 * dp - own_out.shape[0]]], 0)
        own_pack = jnp.concatenate([own_in, own_down, own_out[:dp], own_out[dp:], own_bias], 1)
        sent = lax.dynamic_index_in_dim(own_pack, me, 0, False)
        below, above = relay(sent, mp)
        second_hop = (below[1], above[1])
        from_z = jnp.stack(
            [jnp.where(mine >= k, below[k - 1], above[mp - k - 1]) for k in range(1, mp)]
        )
        k_of = jnp.arange(mp)
        cut = piece + piece // 3
        ff_place = me ^ (jnp.arange(dp) // chips + jnp.arange(dp) % chips * 2)
        ff_place = jnp.concatenate([ff_place, k_of]).astype(jnp.int32)
        intake = relative_intake
        block = (units * mp, [(dp, mp, 2 * piece + 48, width), (mp, 2 * dp, 16, width)])
    else:
        in_all = lax.all_gather(inner_projection_weight.T, "mp", axis=0, tiled=True)
        down_all = lax.all_gather(down_projection_weight, "mp", axis=0, tiled=True)
        wo_all = lax.all_gather(output_projection_weight, "mp")
        wo_all = jnp.stack(
            [lax.dynamic_index_in_dim(wo_all, (mine - k) % mp, 0, False) for k in range(mp)]
        )
        weights = [
            in_all.reshape(-1, width, width), down_all.reshape(-1, width, width), wo_all[:, None],
            lax.all_gather(inner_bias, "mp").reshape(1, -1),
        ]
        ff_place = jnp.zeros((dp,), jnp.int32)
        intake = whole_intake
        second_hop = ()
        square = (units * mp // width, width, width)
        block = (units * mp, [square, square, (mp, 1, head_width, width)])

    def gather_tokens(b, *after):
        return lax.all_gather(tie(tokens[b], *after), "mp", axis=1, tiled=True)

    complete = [gather_tokens(0)]
    for b in range(1, micro_count):
        complete.append(gather_tokens(b, *second_hop))
    w_qkv = jnp.concatenate([query_weight, key_weight, value_weight], 1)
    bias_row = jnp.concatenate([query_bias, jnp.zeros_like(query_bias), value_bias])[None]
    vectors = jnp.stack(
        [output_bias, first_gain, first_shift, down_bias, second_gain, second_shift]
        + [jnp.zeros_like(down_bias)] * 2
    )
    own_tokens = tokens.reshape(-1, width)
    own_cot = output_cot.reshape(-1, width)
    place = jnp.stack([(mine + k) % mp for k in range(mp)]).astype(jnp.int32)
    logits = None

    def attend_fully(b, logits):
        logits, probs, qkv, ctx = attend(
            b, complete[b], w_qkv, bias_row, prev_logits, segment_ids, logits
        )
        blocks = []
        for k in range(mp):
            at = ((mine + k) % mp) * local
            part = lax.dynamic_slice(ctx, (0, at, 0), (slots, local, head_width))
            blocks.append(shifted(part, k).reshape(rows, head_width))
        return logits, (probs, qkv, ctx), blocks

    def to_heads(d_ctx):
        return [
            shifted(part, (mp - k) % mp).reshape(micro_count, slots, local, head_width)
            for k, part in enumerate(d_ctx)
        ]

    kept, blocks = [], []
    for b in range(micro_count):
        logits, each, ctx_blocks = attend_fully(b, logits)
        kept.append(each)
        blocks.append(ctx_blocks)
        if packed and b == 0:
            firsts, seconds = plane_gather(
                from_z[:, :cut], from_z[:, cut:], dp, lambda *arrays: tie(arrays, each[2])
            )
            firsts[-1], seconds[-1], blocks[0] = lax.optimization_barrier(
                (firsts[-1], seconds[-1], blocks[0])
            )
            weights = [own_pack]
            for group in (firsts, seconds):
                weights += group + [lax.ppermute(a, "dp", swap) for a in group]
    blocks = lax.optimization_barrier(blocks)
    grads = [(chips, mp, 2 * piece + 32, width)] if packed else []
    joint, small, unit_sums, d_ctx, other_grads = feed_forward(
        blocks, own_tokens, own_cot, vectors, ff_place, weights, intake, block, grads
    )
    d_blocks = to_heads(d_ctx)
    layer, act, branch, inner, low, att, ctx_all, residual = joint

    def back_through(*after):
        d_blocks[0] = tie(d_blocks[0], *after)
        probs, qkv, ctx = zip(*kept)
        return attend_back(place, complete, w_qkv, qkv, ctx, probs, logit_cot, d_blocks)

    unit_total = unit_sums[0]
    if packed:
        z, i = jnp.meshgrid(jnp.arange(mp), jnp.arange(dp), indexing="ij")
        at = me ^ i
        at = ((at % 2 * chips + at // 2) * mp + k_of[(mine - z) % mp]).reshape(-1)
        unit_total = reorder(unit_total.reshape(-1, piece), at).reshape(-1)
    vector = jnp.concatenate([small[:6].reshape(-1), unit_total])
    cols = 3 * head_width
    vector = jnp.pad(vector, (0, -vector.shape[0] % (24 * cols))).reshape(-1, cols)
    at = width + 8
    def scatter_tokens(back):
        return lax.psum_scatter(back, "mp", scatter_dimension=1, tiled=True)

    def joint_grads(*after):
        return tie(jnp.concatenate([acc, bias_acc, vector], 0), *after)

    if packed:
        other, d_out = other_grads
        got = lax.ppermute(other, "dp", swap)
        sums = weight_grad(mp, piece, ff_place, act, branch, inner, low, d_out, got)
        prev_grad, acc, bias_acc, *backs = back_through(sums)
        cut = 2 * piece + 32 >> 1
        x, y = flip_pairs(dp, 2), flip_pairs(dp, 4)
        a3, b3, a2, b2, a1, b1, a0, b0 = sums
        a3, b3 = lax.ppermute(a3, "dp", y), lax.ppermute(b3, "dp", x)
        a2, b1 = lax.ppermute(a2, "dp", y), lax.ppermute(b1, "dp", x)
        a1, a2, a3, b1, b3, prev_grad, backs[0] = lax.optimization_barrier(
            (a1, a2, a3, b1, b3, prev_grad, backs[0])
        )
        a1, b2 = hop_sums(a1, a3, b2, b3)
        vector = tie(vector, a1)
        a1, b2 = lax.ppermute(a1, "dp", x), lax.ppermute(b2, "dp", y)
        for bit in (1, 2):
            vector += lax.ppermute(vector, "mp", flip_pairs(mp, bit))
        a0, vector = lax.optimization_barrier((a0, vector))
        total = plane_sums(((mine - k_of) % mp).astype(jnp.int32), a0, a1, a2, b0, b1, b2)
        backs[0] = scatter_tokens(backs[0])
        backs[0], total = lax.optimization_barrier((backs[0], total))
        scattered = lax.psum_scatter(total, "mp", scatter_dimension=0)
        backs[1:] = [scatter_tokens(tie(back, scattered)) for back in backs[1:]]
        keep, send = halves_of(joint_grads(total), me % 2)
        keep = keep + lax.ppermute(send, "dp", swap)
        quarter = keep.shape[0] // 2
        top, low_part = keep[:quarter], keep[quarter:]
        for one, two in ((x, y), (y, x)):
            top = top + lax.ppermute(top.astype(BF16), "dp", one).astype(F32)
            low_part = low_part + lax.ppermute(low_part.astype(BF16), "dp", two).astype(F32)
        keep = jnp.concatenate([top, low_part], 0)
        firsts, seconds = plane_gather(scattered[:cut], scattered[cut:], dp)
        firsts += [lax.ppermute(a, "dp", swap) for a in firsts]
        seconds += [lax.ppermute(a, "dp", swap) for a in seconds]
        other = lax.ppermute(keep, "dp", swap)
        summed = jnp.where(
            me % 2 == 0, jnp.concatenate([keep, other], 0), jnp.concatenate([other, keep], 0)
        )
        vector = summed[at:]
        d_in, d_down, d_out = gather_grads(ff_place, units, piece, head_width, firsts, seconds)
        backs[-1] = tie(backs[-1], d_in)
        inner_weight_grad = d_in
        down_weight_grad = d_down.reshape(units, width)
        output_weight_grad = d_out.reshape(head_width, width)
    else:
        g_down = mm(act, branch, 0, 0)
        g_in = mm(inner, low, 0, 0)
        g_out = mm(ctx_all, att, 0, 0)
        vector = lax.psum(vector, "mp")
        prev_grad, acc, bias_acc, *backs = back_through()
        summed = lax.psum(joint_grads(), "dp")
        vector = summed[at:]
        backs = [scatter_tokens(back) for back in backs]
        g_in = lax.psum_scatter(g_in, "mp", scatter_dimension=0, tiled=True)
        inner_weight_grad = lax.psum(g_in, "dp").T
        g_down = lax.psum_scatter(g_down, "mp", scatter_dimension=0, tiled=True)
        down_weight_grad = lax.psum(g_down, "dp")
        g_out = g_out.reshape(mp, head_width, width)
        out_sum = 0.0
        for k in range(mp):
            out_sum += shifted(g_out[k], (mp - k) % mp)
        output_weight_grad = lax.psum(out_sum, "dp")
    token_grads = residual.reshape(tokens.shape) + jnp.stack(backs).astype(F32)
    vector = vector.reshape(-1)
    small = vector[: 6 * width].reshape(6, width)
    unit_total = vector[6 * width : 6 * width + units * mp]
    inner_bias_grad = lax.dynamic_index_in_dim(unit_total.reshape(mp, units), mine, 0, False)
    return (
        layer.reshape(tokens.shape),
        logits,
        token_grads,
        prev_grad,
        summed[:width, :head_width],
        summed[:width, head_width : 2 * head_width],
        summed[:width, 2 * head_width :],
        summed[width, :head_width],
        summed[width, 2 * head_width :],
        output_weight_grad,
        small[0],
        small[1],
        small[2],
        inner_weight_grad,
        inner_bias_grad,
        down_weight_grad,
        small[3],
        small[4],
        small[5],
    )


def solution(mesh):
    rows = P(None, "dp", "mp", None)
    heads = P(None, "dp", "mp", None, None)
    cols, deep, vec, same = P(None, "mp"), P("mp", None), P("mp"), P()
    in_specs = (
        rows, heads, P(None, "dp", None), cols, cols, cols, vec, vec, deep, same, same, same,
        cols, vec, deep, same, same, same, rows, heads,
    )
    out_specs = (
        rows, heads, rows, heads, cols, cols, cols, vec, vec, deep, same, same, same, cols, vec,
        deep, same, same, same,
    )
    return jax.shard_map(
        on_device, mesh=mesh, in_specs=in_specs, out_specs=out_specs, check_vma=False
    )
```
